32 devices in a mesh: seq: 8 (over y, x, core), head: 4 (over z).
Axes of the slice: x: 2, y: 2, z: 4, core: 2. Of those that a mesh axis runs over, the one named last changes fastest.
Arguments:
- queries: bfloat16 [1024, 32, 576], P('seq', 'head'), may hold values from -0.06982422 to 0.06982422
- out_grad: bfloat16 [1024, 32, 512], P('seq', 'head'), may hold values from -12 to 12
- latents: bfloat16 [6144, 576], P('seq'), may hold values from -1.6953125 to 1.6953125
- log_norm: bfloat16 [1024, 32], P('seq', 'head'), may hold values from 0 to 12, as said below
- out_delta: bfloat16 [1024, 32], P('seq', 'head'), may hold values from -4 to 4
- plan: int32 [8, 2], P('seq'), may hold values from 0 to 1
Outputs:
- query_out: bfloat16 [1024, 32, 576], P('seq', 'head')
- latent_out: bfloat16 [6144, 576], P(('seq', 'head'))
The draws below stay inside these ranges and needn't reach their ends.
Inputs may be any that keep to these rules, and one draw needn't show every extreme that they name: plan[k, t] names which of the 2 latent blocks of shard k the queries of shard k + t (modulo the shards) visit at step t. log_norm lies within one unit of the log of 768.
All inputs are finite; a program needn't handle non-finite values.
Results may differ from the reference program's by a relative error of at most 0.0049.
Values may be sent and summed in bfloat16 or wider, within the bound.
No kernel may reach another device: no remote copies, remote signals or barrier semaphores. Data moves between devices by JAX's collectives and lax.ppermute only.
A program may use at most 64 MiB of HBM per device.

```python
import jax
import jax.numpy as jnp
from jax import lax

LAT = 512
KW = 576
HEADS = 32
PACKET = 128
BLOCK = 384
RES_BLOCKS = 2
TICKS = 2
SHARD = 768
TOKENS = 6144
QROWS = 1024
N_SEQ = 8


def draw_log_norm(key, part):
    centre = jnp.log(jnp.float32(TICKS * BLOCK))
    offset = jax.random.uniform(key, (QROWS, HEADS), jnp.float32, -0.4, 0.4)
    return (centre + offset).astype(jnp.bfloat16)


def with_ends(values, rng, least, top_value):
    longest = values.shape.index(max(values.shape))
    spots = []
    for shift in (0, 1):
        where = [jax.random.randint(jax.random.fold_in(rng, axis), (), 0, length) for axis, length in enumerate(values.shape)]
        where[longest] = (where[longest] + shift) % values.shape[longest]
        spots.append(tuple(where))
    return values.at[spots[0]].set(least).at[spots[1]].set(top_value)


def steps_of(stream_key, dims, cuts, smallest, largest):
    def one(axis_at, shards_of):
        heights = jax.random.uniform(jax.random.fold_in(jax.random.fold_in(stream_key, 6), axis_at), (shards_of,), jnp.float32, smallest / len(cuts), largest / len(cuts))
        return jnp.repeat(jnp.exp(heights), dims[axis_at] // shards_of).reshape((-1,) + (1,) * (len(dims) - axis_at - 1))

    gain = one(*cuts[0])
    for cut in cuts[1:]:
        gain = gain * one(*cut)
    return gain


def noise(stream_key, dims, spread, reach, pieces=(), kind=jnp.bfloat16):
    drawn = jax.random.normal(stream_key, dims, jnp.float32) * spread
    if len(pieces) > 0:
        drawn = steps_of(stream_key, dims, pieces, -0.22, 0.18) * drawn
    return jnp.clip(drawn, min=-reach, max=reach).astype(kind)


def setup_inputs(seed: int = 0) -> dict:
    keys = jax.random.split(jax.random.key(seed), 7)
    queries = jnp.clip(jax.random.uniform(keys[0], (QROWS, HEADS, KW), jnp.float32, -0.06982422, 0.06982422) * steps_of(keys[0], (QROWS, HEADS, KW), ((0, 8), (1, 4)), -0.4, 0.0), -0.06982422, 0.06982422).astype(jnp.bfloat16)
    out_grad = noise(keys[1], (QROWS, HEADS, LAT), 2.0, 12.0, ((0, 8), (1, 4)))
    latents = jnp.clip(jax.random.uniform(keys[2], (TOKENS, KW), jnp.float32, -1.6953125, 1.6953125) * steps_of(keys[2], (TOKENS, KW), ((0, 8),), -0.4, 0.0), -1.6953125, 1.6953125).astype(jnp.bfloat16)
    log_norm = draw_log_norm(jax.random.fold_in(keys[6], 71), 0)
    out_delta = noise(keys[4], (QROWS, HEADS), 1.0, 4.0, ((0, 8), (1, 4)))
    plan = with_ends(jax.random.randint(keys[5], (N_SEQ, TICKS), 0, RES_BLOCKS), jax.random.fold_in(keys[5], 1), 0, RES_BLOCKS - 1).astype(jnp.int32)
    return {"queries": queries, "out_grad": out_grad, "latents": latents, "log_norm": log_norm, "out_delta": out_delta, "plan": plan}


def visit(query_rows, grad_rows, norm_rows, delta_rows, key_rows, q_start, k_start):
    query_f = query_rows.astype(jnp.float32)
    grad_f = grad_rows.astype(jnp.float32)
    key_f = key_rows.astype(jnp.float32)
    scores = jnp.einsum("phc,jc->hpj", query_f, key_f)
    q_pos = q_start + jnp.arange(query_rows.shape[0], dtype=jnp.int32)
    k_pos = k_start + jnp.arange(key_rows.shape[0], dtype=jnp.int32)
    visible = k_pos[None, :] <= q_pos[:, None]
    norm_t = norm_rows.astype(jnp.float32).T[:, :, None]
    attn_prob = jnp.where(visible[None], jnp.exp(scores - norm_t), 0.0)
    prob_grad = jnp.einsum("phl,jl->hpj", grad_f, key_f[:, :LAT])
    delta_t = delta_rows.astype(jnp.float32).T[:, :, None]
    score_low = lax.optimization_barrier((attn_prob * (prob_grad - delta_t)).astype(jnp.bfloat16))
    prob_low = lax.optimization_barrier(attn_prob.astype(jnp.bfloat16))
    score_f = score_low.astype(jnp.float32)
    query_grad = jnp.einsum("hpj,jc->phc", score_f, key_f)
    key_grad = jnp.einsum("hpj,phc->jc", score_f, query_f)
    value_grad = jnp.einsum("hpj,phl->jl", prob_low.astype(jnp.float32), grad_f)
    key_grad = key_grad + jnp.pad(value_grad, ((0, 0), (0, key_rows.shape[1] - LAT)))
    return query_grad, key_grad


def reference(queries, out_grad, latents, log_norm, out_delta, plan):
    shards = N_SEQ
    head_count = queries.shape[1]
    width = queries.shape[2]
    query_blocks = queries.reshape(shards, PACKET, head_count, width)
    grad_blocks = out_grad.reshape(shards, PACKET, head_count, LAT)
    norm_blocks = log_norm.reshape(shards, PACKET, head_count)
    delta_blocks = out_delta.reshape(shards, PACKET, head_count)
    latent_blocks = latents.reshape(shards, RES_BLOCKS, BLOCK, width)

    def per_shard(shard_no):
        query_acc = jnp.zeros((PACKET, head_count, width), jnp.float32)
        key_parts = []
        for tick_no in range(TICKS):
            key_shard = (shard_no - tick_no) % shards
            block_no = plan[key_shard, tick_no]
            key_rows = latent_blocks[key_shard, block_no]
            q_start = shard_no * SHARD + SHARD - PACKET
            k_start = key_shard * SHARD + block_no * BLOCK
            query_grad, key_grad = visit(query_blocks[shard_no], grad_blocks[shard_no], norm_blocks[shard_no], delta_blocks[shard_no], key_rows, q_start, k_start)
            query_acc = query_acc + query_grad
            key_parts.append(key_grad)
        return query_acc.astype(jnp.bfloat16), jnp.stack(key_parts)

    query_out, key_parts = lax.map(per_shard, jnp.arange(shards, dtype=jnp.int32))
    latent_acc = jnp.zeros((shards, RES_BLOCKS, BLOCK, width), jnp.float32)
    for tick_no in range(TICKS):
        rolled = jnp.roll(key_parts[:, tick_no], -tick_no, axis=0)
        picked = (plan[:, tick_no][:, None] == jnp.arange(RES_BLOCKS, dtype=jnp.int32)[None, :]).astype(jnp.float32)
        latent_acc = latent_acc + picked[:, :, None, None] * rolled[:, None]
    return query_out.reshape(queries.shape), latent_acc.reshape(latents.shape).astype(jnp.bfloat16)
```

```python
import jax
import jax.numpy as jnp
from jax import lax
from jax.sharding import PartitionSpec as P

LAT = 512
PACKET = 128
BLOCK = 384
SHARD = 768


def visit(query_rows, grad_rows, norm_t, delta_t, key_rows, visible):
    scores = jnp.einsum("phc,jc->hpj", query_rows, key_rows, preferred_element_type=jnp.float32)
    attn_prob = jnp.where(visible[None], jnp.exp(scores - norm_t), 0.0)
    prob_grad = jnp.einsum(
        "phl,jl->hpj", grad_rows, key_rows[:, :LAT], preferred_element_type=jnp.float32
    )
    score_low = (attn_prob * (prob_grad - delta_t)).astype(jnp.bfloat16)
    prob_low = attn_prob.astype(jnp.bfloat16)
    query_grad = jnp.einsum("hpj,jc->phc", score_low, key_rows, preferred_element_type=jnp.float32)
    key_grad = jnp.einsum("hpj,phc->jc", score_low, query_rows, preferred_element_type=jnp.float32)
    value_grad = jnp.einsum("hpj,phl->jl", prob_low, grad_rows, preferred_element_type=jnp.float32)
    key_grad = key_grad + jnp.pad(value_grad, ((0, 0), (0, key_rows.shape[1] - LAT)))
    return query_grad, key_grad


def local(queries, out_grad, latents, log_norm, out_delta, plan):
    s = lax.axis_index("seq")
    h = lax.axis_index("head")
    n_seq = lax.axis_size("seq")
    n_head = lax.axis_size("head")
    low = n_head // 2
    rows = BLOCK // low
    r = h % low
    t = h // low
    b0 = plan[0, 0]
    b1 = plan[0, 1]

    far_block = lax.ppermute(
        lax.dynamic_slice_in_dim(latents, b1 * BLOCK, BLOCK, 0), "seq", [(i, i + 1) for i in range(n_seq - 1)]
    )
    own_block = lax.dynamic_slice_in_dim(latents, b0 * BLOCK, BLOCK, 0)
    norm_t = log_norm.astype(jnp.float32).T[:, :, None]
    delta_t = out_delta.astype(jnp.float32).T[:, :, None]

    q_pos = SHARD - PACKET + lax.iota(jnp.int32, PACKET)
    k_pos = b0 * BLOCK + lax.iota(jnp.int32, BLOCK)
    own_query, own_key = visit(
        queries, out_grad, norm_t, delta_t, own_block, k_pos[None, :] <= q_pos[:, None]
    )

    def piece(x, d):
        return lax.dynamic_slice_in_dim(x, (r + d) % low * rows, rows, 0)

    def route(d, back):
        pairs = []
        for i in range(back, n_seq):
            for j in range(n_head):
                to = j // low * low + (j + d) % low
                pairs.append((i * n_head + j, (i - back) * n_head + to))
        return pairs

    own_part = piece(own_key, 0)
    for d in range(1, low):
        got = lax.ppermute(piece(own_key, d).astype(jnp.bfloat16), ("seq", "head"), route(d, 0))
        own_part = own_part + got.astype(jnp.float32)

    far_query, far_key = visit(
        queries, out_grad, norm_t, delta_t, far_block, jnp.broadcast_to(s > 0, (PACKET, BLOCK))
    )
    far_part = jnp.zeros((rows, latents.shape[1]), jnp.float32)
    for d in reversed(range(low)):
        got = lax.ppermute(piece(far_key, d).astype(jnp.bfloat16), ("seq", "head"), route(d, 1))
        far_part = far_part + got.astype(jnp.float32)

    def total(block):
        return jnp.where(b0 == block, own_part, 0.0) + jnp.where(b1 == block, far_part, 0.0)

    swap = [(j, (j + low) % n_head) for j in range(n_head)]
    got = lax.ppermute(total(1 - t).astype(jnp.bfloat16), "head", swap)
    latent_out = total(t) + got.astype(jnp.float32)
    return ((own_query + far_query).astype(jnp.bfloat16), latent_out.astype(jnp.bfloat16))


def solution(mesh):
    return jax.shard_map(
        local,
        mesh=mesh,
        in_specs=(
            P("seq", "head", None),
            P("seq", "head", None),
            P("seq", None),
            P("seq", "head"),
            P("seq", "head"),
            P("seq", None),
        ),
        out_specs=(P("seq", "head", None), P(("seq", "head"), None)),
        check_vma=False,
    )
```

```python
import functools

import jax
import jax.numpy as jnp
from jax import lax
from jax.experimental import pallas as pl
from jax.experimental.pallas import tpu as pltpu
from jax.sharding import PartitionSpec as P

LAT = 512
PACKET = 128
BLOCK = 384
SHARD = 768
WIDE = 256
VMEM_LIMIT = 24 * 2**20

F32 = jnp.float32
BF16 = jnp.bfloat16


def dot(a, b):
    return lax.dot_general(a, b, (((1,), (0,)), ((), ())), preferred_element_type=F32)


def dot_nt(a, b):
    return lax.dot_general(a, b, (((1,), (1,)), ((), ())), preferred_element_type=F32)


def block_of(lat_ref, block):
    return lat_ref[:, pl.ds(pl.multiple_of(block * BLOCK, 128), BLOCK)]


def send_block_kernel(plan_ref, lat_ref, out_ref):
    out_ref[...] = block_of(lat_ref, plan_ref[0, 1]).T


def heads_side_by_side(q_ref, first, count):
    return jnp.concatenate([q_ref[first + i] for i in range(count)], axis=1)


def visit(keys, q_ref, grad_ref, norm_ref, delta_ref, visible, ds_ref, p_ref, grad_out_ref):
    heads = q_ref.shape[0]
    per = WIDE // PACKET
    for first in range(0, heads, per):
        cols = slice(first * PACKET, (first + per) * PACKET)
        scores = dot(keys, heads_side_by_side(q_ref, first, per))
        prob_grad = dot_nt(keys[:, :LAT], grad_ref[cols, :])
        for i in range(per):
            lanes = slice(i * PACKET, (i + 1) * PACKET)
            norm = norm_ref[first + i : first + i + 1, :].astype(F32)
            delta = delta_ref[first + i : first + i + 1, :].astype(F32)
            prob = jnp.exp(scores[:, lanes] - norm)
            if visible is not None:
                prob = jnp.where(visible, prob, 0.0)
            here = slice((first + i) * PACKET, (first + i + 1) * PACKET)
            ds_ref[:, here] = (prob * (prob_grad[:, lanes] - delta)).astype(BF16)
            p_ref[:, here] = prob.astype(BF16)
    key_grad = dot_nt(ds_ref[...], heads_side_by_side(q_ref, 0, heads))
    value_grad = dot(p_ref[...], grad_ref[...])
    grad_out_ref[:, :LAT] = key_grad[:, :LAT] + value_grad
    grad_out_ref[:, LAT:] = key_grad[:, LAT:]


def pieces_out(total_ref, out_refs, low):
    rows = BLOCK // low
    r = lax.rem(lax.axis_index("head"), low)
    for d, out_ref in enumerate(out_refs):
        start = pl.multiple_of(lax.rem(r + d, low) * rows, 16)
        out_ref[...] = total_ref[pl.ds(start, rows), :].astype(out_ref.dtype)


def own_kernel(low, plan_ref, lat_ref, q_ref, grad_ref, norm_ref, delta_ref, *rest):
    rows_ref, ds_ref = rest[:2]
    out_refs = rest[2 : 2 + low]
    p_ref, total_ref = rest[2 + low :]
    heads = q_ref.shape[0]
    group = WIDE // heads
    at = lax.broadcasted_iota(jnp.int32, (WIDE, WIDE), 0)
    come = lax.broadcasted_iota(jnp.int32, (WIDE, WIDE), 1)
    order = (come == lax.rem(at, group) * heads + lax.div(at, group)).astype(F32).astype(BF16)
    for g in range(PACKET // group):
        moved = dot(order, grad_ref[g * WIDE : (g + 1) * WIDE, :]).astype(BF16)
        for h in range(heads):
            rows_ref[h * PACKET + g * group : h * PACKET + (g + 1) * group, :] = moved[h * group : (h + 1) * group, :]
    b0 = plan_ref[0, 0]
    keys = block_of(lat_ref, b0).T
    k_pos = b0 * BLOCK + lax.broadcasted_iota(jnp.int32, (BLOCK, PACKET), 0)
    q_pos = SHARD - PACKET + lax.broadcasted_iota(jnp.int32, (BLOCK, PACKET), 1)
    visit(keys, q_ref, rows_ref, norm_ref, delta_ref, k_pos <= q_pos, ds_ref, p_ref, total_ref)
    pieces_out(total_ref, out_refs, low)


def far_kernel(low, keys_ref, q_ref, grad_ref, norm_ref, delta_ref, *rest):
    ds_ref = rest[0]
    out_refs = rest[1 : 1 + low]
    p_ref, total_ref = rest[1 + low :]
    visit(keys_ref[...], q_ref, grad_ref, norm_ref, delta_ref, None, ds_ref, p_ref, total_ref)
    pieces_out(total_ref, out_refs, low)


def query_kernel(plan_ref, lat_ref, far_ref, own_ds_ref, far_ds_ref, out_ref):
    heads = out_ref.shape[0]
    per = WIDE // PACKET
    own = block_of(lat_ref, plan_ref[0, 0])
    far = far_ref[...].T
    for first in range(0, heads, per):
        cols = slice(first * PACKET, (first + per) * PACKET)
        total = dot(own, own_ds_ref[:, cols]) + dot(far, far_ds_ref[:, cols])
        for i in range(per):
            out_ref[first + i] = total[:, i * PACKET : (i + 1) * PACKET].astype(BF16)


def combine_kernel(low, plan_ref, *rest):
    own_refs = rest[:low]
    far_refs = rest[low : 2 * low]
    send_ref, mine_ref = rest[2 * low :]
    own = own_refs[0][...]
    for ref in own_refs[1:]:
        own = own + ref[...].astype(F32)
    far = far_refs[0][...].astype(F32)
    for ref in far_refs[1:]:
        far = far + ref[...].astype(F32)
    t = lax.div(lax.axis_index("head"), low)
    b0, b1 = plan_ref[0, 0], plan_ref[0, 1]

    def total(block):
        return jnp.where(b0 == block, own, 0.0) + jnp.where(b1 == block, far, 0.0)

    mine_ref[...] = total(t)
    send_ref[...] = total(1 - t).astype(BF16)


def last_kernel(mine_ref, got_ref, out_ref):
    out_ref[...] = (mine_ref[...] + got_ref[...].astype(F32)).astype(BF16)


def call(kernel, name, ins, outs, scratch=(), smem=0, flops=0, transcendentals=0):
    specs = [pl.BlockSpec(memory_space=pltpu.SMEM if i < smem else pltpu.VMEM) for i in range(len(ins))]
    size = sum(x.size * x.dtype.itemsize for x in ins)
    size += sum(functools.reduce(lambda a, b: a * b, s, jnp.dtype(d).itemsize) for s, d in outs)
    return pl.pallas_call(
        kernel,
        name=name,
        out_shape=[jax.ShapeDtypeStruct(s, d) for s, d in outs],
        in_specs=specs,
        out_specs=[pl.BlockSpec(memory_space=pltpu.VMEM) for _ in outs],
        scratch_shapes=scratch,
        compiler_params=pltpu.CompilerParams(vmem_limit_bytes=VMEM_LIMIT),
        cost_estimate=pl.CostEstimate(flops=flops, bytes_accessed=size, transcendentals=transcendentals),
    )(*ins)


def local(queries, out_grad, latents, log_norm, out_delta, plan):
    n_seq = lax.axis_size("seq")
    n_head = lax.axis_size("head")
    low = n_head // 2
    rows = BLOCK // low
    packet, heads, width = queries.shape
    columns = packet * heads

    lat_t = latents.T
    q_t = jnp.transpose(queries, (1, 2, 0))
    grad = out_grad.reshape(columns, LAT)
    norm_t = log_norm.T
    delta_t = out_delta.T
    visit_flops = 2 * columns * BLOCK * (2 * width + 2 * LAT)

    def route(d, back):
        pairs = []
        for i in range(back, n_seq):
            for j in range(n_head):
                to = j // low * low + (j + d) % low
                pairs.append((i * n_head + j, (i - back) * n_head + to))
        return pairs

    (sent,) = call(send_block_kernel, "send_block", (plan, lat_t), [((BLOCK, width), BF16)], smem=1)
    far_keys = lax.ppermute(sent, "seq", [(i, i + 1) for i in range(n_seq - 1)])

    scratch = [pltpu.VMEM((BLOCK, columns), BF16), pltpu.VMEM((BLOCK, width), F32)]
    grad_rows, own_ds, *own = call(
        functools.partial(own_kernel, low),
        "own_visit",
        (plan, lat_t, q_t, grad, norm_t, delta_t),
        [((columns, LAT), BF16), ((BLOCK, columns), BF16), ((rows, width), F32)] + [((rows, width), BF16)] * (low - 1),
        scratch,
        smem=1,
        flops=visit_flops,
        transcendentals=columns * BLOCK,
    )
    own_parts = [own[0]] + [lax.ppermute(own[d], ("seq", "head"), route(d, 0)) for d in range(1, low)]

    far_ds, *far = call(
        functools.partial(far_kernel, low),
        "far_visit",
        (far_keys, q_t, grad_rows, norm_t, delta_t),
        [((BLOCK, columns), BF16)] + [((rows, width), BF16)] * low,
        scratch,
        flops=visit_flops,
        transcendentals=columns * BLOCK,
    )
    far_parts = [lax.ppermute(far[d], ("seq", "head"), route(d, 1)) for d in reversed(range(low))]

    (query_t,) = call(
        query_kernel,
        "query_grad",
        (plan, lat_t, far_keys, own_ds, far_ds),
        [((heads, width, packet), BF16)],
        smem=1,
        flops=4 * columns * BLOCK * width,
    )
    send, mine = call(
        functools.partial(combine_kernel, low),
        "combine",
        (plan, *own_parts, *far_parts),
        [((rows, width), BF16), ((rows, width), F32)],
        smem=1,
    )
    got = lax.ppermute(send, "head", [(j, (j + low) % n_head) for j in range(n_head)])
    (latent_out,) = call(last_kernel, "last_sum", (mine, got), [((rows, width), BF16)])
    return jnp.transpose(query_t, (2, 0, 1)), latent_out


def solution(mesh):
    return jax.shard_map(
        local,
        mesh=mesh,
        in_specs=(
            P("seq", "head", None),
            P("seq", "head", None),
            P("seq", None),
            P("seq", "head"),
            P("seq", "head"),
            P("seq", None),
        ),
        out_specs=(P("seq", "head", None), P(("seq", "head"), None)),
        check_vma=False,
    )
```

```python
import functools

import jax
import jax.numpy as jnp
from jax import lax
from jax.experimental import pallas as pl
from jax.experimental.pallas import tpu as pltpu
from jax.sharding import PartitionSpec as P

LAT = 512
PACKET = 128
BLOCK = 384
SHARD = 768
WIDE = 256
VMEM_LIMIT = 24 * 2**20
NEVER = 1e30

F32 = jnp.float32
BF16 = jnp.bfloat16


def dot(a, b):
    return lax.dot_general(a, b, (((1,), (0,)), ((), ())), preferred_element_type=F32)


def dot_nt(a, b):
    return lax.dot_general(a, b, (((1,), (1,)), ((), ())), preferred_element_type=F32)


def block_of(lat_ref, block):
    return lat_ref[:, pl.ds(pl.multiple_of(block * BLOCK, 128), BLOCK)]


def send_block_kernel(plan_hbm, lat_hbm, out_ref, plan_ref, lat_ref, sems):
    plan_copy = pltpu.make_async_copy(plan_hbm, plan_ref, sems.at[0])
    lat_copy = pltpu.make_async_copy(lat_hbm, lat_ref, sems.at[1])
    plan_copy.start()
    lat_copy.start()
    plan_copy.wait()
    lat_copy.wait()
    out_ref[...] = block_of(lat_ref, plan_ref[0, 1]).T


def heads_side_by_side(q_ref, first, count):
    return jnp.concatenate([q_ref[first + i] for i in range(count)], axis=1)


def visit(keys, q_ref, grad_ref, norm_ref, delta_ref, live, visible, ds_ref, p_ref, grad_out_ref):
    heads = q_ref.shape[0]
    per = WIDE // PACKET
    for first in range(0, heads, per):
        cols = slice(first * PACKET, (first + per) * PACKET)
        scores = dot(keys, heads_side_by_side(q_ref, first, per))
        prob_grad = dot_nt(keys[:, :LAT], grad_ref[cols, :])
        for i in range(per):
            lanes = slice(i * PACKET, (i + 1) * PACKET)
            norm = norm_ref[first + i : first + i + 1, :].astype(F32)
            if live is not None:
                norm = jnp.where(live, norm, NEVER)
            delta = delta_ref[first + i : first + i + 1, :].astype(F32)
            prob = jnp.exp(scores[:, lanes] - norm)
            if visible is not None:
                prob = jnp.where(visible, prob, 0.0)
            here = slice((first + i) * PACKET, (first + i + 1) * PACKET)
            ds_ref[:, here] = (prob * (prob_grad[:, lanes] - delta)).astype(BF16)
            p_ref[:, here] = prob.astype(BF16)
    key_grad = dot_nt(ds_ref[...], heads_side_by_side(q_ref, 0, heads))
    value_grad = dot(p_ref[...], grad_ref[...])
    grad_out_ref[:, :LAT] = key_grad[:, :LAT] + value_grad
    grad_out_ref[:, LAT:] = key_grad[:, LAT:]


def pieces_out(total_ref, out_refs, low):
    rows = BLOCK // low
    r = lax.rem(lax.axis_index("head"), low)
    for d, out_ref in enumerate(out_refs):
        start = pl.multiple_of(lax.rem(r + d, low) * rows, 16)
        out_ref[...] = total_ref[pl.ds(start, rows), :].astype(out_ref.dtype)


def own_kernel(low, plan_ref, lat_ref, q_ref, grad_ref, norm_ref, delta_ref, *rest):
    rows_ref, ds_ref = rest[:2]
    out_refs = rest[2 : 2 + low]
    p_ref, total_ref = rest[2 + low :]
    heads = q_ref.shape[0]
    group = WIDE // heads
    at = lax.broadcasted_iota(jnp.int32, (WIDE, WIDE), 0)
    come = lax.broadcasted_iota(jnp.int32, (WIDE, WIDE), 1)
    order = (come == lax.rem(at, group) * heads + lax.div(at, group)).astype(F32).astype(BF16)
    for g in range(PACKET // group):
        moved = dot(order, grad_ref[g * WIDE : (g + 1) * WIDE, :]).astype(BF16)
        for h in range(heads):
            rows_ref[h * PACKET + g * group : h * PACKET + (g + 1) * group, :] = moved[h * group : (h + 1) * group, :]
    b0 = plan_ref[0, 0]
    keys = block_of(lat_ref, b0).T
    k_pos = b0 * BLOCK + lax.broadcasted_iota(jnp.int32, (BLOCK, PACKET), 0)
    q_pos = SHARD - PACKET + lax.broadcasted_iota(jnp.int32, (BLOCK, PACKET), 1)
    visit(keys, q_ref, rows_ref, norm_ref, delta_ref, None, k_pos <= q_pos, ds_ref, p_ref, total_ref)
    pieces_out(total_ref, out_refs, low)


def far_kernel(low, keys_ref, q_ref, grad_ref, norm_ref, delta_ref, *rest):
    ds_ref = rest[0]
    out_refs = rest[1 : 1 + low]
    p_ref, total_ref = rest[1 + low :]
    live = lax.axis_index("seq") > 0
    visit(keys_ref[...], q_ref, grad_ref, norm_ref, delta_ref, live, None, ds_ref, p_ref, total_ref)
    pieces_out(total_ref, out_refs, low)


def query_kernel(plan_ref, lat_ref, far_ref, own_ds_ref, far_ds_ref, out_ref):
    heads = out_ref.shape[0]
    per = WIDE // PACKET
    own = block_of(lat_ref, plan_ref[0, 0])
    far = far_ref[...].T
    for first in range(0, heads, per):
        cols = slice(first * PACKET, (first + per) * PACKET)
        total = dot(own, own_ds_ref[:, cols]) + dot(far, far_ds_ref[:, cols])
        for i in range(per):
            out_ref[first + i] = total[:, i * PACKET : (i + 1) * PACKET].astype(BF16)


def combine_kernel(low, plan_ref, *rest):
    own_refs = rest[:low]
    far_refs = rest[low : 2 * low]
    send_ref, mine_ref = rest[2 * low :]
    own = own_refs[0][...]
    for ref in own_refs[1:]:
        own = own + ref[...].astype(F32)
    far = far_refs[0][...].astype(F32)
    for ref in far_refs[1:]:
        far = far + ref[...].astype(F32)
    t = lax.div(lax.axis_index("head"), low)
    b0, b1 = plan_ref[0, 0], plan_ref[0, 1]

    def total(block):
        return jnp.where(b0 == block, own, 0.0) + jnp.where(b1 == block, far, 0.0)

    mine_ref[...] = total(t)
    send_ref[...] = total(1 - t).astype(BF16)


def last_kernel(mine_ref, got_ref, out_ref):
    out_ref[...] = (mine_ref[...] + got_ref[...].astype(F32)).astype(BF16)


def call(kernel, name, ins, outs, scratch=(), smem=0, flops=0, transcendentals=0, raw=False):
    specs = [pl.BlockSpec(memory_space=pltpu.SMEM if i < smem else pltpu.VMEM) for i in range(len(ins))]
    if raw:
        specs = [pl.BlockSpec(memory_space=pl.ANY) for _ in ins]
        ins = [pltpu.with_memory_space_constraint(x, pltpu.HBM) for x in ins]
    size = sum(x.size * x.dtype.itemsize for x in ins)
    size += sum(functools.reduce(lambda a, b: a * b, s, jnp.dtype(d).itemsize) for s, d in outs)
    return pl.pallas_call(
        kernel,
        name=name,
        out_shape=[jax.ShapeDtypeStruct(s, d) for s, d in outs],
        in_specs=specs,
        out_specs=[pl.BlockSpec(memory_space=pltpu.VMEM) for _ in outs],
        scratch_shapes=scratch,
        compiler_params=pltpu.CompilerParams(vmem_limit_bytes=VMEM_LIMIT),
        cost_estimate=pl.CostEstimate(flops=flops, bytes_accessed=size, transcendentals=transcendentals),
    )(*ins)


def local(queries, out_grad, latents, log_norm, out_delta, plan):
    n_seq = lax.axis_size("seq")
    n_head = lax.axis_size("head")
    low = n_head // 2
    rows = BLOCK // low
    packet, heads, width = queries.shape
    columns = packet * heads

    lat_t = latents.T
    q_t = jnp.transpose(queries, (1, 2, 0))
    grad = out_grad.reshape(columns, LAT)
    norm_t = log_norm.T
    delta_t = out_delta.T
    visit_flops = 2 * columns * BLOCK * (2 * width + 2 * LAT)

    def route(d, back):
        pairs = []
        for i in range(n_seq):
            for j in range(n_head):
                to = j // low * low + (j + d) % low
                pairs.append((i * n_head + j, (i - back) % n_seq * n_head + to))
        return pairs

    (sent,) = call(
        send_block_kernel,
        "send_block",
        (plan, lat_t),
        [((BLOCK, width), BF16)],
        [pltpu.SMEM(plan.shape, plan.dtype), pltpu.VMEM(lat_t.shape, BF16), pltpu.SemaphoreType.DMA((2,))],
        flops=visit_flops,
        raw=True,
    )
    far_keys = lax.ppermute(sent, "seq", [(i, (i + 1) % n_seq) for i in range(n_seq)])

    scratch = [pltpu.VMEM((BLOCK, columns), BF16), pltpu.VMEM((BLOCK, width), F32)]
    grad_rows, own_ds, *own = call(
        functools.partial(own_kernel, low),
        "own_visit",
        (plan, lat_t, q_t, grad, norm_t, delta_t),
        [((columns, LAT), BF16), ((BLOCK, columns), BF16), ((rows, width), F32)] + [((rows, width), BF16)] * (low - 1),
        scratch,
        smem=1,
        flops=visit_flops,
        transcendentals=columns * BLOCK,
    )
    own_parts = [own[0]] + [lax.ppermute(own[d], ("seq", "head"), route(d, 0)) for d in range(1, low)]

    far_ds, *far = call(
        functools.partial(far_kernel, low),
        "far_visit",
        (far_keys, q_t, grad_rows, norm_t, delta_t),
        [((BLOCK, columns), BF16)] + [((rows, width), BF16)] * low,
        scratch,
        flops=visit_flops,
        transcendentals=columns * BLOCK,
    )
    far_parts = [lax.ppermute(far[d], ("seq", "head"), route(d, 1)) for d in reversed(range(low))]

    (query_t,) = call(
        query_kernel,
        "query_grad",
        (plan, lat_t, far_keys, own_ds, far_ds),
        [((heads, width, packet), BF16)],
        smem=1,
        flops=4 * columns * BLOCK * width,
    )
    send, mine = call(
        functools.partial(combine_kernel, low),
        "combine",
        (plan, *own_parts, *far_parts),
        [((rows, width), BF16), ((rows, width), F32)],
        smem=1,
    )
    got = lax.ppermute(send, "head", [(j, (j + low) % n_head) for j in range(n_head)])
    (latent_out,) = call(last_kernel, "last_sum", (mine, got), [((rows, width), BF16)])
    return jnp.transpose(query_t, (2, 0, 1)), latent_out


def solution(mesh):
    return jax.shard_map(
        local,
        mesh=mesh,
        in_specs=(
            P("seq", "head", None),
            P("seq", "head", None),
            P("seq", None),
            P("seq", "head"),
            P("seq", "head"),
            P("seq", None),
        ),
        out_specs=(P("seq", "head", None), P(("seq", "head"), None)),
        check_vma=False,
    )
```

```python
import functools

import jax
import jax.numpy as jnp
from jax import lax
from jax.experimental import pallas as pl
from jax.experimental.pallas import tpu as pltpu
from jax.sharding import PartitionSpec as P

LAT = 512
PACKET = 128
BLOCK = 384
SHARD = 768
WIDE = 256
VMEM_LIMIT = 24 * 2**20
NEVER = 1e30
CHUNKS = 2

F32 = jnp.float32
BF16 = jnp.bfloat16


def dot(a, b):
    return lax.dot_general(a, b, (((1,), (0,)), ((), ())), preferred_element_type=F32)


def dot_nt(a, b):
    return lax.dot_general(a, b, (((1,), (1,)), ((), ())), preferred_element_type=F32)


def block_of(lat_ref, block):
    return lat_ref[:, pl.ds(pl.multiple_of(block * BLOCK, 128), BLOCK)]


def send_block_kernel(low, plan_hbm, lat_hbm, *rest):
    out_refs = rest[:CHUNKS]
    plan_ref, lat_ref, sems = rest[CHUNKS:]
    plan_copy = pltpu.make_async_copy(plan_hbm, plan_ref, sems.at[0])
    lat_copy = pltpu.make_async_copy(lat_hbm, lat_ref, sems.at[1])
    plan_copy.start()
    lat_copy.start()
    plan_copy.wait()
    lat_copy.wait()
    keys = block_of(lat_ref, plan_ref[0, 1]).T
    rows = BLOCK // low
    part = rows // CHUNKS
    for c, out_ref in enumerate(out_refs):
        for j in range(low):
            start = j * rows + c * part
            out_ref[j * part : (j + 1) * part, :] = keys[start : start + part, :]


def heads_side_by_side(q_ref, first, count):
    return jnp.concatenate([q_ref[first + i] for i in range(count)], axis=1)


def visit(keys, q_ref, grad_ref, norm_ref, delta_ref, live, visible, ds_ref, p_ref, grad_out_ref):
    heads = q_ref.shape[0]
    per = WIDE // PACKET
    for first in range(0, heads, per):
        cols = slice(first * PACKET, (first + per) * PACKET)
        scores = dot(keys, heads_side_by_side(q_ref, first, per))
        prob_grad = dot_nt(keys[:, :LAT], grad_ref[cols, :])
        for i in range(per):
            lanes = slice(i * PACKET, (i + 1) * PACKET)
            norm = norm_ref[first + i : first + i + 1, :].astype(F32)
            if live is not None:
                norm = jnp.where(live, norm, NEVER)
            delta = delta_ref[first + i : first + i + 1, :].astype(F32)
            prob = jnp.exp(scores[:, lanes] - norm)
            if visible is not None:
                prob = jnp.where(visible, prob, 0.0)
            here = slice((first + i) * PACKET, (first + i + 1) * PACKET)
            ds_ref[:, here] = (prob * (prob_grad[:, lanes] - delta)).astype(BF16)
            p_ref[:, here] = prob.astype(BF16)
    key_grad = dot_nt(ds_ref[...], heads_side_by_side(q_ref, 0, heads))
    value_grad = dot(p_ref[...], grad_ref[...])
    grad_out_ref[:, :LAT] = key_grad[:, :LAT] + value_grad
    grad_out_ref[:, LAT:] = key_grad[:, LAT:]


def pieces_out(total_ref, out_refs, low):
    rows = total_ref.shape[0] // low
    r = lax.rem(lax.axis_index("head"), low)
    for d, out_ref in enumerate(out_refs):
        start = pl.multiple_of(lax.rem(r + d, low) * rows, 16)
        out_ref[...] = total_ref[pl.ds(start, rows), :].astype(out_ref.dtype)


def own_kernel(low, plan_ref, lat_ref, q_ref, grad_ref, norm_ref, delta_ref, *rest):
    rows_ref, ds_ref, sel_ref = rest[:3]
    out_refs = rest[3 : 3 + low]
    p_ref, total_ref = rest[3 + low :]
    t = lax.div(lax.axis_index("head"), low)
    b1 = plan_ref[0, 1]
    for i, hit in enumerate((plan_ref[0, 0] == t, plan_ref[0, 0] != t, b1 == t, b1 != t)):
        sel_ref[i : i + 1, :] = jnp.broadcast_to(jnp.where(hit, 1.0, 0.0), (1, sel_ref.shape[1])).astype(F32)
    heads = q_ref.shape[0]
    group = WIDE // heads
    at = lax.broadcasted_iota(jnp.int32, (WIDE, WIDE), 0)
    come = lax.broadcasted_iota(jnp.int32, (WIDE, WIDE), 1)
    order = (come == lax.rem(at, group) * heads + lax.div(at, group)).astype(F32).astype(BF16)
    for g in range(PACKET // group):
        moved = dot(order, grad_ref[g * WIDE : (g + 1) * WIDE, :]).astype(BF16)
        for h in range(heads):
            rows_ref[h * PACKET + g * group : h * PACKET + (g + 1) * group, :] = moved[h * group : (h + 1) * group, :]
    b0 = plan_ref[0, 0]
    keys = block_of(lat_ref, b0).T
    k_pos = b0 * BLOCK + lax.broadcasted_iota(jnp.int32, (BLOCK, PACKET), 0)
    q_pos = SHARD - PACKET + lax.broadcasted_iota(jnp.int32, (BLOCK, PACKET), 1)
    visit(keys, q_ref, rows_ref, norm_ref, delta_ref, None, k_pos <= q_pos, ds_ref, p_ref, total_ref)
    pieces_out(total_ref, out_refs, low)


def far_kernel(low, keys_ref, q_ref, grad_ref, norm_ref, delta_ref, *rest):
    ds_ref = rest[0]
    out_refs = rest[1 : 1 + low]
    p_ref, total_ref = rest[1 + low :]
    live = lax.axis_index("seq") > 0
    visit(keys_ref[...], q_ref, grad_ref, norm_ref, delta_ref, live, None, ds_ref, p_ref, total_ref)
    pieces_out(total_ref, out_refs, low)


def query_kernel(plan_ref, lat_ref, own_ds_ref, *rest):
    far_refs = rest[:CHUNKS]
    far_ds_refs = rest[CHUNKS : 2 * CHUNKS]
    out_ref = rest[-1]
    heads = out_ref.shape[0]
    per = WIDE // PACKET
    own = block_of(lat_ref, plan_ref[0, 0])
    fars = [ref[...].T for ref in far_refs]
    for first in range(0, heads, per):
        cols = slice(first * PACKET, (first + per) * PACKET)
        total = dot(own, own_ds_ref[:, cols])
        for far, ds_ref in zip(fars, far_ds_refs):
            total = total + dot(far, ds_ref[:, cols])
        for i in range(per):
            out_ref[first + i] = total[:, i * PACKET : (i + 1) * PACKET].astype(BF16)


def combine_kernel(low, chunk, sel_ref, *rest):
    own_refs = rest[:low]
    far_refs = rest[low : 2 * low]
    send_ref, mine_ref = rest[2 * low :]
    part = send_ref.shape[0]
    here = slice(chunk * part, (chunk + 1) * part)
    own = own_refs[0][here, :]
    for ref in own_refs[1:]:
        own = own + ref[here, :].astype(F32)
    far = far_refs[0][...].astype(F32)
    for ref in far_refs[1:]:
        far = far + ref[...].astype(F32)
    send_ref[...] = (own * sel_ref[1:2, :] + far * sel_ref[3:4, :]).astype(BF16)
    mine_ref[...] = own * sel_ref[0:1, :] + far * sel_ref[2:3, :]


def last_kernel(*refs):
    mine_refs, got_refs, out_ref = refs[:CHUNKS], refs[CHUNKS : 2 * CHUNKS], refs[-1]
    part = out_ref.shape[0] // CHUNKS
    for c in range(CHUNKS):
        out_ref[c * part : (c + 1) * part, :] = (mine_refs[c][...] + got_refs[c][...].astype(F32)).astype(BF16)


def call(kernel, name, ins, outs, scratch=(), smem=0, flops=0, transcendentals=0, raw=False):
    specs = [pl.BlockSpec(memory_space=pltpu.SMEM if i < smem else pltpu.VMEM) for i in range(len(ins))]
    if raw:
        specs = [pl.BlockSpec(memory_space=pl.ANY) for _ in ins]
        ins = [pltpu.with_memory_space_constraint(x, pltpu.HBM) for x in ins]
    size = sum(x.size * x.dtype.itemsize for x in ins)
    size += sum(functools.reduce(lambda a, b: a * b, s, jnp.dtype(d).itemsize) for s, d in outs)
    return pl.pallas_call(
        kernel,
        name=name,
        out_shape=[jax.ShapeDtypeStruct(s, d) for s, d in outs],
        in_specs=specs,
        out_specs=[pl.BlockSpec(memory_space=pltpu.VMEM) for _ in outs],
        scratch_shapes=scratch,
        compiler_params=pltpu.CompilerParams(vmem_limit_bytes=VMEM_LIMIT),
        cost_estimate=pl.CostEstimate(flops=flops, bytes_accessed=size, transcendentals=transcendentals),
    )(*ins)


def local(queries, out_grad, latents, log_norm, out_delta, plan):
    n_seq = lax.axis_size("seq")
    n_head = lax.axis_size("head")
    low = n_head // 2
    rows = BLOCK // low
    packet, heads, width = queries.shape
    columns = packet * heads

    lat_t = latents.T
    q_t = jnp.transpose(queries, (1, 2, 0))
    grad = out_grad.reshape(columns, LAT)
    norm_t = log_norm.T
    delta_t = out_delta.T
    visit_flops = 2 * columns * BLOCK * (2 * width + 2 * LAT)

    def route(d, back):
        pairs = []
        for i in range(n_seq):
            for j in range(n_head):
                to = j // low * low + (j + d) % low
                pairs.append((i * n_head + j, (i - back) % n_seq * n_head + to))
        return pairs

    part = rows // CHUNKS
    keys = BLOCK // CHUNKS

    sent = call(
        functools.partial(send_block_kernel, low),
        "send_block",
        (plan, lat_t),
        [((keys, width), BF16)] * CHUNKS,
        [pltpu.SMEM(plan.shape, plan.dtype), pltpu.VMEM(lat_t.shape, BF16), pltpu.SemaphoreType.DMA((2,))],
        flops=visit_flops,
        raw=True,
    )
    far_keys = [lax.ppermute(x, "seq", [(i, (i + 1) % n_seq) for i in range(n_seq)]) for x in sent]

    grad_rows, own_ds, sel, *own = call(
        functools.partial(own_kernel, low),
        "own_visit",
        (plan, lat_t, q_t, grad, norm_t, delta_t),
        [((columns, LAT), BF16), ((BLOCK, columns), BF16), ((8, width), F32), ((rows, width), F32)]
        + [((rows, width), BF16)] * (low - 1),
        [pltpu.VMEM((BLOCK, columns), BF16), pltpu.VMEM((BLOCK, width), F32)],
        smem=1,
        flops=visit_flops,
        transcendentals=columns * BLOCK,
    )
    own_parts = [own[0]] + [lax.ppermute(own[d], ("seq", "head"), route(d, 0)) for d in range(1, low)]

    far_ds, far_parts = [], []
    for c in range(CHUNKS):
        ds, *far = call(
            functools.partial(far_kernel, low),
            f"far_visit_{c}",
            (far_keys[c], q_t, grad_rows, norm_t, delta_t),
            [((keys, columns), BF16)] + [((part, width), BF16)] * low,
            [pltpu.VMEM((keys, columns), BF16), pltpu.VMEM((keys, width), F32)],
            flops=visit_flops // CHUNKS,
            transcendentals=columns * keys,
        )
        far_ds.append(ds)
        far_parts.append([lax.ppermute(far[d], ("seq", "head"), route(d, 1)) for d in reversed(range(low))])

    mine, got = [], []
    for c in range(CHUNKS):
        send, kept = call(
            functools.partial(combine_kernel, low, c),
            f"combine_{c}",
            (sel, *own_parts, *far_parts[c]),
            [((part, width), BF16), ((part, width), F32)],
        )
        mine.append(kept)
        got.append(lax.ppermute(send, "head", [(j, (j + low) % n_head) for j in range(n_head)]))

    (query_t,) = call(
        query_kernel,
        "query_grad",
        (plan, lat_t, own_ds, *far_keys, *far_ds),
        [((heads, width, packet), BF16)],
        smem=1,
        flops=4 * columns * BLOCK * width,
    )
    (latent_out,) = call(last_kernel, "last_sum", (*mine, *got), [((rows, width), BF16)])
    return jnp.transpose(query_t, (2, 0, 1)), latent_out


def solution(mesh):
    return jax.shard_map(
        local,
        mesh=mesh,
        in_specs=(
            P("seq", "head", None),
            P("seq", "head", None),
            P("seq", None),
            P("seq", "head"),
            P("seq", "head"),
            P("seq", None),
        ),
        out_specs=(P("seq", "head", None), P(("seq", "head"), None)),
        check_vma=False,
    )
```

```python
import functools

import jax
import jax.numpy as jnp
from jax import lax
from jax.experimental import pallas as pl
from jax.experimental.pallas import tpu as pltpu
from jax.sharding import PartitionSpec as P

LAT = 512
PACKET = 128
BLOCK = 384
SHARD = 768
WIDE = 256
VMEM_LIMIT = 24 * 2**20
NEVER = 1e30
CHUNKS = 2
COPIES = 6

F32 = jnp.float32
BF16 = jnp.bfloat16


def dot(a, b):
    return lax.dot_general(a, b, (((1,), (0,)), ((), ())), preferred_element_type=F32)


def dot_nt(a, b):
    return lax.dot_general(a, b, (((1,), (1,)), ((), ())), preferred_element_type=F32)


def block_of(lat_ref, block):
    return lat_ref[:, pl.ds(pl.multiple_of(block * BLOCK, 128), BLOCK)]


def send_block_kernel(low, plan_hbm, lat_hbm, *rest):
    out_refs = rest[:CHUNKS]
    plan_ref, lat_ref, sems = rest[CHUNKS:]
    step = lat_ref.shape[0] // COPIES
    copies = [pltpu.make_async_copy(plan_hbm, plan_ref, sems.at[COPIES])]
    for i in range(COPIES):
        here = pl.ds(i * step, step)
        copies.append(pltpu.make_async_copy(lat_hbm.at[here], lat_ref.at[here], sems.at[i]))
    for copy in copies:
        copy.start()
    for copy in copies:
        copy.wait()
    keys = block_of(lat_ref, plan_ref[0, 1]).T
    rows = BLOCK // low
    part = rows // CHUNKS
    for c, out_ref in enumerate(out_refs):
        for j in range(low):
            start = j * rows + c * part
            out_ref[j * part : (j + 1) * part, :] = keys[start : start + part, :]


def heads_side_by_side(q_ref, first, count):
    return jnp.concatenate([q_ref[first + i] for i in range(count)], axis=1)


def visit(keys, q_ref, grad_ref, norm_ref, delta_ref, live, visible, ds_ref, p_ref, grad_out_ref):
    heads = q_ref.shape[0]
    per = WIDE // PACKET
    for first in range(0, heads, per):
        cols = slice(first * PACKET, (first + per) * PACKET)
        scores = dot(keys, heads_side_by_side(q_ref, first, per))
        prob_grad = dot_nt(keys[:, :LAT], grad_ref[cols, :])
        for i in range(per):
            lanes = slice(i * PACKET, (i + 1) * PACKET)
            norm = norm_ref[first + i : first + i + 1, :].astype(F32)
            if live is not None:
                norm = jnp.where(live, norm, NEVER)
            delta = delta_ref[first + i : first + i + 1, :].astype(F32)
            prob = jnp.exp(scores[:, lanes] - norm)
            if visible is not None:
                prob = jnp.where(visible, prob, 0.0)
            here = slice((first + i) * PACKET, (first + i + 1) * PACKET)
            ds_ref[:, here] = (prob * (prob_grad[:, lanes] - delta)).astype(BF16)
            p_ref[:, here] = prob.astype(BF16)
    key_grad = dot_nt(ds_ref[...], heads_side_by_side(q_ref, 0, heads))
    value_grad = dot(p_ref[...], grad_ref[...])
    grad_out_ref[:, :LAT] = key_grad[:, :LAT] + value_grad
    grad_out_ref[:, LAT:] = key_grad[:, LAT:]


def pieces_out(total_ref, low, offset, out_refs):
    rows = total_ref.shape[0] // low
    r = lax.rem(lax.axis_index("head"), low)
    for d, out_ref in out_refs:
        start = pl.multiple_of(lax.rem(r + d, low) * rows, 16) + offset
        out_ref[...] = total_ref[pl.ds(start, out_ref.shape[0]), :].astype(out_ref.dtype)


def own_kernel(low, plan_hbm, lat_ref, q_ref, grad_ref, norm_ref, delta_ref, *rest):
    rows_ref, ds_ref, sel_ref, keep_ref = rest[:4]
    out_refs = rest[4:-4]
    plan_ref, p_ref, total_ref, sem = rest[-4:]
    plan_copy = pltpu.make_async_copy(plan_hbm, plan_ref, sem)
    plan_copy.start()
    heads = q_ref.shape[0]
    group = WIDE // heads
    at = lax.broadcasted_iota(jnp.int32, (WIDE, WIDE), 0)
    come = lax.broadcasted_iota(jnp.int32, (WIDE, WIDE), 1)
    order = (come == lax.rem(at, group) * heads + lax.div(at, group)).astype(F32).astype(BF16)
    for g in range(PACKET // group):
        moved = dot(order, grad_ref[g * WIDE : (g + 1) * WIDE, :]).astype(BF16)
        for h in range(heads):
            rows_ref[h * PACKET + g * group : h * PACKET + (g + 1) * group, :] = moved[h * group : (h + 1) * group, :]
    plan_copy.wait()
    b0, b1 = plan_ref[0, 0], plan_ref[0, 1]
    t = lax.div(lax.axis_index("head"), low)
    for i, hit in enumerate((b0 == t, b0 != t, b1 == t, b1 != t)):
        sel_ref[i : i + 1, :] = jnp.broadcast_to(jnp.where(hit, 1.0, 0.0), (1, sel_ref.shape[1])).astype(F32)
    keys = block_of(lat_ref, b0).T
    k_pos = b0 * BLOCK + lax.broadcasted_iota(jnp.int32, (BLOCK, PACKET), 0)
    q_pos = SHARD - PACKET + lax.broadcasted_iota(jnp.int32, (BLOCK, PACKET), 1)
    visit(keys, q_ref, rows_ref, norm_ref, delta_ref, None, k_pos <= q_pos, ds_ref, p_ref, total_ref)
    pieces_out(total_ref, low, 0, [(0, keep_ref)])
    for i, out_ref in enumerate(out_refs):
        part = out_ref.shape[0]
        pieces_out(total_ref, low, i % CHUNKS * part, [(1 + i // CHUNKS, out_ref)])


def far_kernel(low, held, keys_ref, q_ref, grad_ref, norm_ref, delta_ref, *rest):
    ds_ref = rest[held]
    out_refs = rest[held + 1 : held + 1 + low]
    p_ref, total_ref = rest[-2:]
    live = lax.axis_index("seq") > 0
    visit(keys_ref[...], q_ref, grad_ref, norm_ref, delta_ref, live, None, ds_ref, p_ref, total_ref)
    pieces_out(total_ref, low, 0, list(enumerate(out_refs)))


def query_kernel(plan_ref, lat_ref, own_ds_ref, *rest):
    far_refs = rest[:CHUNKS]
    far_ds_refs = rest[CHUNKS : 2 * CHUNKS]
    out_ref = rest[-1]
    heads = out_ref.shape[0]
    per = WIDE // PACKET
    own = block_of(lat_ref, plan_ref[0, 0])
    fars = [ref[...].T for ref in far_refs]
    for first in range(0, heads, per):
        cols = slice(first * PACKET, (first + per) * PACKET)
        total = dot(own, own_ds_ref[:, cols])
        for far, ds_ref in zip(fars, far_ds_refs):
            total = total + dot(far, ds_ref[:, cols])
        for i in range(per):
            out_ref[first + i] = total[:, i * PACKET : (i + 1) * PACKET].astype(BF16)


def combine_kernel(low, chunk, sel_ref, *rest):
    own_refs = rest[:low]
    far_refs = rest[low : 2 * low]
    send_ref, mine_ref = rest[-2:]
    part = send_ref.shape[0]
    here = slice(chunk * part, (chunk + 1) * part)
    own = own_refs[0][here, :]
    for ref in own_refs[1:]:
        own = own + ref[...].astype(F32)
    far = far_refs[0][...].astype(F32)
    for ref in far_refs[1:]:
        far = far + ref[...].astype(F32)
    send_ref[...] = (own * sel_ref[1:2, :] + far * sel_ref[3:4, :]).astype(BF16)
    mine_ref[...] = own * sel_ref[0:1, :] + far * sel_ref[2:3, :]


def last_kernel(*refs):
    mine_refs, got_refs, out_ref = refs[:CHUNKS][::-1], refs[CHUNKS : 2 * CHUNKS][::-1], refs[-1]
    part = out_ref.shape[0] // CHUNKS
    for c in range(CHUNKS):
        out_ref[c * part : (c + 1) * part, :] = (mine_refs[c][...] + got_refs[c][...].astype(F32)).astype(BF16)


def call(kernel, name, ins, outs, scratch=(), smem=(), raw=(), passed=(), flops=0, transcendentals=0):
    spaces = [pltpu.SMEM if i in smem else pltpu.VMEM for i in range(len(ins))]
    ins = list(ins)
    for i in raw:
        spaces[i] = pl.ANY
        ins[i] = pltpu.with_memory_space_constraint(ins[i], pltpu.HBM)
    size = sum(x.size * x.dtype.itemsize for x in ins)
    size += sum(functools.reduce(lambda a, b: a * b, s, jnp.dtype(d).itemsize) for s, d in outs)
    out_spaces = [pltpu.VMEM] * len(outs) + [pl.ANY] * len(passed)
    shapes = [jax.ShapeDtypeStruct(s, d) for s, d in outs]
    shapes += [jax.ShapeDtypeStruct(x.shape, x.dtype) for x in passed]
    aliases = {len(ins) + i: len(outs) + i for i in range(len(passed))}
    return pl.pallas_call(
        kernel,
        name=name,
        out_shape=shapes,
        in_specs=[pl.BlockSpec(memory_space=space) for space in spaces + [pl.ANY] * len(passed)],
        out_specs=[pl.BlockSpec(memory_space=space) for space in out_spaces],
        scratch_shapes=scratch,
        input_output_aliases=aliases,
        compiler_params=pltpu.CompilerParams(vmem_limit_bytes=VMEM_LIMIT),
        cost_estimate=pl.CostEstimate(flops=flops, bytes_accessed=size, transcendentals=transcendentals),
    )(*ins, *passed)


def local(queries, out_grad, latents, log_norm, out_delta, plan):
    n_seq = lax.axis_size("seq")
    n_head = lax.axis_size("head")
    low = n_head // 2
    rows = BLOCK // low
    packet, heads, width = queries.shape
    columns = packet * heads

    lat_t = latents.T
    q_t = jnp.transpose(queries, (1, 2, 0))
    grad = out_grad.reshape(columns, LAT)
    norm_t = log_norm.T
    delta_t = out_delta.T
    visit_flops = 2 * columns * BLOCK * (2 * width + 2 * LAT)

    def route(d, back):
        pairs = []
        for i in range(n_seq):
            for j in range(n_head):
                to = j // low * low + (j + d) % low
                pairs.append((i * n_head + j, (i - back) % n_seq * n_head + to))
        return pairs

    part = rows // CHUNKS
    keys = BLOCK // CHUNKS

    sent = call(
        functools.partial(send_block_kernel, low),
        "send_block",
        (plan, lat_t),
        [((keys, width), BF16)] * CHUNKS,
        [pltpu.SMEM(plan.shape, plan.dtype), pltpu.VMEM(lat_t.shape, BF16), pltpu.SemaphoreType.DMA((COPIES + 1,))],
        flops=visit_flops,
        raw=(0, 1),
    )
    far_keys = [lax.ppermute(x, "seq", [(i, (i + 1) % n_seq) for i in range(n_seq)]) for x in sent]

    grad_rows, own_ds, sel, keep, *own = call(
        functools.partial(own_kernel, low),
        "own_visit",
        (plan, lat_t, q_t, grad, norm_t, delta_t),
        [((columns, LAT), BF16), ((BLOCK, columns), BF16), ((8, width), F32), ((rows, width), F32)]
        + [((part, width), BF16)] * (CHUNKS * (low - 1)),
        [
            pltpu.SMEM(plan.shape, plan.dtype),
            pltpu.VMEM((BLOCK, columns), BF16),
            pltpu.VMEM((BLOCK, width), F32),
            pltpu.SemaphoreType.DMA,
        ],
        raw=(0,),
    )

    far_ds, own_parts, far_parts = [], [], []
    for c in range(CHUNKS):
        parts = own[c::CHUNKS]
        own_parts.append([keep] + [lax.ppermute(parts[d - 1], ("seq", "head"), route(d, 0)) for d in range(1, low)])
        later = [i for i in range(len(own)) if i % CHUNKS > c]
        ds, *far = call(
            functools.partial(far_kernel, low, len(later)),
            f"far_visit_{c}",
            (far_keys[c], q_t, grad_rows, norm_t, delta_t),
            [((keys, columns), BF16)] + [((part, width), BF16)] * low,
            [pltpu.VMEM((keys, columns), BF16), pltpu.VMEM((keys, width), F32)],
            passed=[own[i] for i in later],
        )
        for i, x in zip(later, far[low:]):
            own[i] = x
        far_ds.append(ds)
        far_parts.append([lax.ppermute(far[d], ("seq", "head"), route(d, 1)) for d in reversed(range(low))])

    mine, got = [None] * CHUNKS, [None] * CHUNKS
    for c in reversed(range(CHUNKS)):
        send, mine[c] = call(
            functools.partial(combine_kernel, low, c),
            f"combine_{c}",
            (sel, *own_parts[c], *far_parts[c]),
            [((part, width), BF16), ((part, width), F32)],
        )
        got[c] = lax.ppermute(send, "head", [(j, (j + low) % n_head) for j in range(n_head)])

    (query_t,) = call(
        query_kernel,
        "query_grad",
        (plan, lat_t, own_ds, *far_keys, *far_ds),
        [((heads, width, packet), BF16)],
        smem=(0,),
        flops=4 * columns * BLOCK * width,
    )
    (latent_out,) = call(last_kernel, "last_sum", (*mine[::-1], *got[::-1]), [((rows, width), BF16)])
    return jnp.transpose(query_t, (2, 0, 1)), latent_out


def solution(mesh):
    return jax.shard_map(
        local,
        mesh=mesh,
        in_specs=(
            P("seq", "head", None),
            P("seq", "head", None),
            P("seq", None),
            P("seq", "head"),
            P("seq", "head"),
            P("seq", None),
        ),
        out_specs=(P("seq", "head", None), P(("seq", "head"), None)),
        check_vma=False,
    )
```

```python
import functools

import jax
import jax.numpy as jnp
from jax import lax
from jax.experimental import pallas as pl
from jax.experimental.pallas import tpu as pltpu
from jax.sharding import PartitionSpec as P

LAT = 512
PACKET = 128
BLOCK = 384
SHARD = 768
WIDE = 256
VMEM_LIMIT = 24 * 2**20
NEVER = 1e30
CHUNKS = 2
COPIES = 1

F32 = jnp.float32
BF16 = jnp.bfloat16


def dot(a, b):
    return lax.dot_general(a, b, (((1,), (0,)), ((), ())), preferred_element_type=F32)


def dot_nt(a, b):
    return lax.dot_general(a, b, (((1,), (1,)), ((), ())), preferred_element_type=F32)


def block_of(lat_ref, block):
    return lat_ref[:, pl.ds(pl.multiple_of(block * BLOCK, 128), BLOCK)]


def send_block_kernel(low, plan_hbm, lat_hbm, *rest):
    out_refs = rest[:CHUNKS]
    plan_ref, lat_ref, sems = rest[CHUNKS:]
    step = lat_ref.shape[0] // COPIES
    copies = [pltpu.make_async_copy(plan_hbm, plan_ref, sems.at[COPIES])]
    for i in range(COPIES):
        here = pl.ds(i * step, step)
        copies.append(pltpu.make_async_copy(lat_hbm.at[here], lat_ref.at[here], sems.at[i]))
    for copy in copies:
        copy.start(priority=1)
    for copy in copies:
        copy.wait()
    keys = block_of(lat_ref, plan_ref[0, 1]).T
    rows = BLOCK // low
    part = rows // CHUNKS
    for c, out_ref in enumerate(out_refs):
        for j in range(low):
            start = j * rows + c * part
            out_ref[j * part : (j + 1) * part, :] = keys[start : start + part, :]


def heads_side_by_side(q_ref, first, count):
    return jnp.concatenate([q_ref[first + i] for i in range(count)], axis=1)


def visit(keys, q_ref, grad_ref, norm_ref, delta_ref, live, visible, ds_ref, p_ref, grad_out_ref):
    heads = q_ref.shape[0]
    per = WIDE // PACKET
    for first in range(0, heads, per):
        cols = slice(first * PACKET, (first + per) * PACKET)
        scores = dot(keys, heads_side_by_side(q_ref, first, per))
        prob_grad = dot_nt(keys[:, :LAT], grad_ref[cols, :])
        for i in range(per):
            lanes = slice(i * PACKET, (i + 1) * PACKET)
            norm = norm_ref[first + i : first + i + 1, :].astype(F32)
            if live is not None:
                norm = jnp.where(live, norm, NEVER)
            delta = delta_ref[first + i : first + i + 1, :].astype(F32)
            prob = jnp.exp(scores[:, lanes] - norm)
            if visible is not None:
                prob = jnp.where(visible, prob, 0.0)
            here = slice((first + i) * PACKET, (first + i + 1) * PACKET)
            ds_ref[:, here] = (prob * (prob_grad[:, lanes] - delta)).astype(BF16)
            p_ref[:, here] = prob.astype(BF16)
    key_grad = dot_nt(ds_ref[...], heads_side_by_side(q_ref, 0, heads))
    value_grad = dot(p_ref[...], grad_ref[...])
    grad_out_ref[:, :LAT] = key_grad[:, :LAT] + value_grad
    grad_out_ref[:, LAT:] = key_grad[:, LAT:]


def pieces_out(total_ref, low, offset, out_refs):
    rows = total_ref.shape[0] // low
    r = lax.rem(lax.axis_index("head"), low)
    for d, out_ref in out_refs:
        start = pl.multiple_of(lax.rem(r + d, low) * rows, 16) + offset
        out_ref[...] = total_ref[pl.ds(start, out_ref.shape[0]), :].astype(out_ref.dtype)


def own_kernel(low, held, plan_hbm, lat_ref, q_ref, grad_ref, norm_ref, delta_ref, *rest):
    rows_ref, ds_ref, sel_ref, keep_ref = rest[held : held + 4]
    out_refs = rest[held + 4 : held + 3 + low]
    plan_ref, p_ref, total_ref, sem = rest[-4:]
    plan_copy = pltpu.make_async_copy(plan_hbm, plan_ref, sem)
    plan_copy.start()
    heads = q_ref.shape[0]
    group = WIDE // heads
    at = lax.broadcasted_iota(jnp.int32, (WIDE, WIDE), 0)
    come = lax.broadcasted_iota(jnp.int32, (WIDE, WIDE), 1)
    order = (come == lax.rem(at, group) * heads + lax.div(at, group)).astype(F32).astype(BF16)
    for g in range(PACKET // group):
        moved = dot(order, grad_ref[g * WIDE : (g + 1) * WIDE, :]).astype(BF16)
        for h in range(heads):
            rows_ref[h * PACKET + g * group : h * PACKET + (g + 1) * group, :] = moved[h * group : (h + 1) * group, :]
    plan_copy.wait()
    b0, b1 = plan_ref[0, 0], plan_ref[0, 1]
    t = lax.div(lax.axis_index("head"), low)
    for i, hit in enumerate((b0 == t, b0 != t, b1 == t, b1 != t)):
        sel_ref[i : i + 1, :] = jnp.broadcast_to(jnp.where(hit, 1.0, 0.0), (1, sel_ref.shape[1])).astype(F32)
    keys = block_of(lat_ref, b0).T
    k_pos = b0 * BLOCK + lax.broadcasted_iota(jnp.int32, (BLOCK, PACKET), 0)
    q_pos = SHARD - PACKET + lax.broadcasted_iota(jnp.int32, (BLOCK, PACKET), 1)
    visit(keys, q_ref, rows_ref, norm_ref, delta_ref, None, k_pos <= q_pos, ds_ref, p_ref, total_ref)
    pieces_out(total_ref, low, 0, [(0, keep_ref)])
    pieces_out(total_ref, low, 0, list(enumerate(out_refs, 1)))


def far_kernel(low, keys_ref, q_ref, grad_ref, norm_ref, delta_ref, *rest):
    ds_ref = rest[-3 - low]
    out_refs = rest[-2 - low : -2]
    p_ref, total_ref = rest[-2:]
    live = lax.axis_index("seq") > 0
    visit(keys_ref[...], q_ref, grad_ref, norm_ref, delta_ref, live, None, ds_ref, p_ref, total_ref)
    pieces_out(total_ref, low, 0, list(enumerate(out_refs)))


def query_kernel(plan_ref, lat_ref, own_ds_ref, *rest):
    far_refs = rest[:CHUNKS]
    far_ds_refs = rest[CHUNKS : 2 * CHUNKS]
    out_ref = rest[-1]
    heads = out_ref.shape[0]
    per = WIDE // PACKET
    own = block_of(lat_ref, plan_ref[0, 0])
    fars = [ref[...].T for ref in far_refs]
    for first in range(0, heads, per):
        cols = slice(first * PACKET, (first + per) * PACKET)
        total = dot(own, own_ds_ref[:, cols])
        for far, ds_ref in zip(fars, far_ds_refs):
            total = total + dot(far, ds_ref[:, cols])
        for i in range(per):
            out_ref[first + i] = total[:, i * PACKET : (i + 1) * PACKET].astype(BF16)


def combine_kernel(low, chunk, sel_ref, *rest):
    far_refs = rest[:low]
    own_refs = rest[low : 2 * low]
    send_ref, mine_ref = rest[-2:]
    part = send_ref.shape[0]
    here = slice(chunk * part, (chunk + 1) * part)
    own = own_refs[0][here, :]
    for ref in own_refs[1:]:
        own = own + ref[here, :].astype(F32)
    far = far_refs[0][...].astype(F32)
    for ref in far_refs[1:]:
        far = far + ref[...].astype(F32)
    send_ref[...] = (own * sel_ref[1:2, :] + far * sel_ref[3:4, :]).astype(BF16)
    mine_ref[...] = own * sel_ref[0:1, :] + far * sel_ref[2:3, :]


def last_kernel(*refs):
    mine_refs, got_refs, out_ref = refs[:CHUNKS][::-1], refs[CHUNKS : 2 * CHUNKS][::-1], refs[-1]
    part = out_ref.shape[0] // CHUNKS
    for c in range(CHUNKS):
        out_ref[c * part : (c + 1) * part, :] = (mine_refs[c][...] + got_refs[c][...].astype(F32)).astype(BF16)


def call(kernel, name, ins, outs, scratch=(), smem=(), raw=(), passed=(), flops=0, transcendentals=0):
    spaces = [pltpu.SMEM if i in smem else pltpu.VMEM for i in range(len(ins))]
    ins = list(ins)
    for i in raw:
        spaces[i] = pl.ANY
        ins[i] = pltpu.with_memory_space_constraint(ins[i], pltpu.HBM)
    size = sum(x.size * x.dtype.itemsize for x in ins)
    size += sum(functools.reduce(lambda a, b: a * b, s, jnp.dtype(d).itemsize) for s, d in outs)
    out_spaces = [pltpu.VMEM] * len(outs) + [pl.ANY] * len(passed)
    shapes = [jax.ShapeDtypeStruct(s, d) for s, d in outs]
    shapes += [jax.ShapeDtypeStruct(x.shape, x.dtype) for x in passed]
    aliases = {len(ins) + i: len(outs) + i for i in range(len(passed))}
    return pl.pallas_call(
        kernel,
        name=name,
        out_shape=shapes,
        in_specs=[pl.BlockSpec(memory_space=space) for space in spaces + [pl.ANY] * len(passed)],
        out_specs=[pl.BlockSpec(memory_space=space) for space in out_spaces],
        scratch_shapes=scratch,
        input_output_aliases=aliases,
        compiler_params=pltpu.CompilerParams(vmem_limit_bytes=VMEM_LIMIT),
        cost_estimate=pl.CostEstimate(flops=flops, bytes_accessed=size, transcendentals=transcendentals),
    )(*ins, *passed)


def local(queries, out_grad, latents, log_norm, out_delta, plan):
    n_seq = lax.axis_size("seq")
    n_head = lax.axis_size("head")
    low = n_head // 2
    rows = BLOCK // low
    packet, heads, width = queries.shape
    columns = packet * heads

    lat_t = latents.T
    q_t = jnp.transpose(queries, (1, 2, 0))
    grad = out_grad.reshape(columns, LAT)
    norm_t = log_norm.T
    delta_t = out_delta.T
    visit_flops = 2 * columns * BLOCK * (2 * width + 2 * LAT)

    def route(d, back):
        pairs = []
        for i in range(n_seq):
            for j in range(n_head):
                to = j // low * low + (j + d) % low
                pairs.append((i * n_head + j, (i - back) % n_seq * n_head + to))
        return pairs

    part = rows // CHUNKS
    keys = BLOCK // CHUNKS

    sent = call(
        functools.partial(send_block_kernel, low),
        "send_block",
        (plan, lat_t),
        [((keys, width), BF16)] * CHUNKS,
        [pltpu.SMEM(plan.shape, plan.dtype), pltpu.VMEM(lat_t.shape, BF16), pltpu.SemaphoreType.DMA((COPIES + 1,))],
        flops=visit_flops,
        raw=(0, 1),
    )

    def forward(x):
        return lax.ppermute(x, "seq", [(i, (i + 1) % n_seq) for i in range(n_seq)])

    first_keys = forward(sent[0])
    grad_rows, own_ds, sel, keep, *own = call(
        functools.partial(own_kernel, low, CHUNKS - 1),
        "own_visit",
        (plan, lat_t, q_t, grad, norm_t, delta_t),
        [((columns, LAT), BF16), ((BLOCK, columns), BF16), ((8, width), F32), ((rows, width), F32)]
        + [((rows, width), BF16)] * (low - 1),
        [
            pltpu.SMEM(plan.shape, plan.dtype),
            pltpu.VMEM((BLOCK, columns), BF16),
            pltpu.VMEM((BLOCK, width), F32),
            pltpu.SemaphoreType.DMA,
        ],
        raw=(0,),
        passed=sent[1:],
    )
    far_keys = [first_keys] + [forward(x) for x in own[low - 1 :]]
    own_parts = [keep] + [lax.ppermute(own[d - 1], ("seq", "head"), route(d, 0)) for d in range(1, low)]

    far_ds, far_parts = [], []
    for c in range(CHUNKS):
        ds, *far = call(
            functools.partial(far_kernel, low),
            f"far_visit_{c}",
            (far_keys[c], q_t, grad_rows, norm_t, delta_t, *(own_parts[1:] if c else ())),
            [((keys, columns), BF16)] + [((part, width), BF16)] * low,
            [pltpu.VMEM((keys, columns), BF16), pltpu.VMEM((keys, width), F32)],
        )
        far_ds.append(ds)
        far_parts.append([lax.ppermute(far[d], ("seq", "head"), route(d, 1)) for d in reversed(range(low))])

    mine, got = [None] * CHUNKS, [None] * CHUNKS
    for c in reversed(range(CHUNKS)):
        send, mine[c] = call(
            functools.partial(combine_kernel, low, c),
            f"combine_{c}",
            (sel, *far_parts[c], *own_parts),
            [((part, width), BF16), ((part, width), F32)],
        )
        got[c] = lax.ppermute(send, "head", [(j, (j + low) % n_head) for j in range(n_head)])

    (query_t,) = call(
        query_kernel,
        "query_grad",
        (plan, lat_t, own_ds, *far_keys, *far_ds),
        [((heads, width, packet), BF16)],
        smem=(0,),
        flops=4 * columns * BLOCK * width,
    )
    (latent_out,) = call(last_kernel, "last_sum", (*mine[::-1], *got[::-1]), [((rows, width), BF16)])
    return jnp.transpose(query_t, (2, 0, 1)), latent_out


def solution(mesh):
    return jax.shard_map(
        local,
        mesh=mesh,
        in_specs=(
            P("seq", "head", None),
            P("seq", "head", None),
            P("seq", None),
            P("seq", "head"),
            P("seq", "head"),
            P("seq", None),
        ),
        out_specs=(P("seq", "head", None), P(("seq", "head"), None)),
        check_vma=False,
    )
```

```python
import functools

import jax
import jax.numpy as jnp
from jax import lax
from jax.experimental import pallas as pl
from jax.experimental.pallas import tpu as pltpu
from jax.sharding import PartitionSpec as P

LAT = 512
PACKET = 128
BLOCK = 384
SHARD = 768
WIDE = 256
VMEM_LIMIT = 24 * 2**20
NEVER = 1e30
CHUNKS = 2
COPIES = 1

F32 = jnp.float32
BF16 = jnp.bfloat16


def dot(a, b):
    return lax.dot_general(a, b, (((1,), (0,)), ((), ())), preferred_element_type=F32)


def dot_nt(a, b):
    return lax.dot_general(a, b, (((1,), (1,)), ((), ())), preferred_element_type=F32)


def block_of(lat_ref, block):
    return lat_ref[:, pl.ds(pl.multiple_of(block * BLOCK, 128), BLOCK)]


def send_block_kernel(low, plan_hbm, lat_hbm, *rest):
    out_refs = rest[:CHUNKS]
    plan_ref, lat_ref, sems = rest[CHUNKS:]
    step = lat_ref.shape[0] // COPIES
    copies = [pltpu.make_async_copy(plan_hbm, plan_ref, sems.at[COPIES])]
    for i in range(COPIES):
        here = pl.ds(i * step, step)
        copies.append(pltpu.make_async_copy(lat_hbm.at[here], lat_ref.at[here], sems.at[i]))
    for copy in copies:
        copy.start()
    for copy in copies:
        copy.wait()
    keys = block_of(lat_ref, plan_ref[0, 1]).T
    rows = BLOCK // low
    part = rows // CHUNKS
    for c, out_ref in enumerate(out_refs):
        for j in range(low):
            start = j * rows + c * part
            out_ref[j * part : (j + 1) * part, :] = keys[start : start + part, :]


def heads_side_by_side(q_ref, first, count):
    return jnp.concatenate([q_ref[first + i] for i in range(count)], axis=1)


def visit(keys, q_ref, grad_ref, norm_ref, delta_ref, live, visible, ds_ref, p_ref, grad_out_ref):
    heads = q_ref.shape[0]
    per = WIDE // PACKET
    for first in range(0, heads, per):
        cols = slice(first * PACKET, (first + per) * PACKET)
        scores = dot(keys, heads_side_by_side(q_ref, first, per))
        prob_grad = dot_nt(keys[:, :LAT], grad_ref[cols, :])
        for i in range(per):
            lanes = slice(i * PACKET, (i + 1) * PACKET)
            norm = norm_ref[first + i : first + i + 1, :].astype(F32)
            if live is not None:
                norm = jnp.where(live, norm, NEVER)
            delta = delta_ref[first + i : first + i + 1, :].astype(F32)
            prob = jnp.exp(scores[:, lanes] - norm)
            if visible is not None:
                tail = jnp.where(visible[-PACKET:], prob[-PACKET:], 0.0)
                prob = jnp.concatenate([prob[:-PACKET], tail], axis=0)
            here = slice((first + i) * PACKET, (first + i + 1) * PACKET)
            ds_ref[:, here] = (prob * (prob_grad[:, lanes] - delta)).astype(BF16)
            p_ref[:, here] = prob.astype(BF16)
    key_grad = dot_nt(ds_ref[...], heads_side_by_side(q_ref, 0, heads))
    value_grad = dot(p_ref[...], grad_ref[...])
    grad_out_ref[:, :LAT] = key_grad[:, :LAT] + value_grad
    grad_out_ref[:, LAT:] = key_grad[:, LAT:]


def pieces_out(total_ref, low, offset, out_refs):
    rows = total_ref.shape[0] // low
    r = lax.rem(lax.axis_index("head"), low)
    for d, out_ref in out_refs:
        start = pl.multiple_of(lax.rem(r + d, low) * rows, 16) + offset
        out_ref[...] = total_ref[pl.ds(start, out_ref.shape[0]), :].astype(out_ref.dtype)


def own_kernel(low, plan_ref, lat_ref, q_ref, grad_ref, norm_ref, delta_ref, *rest):
    rows_ref, ds_ref, sel_ref, keep_ref = rest[:4]
    out_refs = rest[4:-2]
    p_ref, total_ref = rest[-2:]
    heads = q_ref.shape[0]
    group = WIDE // heads
    at = lax.broadcasted_iota(jnp.int32, (WIDE, WIDE), 0)
    come = lax.broadcasted_iota(jnp.int32, (WIDE, WIDE), 1)
    order = (come == lax.rem(at, group) * heads + lax.div(at, group)).astype(F32).astype(BF16)
    for g in range(PACKET // group):
        moved = dot(order, grad_ref[g * WIDE : (g + 1) * WIDE, :]).astype(BF16)
        for h in range(heads):
            rows_ref[h * PACKET + g * group : h * PACKET + (g + 1) * group, :] = moved[h * group : (h + 1) * group, :]
    b0, b1 = plan_ref[0:1, 0:1], plan_ref[0:1, 1:2]
    t = lax.div(lax.axis_index("head"), low)
    for i, hit in enumerate((b0 == t, b0 != t, b1 == t, b1 != t)):
        sel_ref[i : i + 1, :] = jnp.broadcast_to(jnp.where(hit, 1.0, 0.0), (1, sel_ref.shape[1])).astype(F32)
    last = jnp.where(b0 > 0, 1.0, 0.0).astype(BF16)
    first = jnp.where(b0 > 0, 0.0, 1.0).astype(BF16)
    keys = (lat_ref[:, :BLOCK] * first + lat_ref[:, BLOCK:] * last).T
    k_pos = b0 * BLOCK + lax.broadcasted_iota(jnp.int32, (BLOCK, PACKET), 0)
    q_pos = SHARD - PACKET + lax.broadcasted_iota(jnp.int32, (BLOCK, PACKET), 1)
    visit(keys, q_ref, rows_ref, norm_ref, delta_ref, None, k_pos <= q_pos, ds_ref, p_ref, total_ref)
    pieces_out(total_ref, low, 0, [(0, keep_ref)])
    for i, out_ref in enumerate(out_refs):
        part = out_ref.shape[0]
        pieces_out(total_ref, low, i % CHUNKS * part, [(1 + i // CHUNKS, out_ref)])


def far_kernel(low, held, keys_ref, q_ref, grad_ref, norm_ref, delta_ref, *rest):
    ds_ref = rest[held]
    out_refs = rest[held + 1 : held + 1 + low]
    p_ref, total_ref = rest[-2:]
    live = lax.axis_index("seq") > 0
    visit(keys_ref[...], q_ref, grad_ref, norm_ref, delta_ref, live, None, ds_ref, p_ref, total_ref)
    pieces_out(total_ref, low, 0, list(enumerate(out_refs)))


def query_kernel(plan_ref, lat_ref, own_ds_ref, *rest):
    far_refs = rest[:CHUNKS]
    far_ds_refs = rest[CHUNKS : 2 * CHUNKS]
    out_ref = rest[-1]
    heads = out_ref.shape[0]
    per = WIDE // PACKET
    own = block_of(lat_ref, plan_ref[0, 0])
    fars = [ref[...].T for ref in far_refs]
    for first in range(0, heads, per):
        cols = slice(first * PACKET, (first + per) * PACKET)
        total = dot(own, own_ds_ref[:, cols])
        for far, ds_ref in zip(fars, far_ds_refs):
            total = total + dot(far, ds_ref[:, cols])
        for i in range(per):
            out_ref[first + i] = total[:, i * PACKET : (i + 1) * PACKET].astype(BF16)


def combine_kernel(low, chunk, sel_ref, *rest):
    own_refs = rest[:low]
    far_refs = rest[low : 2 * low]
    send_ref, mine_ref = rest[-2:]
    part = send_ref.shape[0]
    here = slice(chunk * part, (chunk + 1) * part)
    own = own_refs[0][here, :]
    for ref in own_refs[1:]:
        own = own + ref[...].astype(F32)
    far = far_refs[0][...].astype(F32)
    for ref in far_refs[1:]:
        far = far + ref[...].astype(F32)
    send_ref[...] = (own * sel_ref[1:2, :] + far * sel_ref[3:4, :]).astype(BF16)
    mine_ref[...] = own * sel_ref[0:1, :] + far * sel_ref[2:3, :]


def last_kernel(*refs):
    mine_refs, got_refs, out_ref = refs[:CHUNKS][::-1], refs[CHUNKS : 2 * CHUNKS][::-1], refs[-1]
    part = out_ref.shape[0] // CHUNKS
    for c in range(CHUNKS):
        out_ref[c * part : (c + 1) * part, :] = (mine_refs[c][...] + got_refs[c][...].astype(F32)).astype(BF16)


def call(kernel, name, ins, outs, scratch=(), smem=(), raw=(), passed=(), flops=0, transcendentals=0):
    spaces = [pltpu.SMEM if i in smem else pltpu.VMEM for i in range(len(ins))]
    ins = list(ins)
    for i in raw:
        spaces[i] = pl.ANY
        ins[i] = pltpu.with_memory_space_constraint(ins[i], pltpu.HBM)
    size = sum(x.size * x.dtype.itemsize for x in ins)
    size += sum(functools.reduce(lambda a, b: a * b, s, jnp.dtype(d).itemsize) for s, d in outs)
    out_spaces = [pltpu.VMEM] * len(outs) + [pl.ANY] * len(passed)
    shapes = [jax.ShapeDtypeStruct(s, d) for s, d in outs]
    shapes += [jax.ShapeDtypeStruct(x.shape, x.dtype) for x in passed]
    aliases = {len(ins) + i: len(outs) + i for i in range(len(passed))}
    return pl.pallas_call(
        kernel,
        name=name,
        out_shape=shapes,
        in_specs=[pl.BlockSpec(memory_space=space) for space in spaces + [pl.ANY] * len(passed)],
        out_specs=[pl.BlockSpec(memory_space=space) for space in out_spaces],
        scratch_shapes=scratch,
        input_output_aliases=aliases,
        compiler_params=pltpu.CompilerParams(vmem_limit_bytes=VMEM_LIMIT),
        cost_estimate=pl.CostEstimate(flops=flops, bytes_accessed=size, transcendentals=transcendentals),
    )(*ins, *passed)


def local(queries, out_grad, latents, log_norm, out_delta, plan):
    n_seq = lax.axis_size("seq")
    n_head = lax.axis_size("head")
    low = n_head // 2
    rows = BLOCK // low
    packet, heads, width = queries.shape
    columns = packet * heads

    lat_t = latents.T
    q_t = jnp.transpose(queries, (1, 2, 0))
    grad = out_grad.reshape(columns, LAT)
    norm_t = log_norm.T
    delta_t = out_delta.T
    visit_flops = 2 * columns * BLOCK * (2 * width + 2 * LAT)

    def route(d, back):
        pairs = []
        for i in range(n_seq):
            for j in range(n_head):
                to = j // low * low + (j + d) % low
                pairs.append((i * n_head + j, (i - back) % n_seq * n_head + to))
        return pairs

    part = rows // CHUNKS
    keys = BLOCK // CHUNKS

    sent = call(
        functools.partial(send_block_kernel, low),
        "send_block",
        (plan, lat_t),
        [((keys, width), BF16)] * CHUNKS,
        [pltpu.SMEM(plan.shape, plan.dtype), pltpu.VMEM(lat_t.shape, BF16), pltpu.SemaphoreType.DMA((COPIES + 1,))],
        flops=visit_flops,
        raw=(0, 1),
    )
    far_keys = [lax.ppermute(x, "seq", [(i, (i + 1) % n_seq) for i in range(n_seq)]) for x in sent]

    grad_rows, own_ds, sel, keep, *own = call(
        functools.partial(own_kernel, low),
        "own_visit",
        (plan, lat_t, q_t, grad, norm_t, delta_t),
        [((columns, LAT), BF16), ((BLOCK, columns), BF16), ((8, width), F32), ((rows, width), F32)]
        + [((part, width), BF16)] * (CHUNKS * (low - 1)),
        [pltpu.VMEM((BLOCK, columns), BF16), pltpu.VMEM((BLOCK, width), F32)],
    )

    far_ds, own_parts, far_parts = [], [], []
    for c in range(CHUNKS):
        later = [i for i in range(len(own)) if i % CHUNKS and i % CHUNKS >= c]
        ds, *far = call(
            functools.partial(far_kernel, low, len(later)),
            f"far_visit_{c}",
            (far_keys[c], q_t, grad_rows, norm_t, delta_t),
            [((keys, columns), BF16)] + [((part, width), BF16)] * low,
            [pltpu.VMEM((keys, columns), BF16), pltpu.VMEM((keys, width), F32)],
            passed=[own[i] for i in later],
        )
        for i, x in zip(later, far[low:]):
            own[i] = x
        parts = own[c::CHUNKS]
        own_parts.append([keep] + [lax.ppermute(parts[d - 1], ("seq", "head"), route(d, 0)) for d in range(1, low)])
        far_ds.append(ds)
        far_parts.append([lax.ppermute(far[d], ("seq", "head"), route(d, 1)) for d in reversed(range(low))])

    mine, got = [None] * CHUNKS, [None] * CHUNKS
    for c in reversed(range(CHUNKS)):
        send, mine[c] = call(
            functools.partial(combine_kernel, low, c),
            f"combine_{c}",
            (sel, *own_parts[c], *far_parts[c]),
            [((part, width), BF16), ((part, width), F32)],
        )
        got[c] = lax.ppermute(send, "head", [(j, (j + low) % n_head) for j in range(n_head)])

    (query_t,) = call(
        query_kernel,
        "query_grad",
        (plan, lat_t, own_ds, *far_keys, *far_ds),
        [((heads, width, packet), BF16)],
        smem=(0,),
        flops=4 * columns * BLOCK * width,
    )
    (latent_out,) = call(last_kernel, "last_sum", (*mine[::-1], *got[::-1]), [((rows, width), BF16)])
    return jnp.transpose(query_t, (2, 0, 1)), latent_out


def solution(mesh):
    return jax.shard_map(
        local,
        mesh=mesh,
        in_specs=(
            P("seq", "head", None),
            P("seq", "head", None),
            P("seq", None),
            P("seq", "head"),
            P("seq", "head"),
            P("seq", None),
        ),
        out_specs=(P("seq", "head", None), P(("seq", "head"), None)),
        check_vma=False,
    )
```

```python
import functools

import jax
import jax.numpy as jnp
from jax import lax
from jax.experimental import pallas as pl
from jax.experimental.pallas import tpu as pltpu
from jax.sharding import PartitionSpec as P

LAT = 512
PACKET = 128
BLOCK = 384
SHARD = 768
WIDE = 256
VMEM_LIMIT = 24 * 2**20
NEVER = 1e30
CHUNKS = 2
FIRST_SHARE = 1 / 2

F32 = jnp.float32
BF16 = jnp.bfloat16


def dot(a, b):
    return lax.dot_general(a, b, (((1,), (0,)), ((), ())), preferred_element_type=F32)


def dot_nt(a, b):
    return lax.dot_general(a, b, (((1,), (1,)), ((), ())), preferred_element_type=F32)


def block_of(lat_ref, block):
    return lat_ref[:, pl.ds(pl.multiple_of(block * BLOCK, 128), BLOCK)]


def chunks_of(rows):
    first = -(-int(rows * FIRST_SHARE) // 16) * 16
    return [(0, first), (first, rows - first)]


def send_block_kernel(low, plan_hbm, lat_hbm, *rest):
    out_refs = rest[:CHUNKS]
    plan_ref, lat_ref, sems = rest[CHUNKS:]
    copies = [
        pltpu.make_async_copy(plan_hbm, plan_ref, sems.at[0]),
        pltpu.make_async_copy(lat_hbm, lat_ref, sems.at[1]),
    ]
    for copy in copies:
        copy.start()
    for copy in copies:
        copy.wait()
    keys = block_of(lat_ref, plan_ref[0, 1]).T
    rows = BLOCK // low
    for (offset, part), out_ref in zip(chunks_of(rows), out_refs):
        for j in range(low):
            start = j * rows + offset
            out_ref[j * part : (j + 1) * part, :] = keys[start : start + part, :]


def heads_side_by_side(q_ref, first, count):
    return jnp.concatenate([q_ref[first + i] for i in range(count)], axis=1)


def visit(keys, q_ref, grad_ref, norm_ref, delta_ref, live, visible, ds_ref, p_ref, grad_out_ref):
    heads = q_ref.shape[0]
    per = WIDE // PACKET
    for first in range(0, heads, per):
        cols = slice(first * PACKET, (first + per) * PACKET)
        scores = dot(keys, heads_side_by_side(q_ref, first, per))
        prob_grad = dot_nt(keys[:, :LAT], grad_ref[cols, :])
        for i in range(per):
            lanes = slice(i * PACKET, (i + 1) * PACKET)
            norm = norm_ref[first + i : first + i + 1, :].astype(F32)
            if live is not None:
                norm = jnp.where(live, norm, NEVER)
            delta = delta_ref[first + i : first + i + 1, :].astype(F32)
            prob = jnp.exp(scores[:, lanes] - norm)
            if visible is not None:
                tail = jnp.where(visible[-PACKET:], prob[-PACKET:], 0.0)
                prob = jnp.concatenate([prob[:-PACKET], tail], axis=0)
            here = slice((first + i) * PACKET, (first + i + 1) * PACKET)
            ds_ref[:, here] = (prob * (prob_grad[:, lanes] - delta)).astype(BF16)
            p_ref[:, here] = prob.astype(BF16)
    key_grad = dot_nt(ds_ref[...], heads_side_by_side(q_ref, 0, heads))
    value_grad = dot(p_ref[...], grad_ref[...])
    grad_out_ref[:, :LAT] = key_grad[:, :LAT] + value_grad
    grad_out_ref[:, LAT:] = key_grad[:, LAT:]


def pieces_out(total_ref, low, offset, out_refs):
    rows = total_ref.shape[0] // low
    r = lax.rem(lax.axis_index("head"), low)
    for d, out_ref in out_refs:
        start = pl.multiple_of(lax.rem(r + d, low) * rows, 16) + offset
        out_ref[...] = total_ref[pl.ds(start, out_ref.shape[0]), :].astype(out_ref.dtype)


def own_kernel(low, plan_ref, lat_ref, q_ref, grad_ref, norm_ref, delta_ref, *rest):
    rows_ref, ds_ref, sel_ref, keep_ref = rest[:4]
    out_refs = rest[4:-2]
    p_ref, total_ref = rest[-2:]
    heads = q_ref.shape[0]
    group = WIDE // heads
    at = lax.broadcasted_iota(jnp.int32, (WIDE, WIDE), 0)
    come = lax.broadcasted_iota(jnp.int32, (WIDE, WIDE), 1)
    order = (come == lax.rem(at, group) * heads + lax.div(at, group)).astype(F32).astype(BF16)
    for g in range(PACKET // group):
        moved = dot(order, grad_ref[g * WIDE : (g + 1) * WIDE, :]).astype(BF16)
        for h in range(heads):
            rows_ref[h * PACKET + g * group : h * PACKET + (g + 1) * group, :] = moved[h * group : (h + 1) * group, :]
    b0, b1 = plan_ref[0:1, 0:1], plan_ref[0:1, 1:2]
    t = lax.div(lax.axis_index("head"), low)
    for i, hit in enumerate((b0 == t, b0 != t, b1 == t, b1 != t)):
        sel_ref[i : i + 1, :] = jnp.broadcast_to(jnp.where(hit, 1.0, 0.0), (1, sel_ref.shape[1])).astype(F32)
    last = jnp.where(b0 > 0, 1.0, 0.0).astype(BF16)
    first = jnp.where(b0 > 0, 0.0, 1.0).astype(BF16)
    keys = (lat_ref[:, :BLOCK] * first + lat_ref[:, BLOCK:] * last).T
    k_pos = b0 * BLOCK + lax.broadcasted_iota(jnp.int32, (BLOCK, PACKET), 0)
    q_pos = SHARD - PACKET + lax.broadcasted_iota(jnp.int32, (BLOCK, PACKET), 1)
    visit(keys, q_ref, rows_ref, norm_ref, delta_ref, None, k_pos <= q_pos, ds_ref, p_ref, total_ref)
    pieces_out(total_ref, low, 0, [(0, keep_ref)])
    pieces_out(total_ref, low, 0, list(enumerate(out_refs, 1)))


def far_kernel(low, keys_ref, q_ref, grad_ref, norm_ref, delta_ref, *rest):
    ds_ref = rest[0]
    out_refs = rest[1 : 1 + low]
    p_ref, total_ref = rest[-2:]
    live = lax.axis_index("seq") > 0
    visit(keys_ref[...], q_ref, grad_ref, norm_ref, delta_ref, live, None, ds_ref, p_ref, total_ref)
    pieces_out(total_ref, low, 0, list(enumerate(out_refs)))


def query_kernel(plan_ref, lat_ref, own_ds_ref, *rest):
    far_refs = rest[:CHUNKS]
    far_ds_refs = rest[CHUNKS : 2 * CHUNKS]
    out_ref = rest[-1]
    heads = out_ref.shape[0]
    per = WIDE // PACKET
    own = block_of(lat_ref, plan_ref[0, 0])
    fars = [ref[...].T for ref in far_refs]
    for first in range(0, heads, per):
        cols = slice(first * PACKET, (first + per) * PACKET)
        total = dot(own, own_ds_ref[:, cols])
        for far, ds_ref in zip(fars, far_ds_refs):
            total = total + dot(far, ds_ref[:, cols])
        for i in range(per):
            out_ref[first + i] = total[:, i * PACKET : (i + 1) * PACKET].astype(BF16)


def combine_kernel(low, offset, sel_ref, *rest):
    own_refs = rest[:low]
    far_refs = rest[low : 2 * low]
    send_ref, mine_ref = rest[-2:]
    part = send_ref.shape[0]
    here = slice(offset, offset + part)
    own = own_refs[0][here, :]
    for ref in own_refs[1:]:
        own = own + ref[here, :].astype(F32)
    far = far_refs[0][...].astype(F32)
    for ref in far_refs[1:]:
        far = far + ref[...].astype(F32)
    send_ref[...] = (own * sel_ref[1:2, :] + far * sel_ref[3:4, :]).astype(BF16)
    mine_ref[...] = own * sel_ref[0:1, :] + far * sel_ref[2:3, :]


def last_kernel(*refs):
    mine_refs, got_refs, out_ref = refs[:CHUNKS][::-1], refs[CHUNKS : 2 * CHUNKS][::-1], refs[-1]
    for (offset, part), mine_ref, got_ref in zip(chunks_of(out_ref.shape[0]), mine_refs, got_refs):
        out_ref[offset : offset + part, :] = (mine_ref[...] + got_ref[...].astype(F32)).astype(BF16)


def call(kernel, name, ins, outs, scratch=(), smem=(), raw=(), flops=0, size=None):
    spaces = [pltpu.SMEM if i in smem else pltpu.VMEM for i in range(len(ins))]
    ins = list(ins)
    for i in raw:
        spaces[i] = pl.ANY
        ins[i] = pltpu.with_memory_space_constraint(ins[i], pltpu.HBM)
    if size is None:
        size = sum(x.size * x.dtype.itemsize for x in ins)
        size += sum(functools.reduce(lambda a, b: a * b, s, jnp.dtype(d).itemsize) for s, d in outs)
    return pl.pallas_call(
        kernel,
        name=name,
        out_shape=[jax.ShapeDtypeStruct(s, d) for s, d in outs],
        in_specs=[pl.BlockSpec(memory_space=space) for space in spaces],
        out_specs=[pl.BlockSpec(memory_space=pltpu.VMEM) for _ in outs],
        scratch_shapes=scratch,
        compiler_params=pltpu.CompilerParams(vmem_limit_bytes=VMEM_LIMIT),
        cost_estimate=pl.CostEstimate(flops=flops, bytes_accessed=size, transcendentals=0),
    )(*ins)


def local(queries, out_grad, latents, log_norm, out_delta, plan):
    n_seq = lax.axis_size("seq")
    n_head = lax.axis_size("head")
    low = n_head // 2
    rows = BLOCK // low
    packet, heads, width = queries.shape
    columns = packet * heads

    lat_t = latents.T
    q_t = jnp.transpose(queries, (1, 2, 0))
    grad = out_grad.reshape(columns, LAT)
    norm_t = log_norm.T
    delta_t = out_delta.T
    visit_flops = 2 * columns * BLOCK * (2 * width + 2 * LAT)

    def route(d, back):
        pairs = []
        for i in range(n_seq):
            for j in range(n_head):
                to = j // low * low + (j + d) % low
                pairs.append((i * n_head + j, (i - back) % n_seq * n_head + to))
        return pairs

    chunks = chunks_of(rows)

    sent = call(
        functools.partial(send_block_kernel, low),
        "send_block",
        (plan, lat_t),
        [((low * part, width), BF16) for _, part in chunks],
        [pltpu.SMEM(plan.shape, plan.dtype), pltpu.VMEM(lat_t.shape, BF16), pltpu.SemaphoreType.DMA((2,))],
        flops=visit_flops,
        raw=(0, 1),
    )
    far_keys = [lax.ppermute(x, "seq", [(i, (i + 1) % n_seq) for i in range(n_seq)]) for x in sent]

    grad_rows, own_ds, sel, keep, *own = call(
        functools.partial(own_kernel, low),
        "own_visit",
        (plan, lat_t, q_t, grad, norm_t, delta_t),
        [((columns, LAT), BF16), ((BLOCK, columns), BF16), ((8, width), F32), ((rows, width), F32)]
        + [((rows, width), BF16)] * (low - 1),
        [pltpu.VMEM((BLOCK, columns), BF16), pltpu.VMEM((BLOCK, width), F32)],
    )
    own_parts = [keep] + [lax.ppermute(own[d - 1], ("seq", "head"), route(d, 0)) for d in range(1, low)]

    far_ds, far_parts = [], []
    for c, (_, part) in enumerate(chunks):
        keys = low * part
        ds, *far = call(
            functools.partial(far_kernel, low),
            f"far_visit_{c}",
            (far_keys[c], q_t, grad_rows, norm_t, delta_t),
            [((keys, columns), BF16)] + [((part, width), BF16)] * low,
            [pltpu.VMEM((keys, columns), BF16), pltpu.VMEM((keys, width), F32)],
            size=0,
        )
        far_ds.append(ds)
        far_parts.append([lax.ppermute(far[d], ("seq", "head"), route(d, 1)) for d in reversed(range(low))])

    mine, got = [None] * CHUNKS, [None] * CHUNKS
    for c, (offset, part) in reversed(list(enumerate(chunks))):
        send, mine[c] = call(
            functools.partial(combine_kernel, low, offset),
            f"combine_{c}",
            (sel, *own_parts, *far_parts[c]),
            [((part, width), BF16), ((part, width), F32)],
        )
        got[c] = lax.ppermute(send, "head", [(j, (j + low) % n_head) for j in range(n_head)])

    (query_t,) = call(
        query_kernel,
        "query_grad",
        (plan, lat_t, own_ds, *far_keys, *far_ds),
        [((heads, width, packet), BF16)],
        smem=(0,),
        flops=4 * columns * BLOCK * width,
    )
    (latent_out,) = call(last_kernel, "last_sum", (*mine[::-1], *got[::-1]), [((rows, width), BF16)])
    return jnp.transpose(query_t, (2, 0, 1)), latent_out


def solution(mesh):
    return jax.shard_map(
        local,
        mesh=mesh,
        in_specs=(
            P("seq", "head", None),
            P("seq", "head", None),
            P("seq", None),
            P("seq", "head"),
            P("seq", "head"),
            P("seq", None),
        ),
        out_specs=(P("seq", "head", None), P(("seq", "head"), None)),
        check_vma=False,
    )
```

```python
import functools

import jax
import jax.numpy as jnp
from jax import lax
from jax.experimental import pallas as pl
from jax.experimental.pallas import tpu as pltpu
from jax.sharding import PartitionSpec as P

LAT = 512
PACKET = 128
BLOCK = 384
SHARD = 768
WIDE = 256
VMEM_LIMIT = 24 * 2**20
NEVER = 1e30
CHUNKS = 2
FIRST_SHARE = 1 / 2

F32 = jnp.float32
BF16 = jnp.bfloat16


def dot(a, b):
    return lax.dot_general(a, b, (((1,), (0,)), ((), ())), preferred_element_type=F32)


def dot_nt(a, b):
    return lax.dot_general(a, b, (((1,), (1,)), ((), ())), preferred_element_type=F32)


def chunks_of(rows):
    first = -(-int(rows * FIRST_SHARE) // 16) * 16
    return [(0, first), (first, rows - first)]


def chunk_rows(keys, low, out_refs):
    rows = BLOCK // low
    for (offset, part), out_ref in zip(chunks_of(rows), out_refs):
        for j in range(low):
            start = j * rows + offset
            out_ref[j * part : (j + 1) * part, :] = keys[start : start + part, :]


def send_block_kernel(low, plan_hbm, lat_hbm, *rest):
    out_refs = rest[:CHUNKS]
    plan_ref, lat_ref, sems = rest[CHUNKS:]
    copies = [
        pltpu.make_async_copy(plan_hbm, plan_ref, sems.at[0]),
        pltpu.make_async_copy(lat_hbm, lat_ref, sems.at[1]),
    ]
    for copy in copies:
        copy.start()
    for copy in copies:
        copy.wait()
    block = pl.multiple_of(plan_ref[0, 1] * BLOCK, 128)
    chunk_rows(lat_ref[:, pl.ds(block, BLOCK)].T, low, out_refs)


def heads_side_by_side(q_ref, first, count):
    return jnp.concatenate([q_ref[first + i] for i in range(count)], axis=1)


def visit(keys, q_ref, grad_ref, norm_ref, delta_ref, live, visible, ds_ref, p_ref, grad_out_ref):
    heads = q_ref.shape[0]
    per = WIDE // PACKET
    for first in range(0, heads, per):
        cols = slice(first * PACKET, (first + per) * PACKET)
        scores = dot(keys, heads_side_by_side(q_ref, first, per))
        prob_grad = dot_nt(keys[:, :LAT], grad_ref[cols, :])
        for i in range(per):
            lanes = slice(i * PACKET, (i + 1) * PACKET)
            norm = norm_ref[first + i : first + i + 1, :].astype(F32)
            if live is not None:
                norm = jnp.where(live, norm, NEVER)
            delta = delta_ref[first + i : first + i + 1, :].astype(F32)
            prob = jnp.exp(scores[:, lanes] - norm)
            if visible is not None:
                prob = jnp.where(visible, prob, 0.0)
            here = slice((first + i) * PACKET, (first + i + 1) * PACKET)
            ds_ref[:, here] = (prob * (prob_grad[:, lanes] - delta)).astype(BF16)
            p_ref[:, here] = prob.astype(BF16)
    key_grad = dot_nt(ds_ref[...], heads_side_by_side(q_ref, 0, heads))
    value_grad = dot(p_ref[...], grad_ref[...])
    grad_out_ref[:, :LAT] = key_grad[:, :LAT] + value_grad
    grad_out_ref[:, LAT:] = key_grad[:, LAT:]


def pieces_out(total_ref, low, offset, out_refs):
    rows = total_ref.shape[0] // low
    r = lax.rem(lax.axis_index("head"), low)
    for d, out_ref in out_refs:
        start = pl.multiple_of(lax.rem(r + d, low) * rows, 16) + offset
        out_ref[...] = total_ref[pl.ds(start, out_ref.shape[0]), :].astype(out_ref.dtype)


def own_chunk(plan_ref, keys, offset, part, refs, low, q_ref, rows_ref, norm_ref, delta_ref):
    ds_ref, keep_ref, *out_refs, p_ref, total_ref = refs
    rows = BLOCK // low
    at = lax.broadcasted_iota(jnp.int32, (part, PACKET), 0)
    at = jnp.concatenate([at + (j * rows + offset) for j in range(low)], axis=0)
    k_pos = plan_ref[0:1, 0:1] * BLOCK + at
    q_pos = SHARD - PACKET + lax.broadcasted_iota(jnp.int32, at.shape, 1)
    visit(keys, q_ref, rows_ref, norm_ref, delta_ref, None, k_pos <= q_pos, ds_ref, p_ref, total_ref)
    pieces_out(total_ref, low, 0, list(enumerate([keep_ref, *out_refs])))


def own_first_kernel(low, held, plan_ref, lat_ref, q_ref, grad_ref, norm_ref, delta_ref, *rest):
    rest = rest[held:]
    rows_ref, sel_ref = rest[:2]
    keys_refs = rest[2 : 2 + CHUNKS]
    ds_ref, keep_ref = rest[2 + CHUNKS : 4 + CHUNKS]
    out_refs = rest[4 + CHUNKS : 3 + CHUNKS + low]
    heads = q_ref.shape[0]
    group = WIDE // heads
    at = lax.broadcasted_iota(jnp.int32, (WIDE, WIDE), 0)
    come = lax.broadcasted_iota(jnp.int32, (WIDE, WIDE), 1)
    order = (come == lax.rem(at, group) * heads + lax.div(at, group)).astype(F32).astype(BF16)
    for g in range(PACKET // group):
        moved = dot(order, grad_ref[g * WIDE : (g + 1) * WIDE, :]).astype(BF16)
        for h in range(heads):
            rows_ref[h * PACKET + g * group : h * PACKET + (g + 1) * group, :] = moved[h * group : (h + 1) * group, :]
    b0, b1 = plan_ref[0:1, 0:1], plan_ref[0:1, 1:2]
    t = lax.div(lax.axis_index("head"), low)
    for i, hit in enumerate((b0 == t, b0 != t, b1 == t, b1 != t)):
        sel_ref[i : i + 1, :] = jnp.broadcast_to(jnp.where(hit, 1.0, 0.0), (1, sel_ref.shape[1])).astype(F32)
    last = jnp.where(b0 > 0, 1.0, 0.0).astype(BF16)
    first = jnp.where(b0 > 0, 0.0, 1.0).astype(BF16)
    keys = (lat_ref[:, :BLOCK] * first + lat_ref[:, BLOCK:] * last).T
    chunk_rows(keys, low, keys_refs)
    (offset, part), *_ = chunks_of(BLOCK // low)
    refs = [ds_ref, keep_ref, *out_refs, *rest[-2:]]
    own_chunk(plan_ref, keys_refs[0][...], offset, part, refs, low, q_ref, rows_ref, norm_ref, delta_ref)


def own_next_kernel(low, offset, plan_ref, keys_ref, q_ref, rows_ref, norm_ref, delta_ref, *rest):
    part = keys_ref.shape[0] // low
    own_chunk(plan_ref, keys_ref[...], offset, part, rest, low, q_ref, rows_ref, norm_ref, delta_ref)


def far_kernel(low, keys_ref, q_ref, grad_ref, norm_ref, delta_ref, *rest):
    ds_ref = rest[-3 - low]
    out_refs = rest[-2 - low : -2]
    p_ref, total_ref = rest[-2:]
    live = lax.axis_index("seq") > 0
    visit(keys_ref[...], q_ref, grad_ref, norm_ref, delta_ref, live, None, ds_ref, p_ref, total_ref)
    pieces_out(total_ref, low, 0, list(enumerate(out_refs)))


def query_kernel(*refs):
    count = len(refs) // 2
    keys_refs, ds_refs, out_ref = refs[:count], refs[count:-1], refs[-1]
    heads = out_ref.shape[0]
    per = WIDE // PACKET
    keys = [ref[...].T for ref in keys_refs]
    for first in range(0, heads, per):
        cols = slice(first * PACKET, (first + per) * PACKET)
        total = sum(dot(k, ds_ref[:, cols]) for k, ds_ref in zip(keys, ds_refs))
        for i in range(per):
            out_ref[first + i] = total[:, i * PACKET : (i + 1) * PACKET].astype(BF16)


def combine_kernel(low, sel_ref, *rest):
    own_refs = rest[:low]
    far_refs = rest[low : 2 * low]
    send_ref, mine_ref = rest[-2:]
    own = own_refs[0][...]
    for ref in own_refs[1:]:
        own = own + ref[...].astype(F32)
    far = far_refs[0][...].astype(F32)
    for ref in far_refs[1:]:
        far = far + ref[...].astype(F32)
    send_ref[...] = (own * sel_ref[1:2, :] + far * sel_ref[3:4, :]).astype(BF16)
    mine_ref[...] = own * sel_ref[0:1, :] + far * sel_ref[2:3, :]


def last_kernel(*refs):
    mine_refs, got_refs, out_ref = refs[:CHUNKS][::-1], refs[CHUNKS : 2 * CHUNKS][::-1], refs[-1]
    for (offset, part), mine_ref, got_ref in zip(chunks_of(out_ref.shape[0]), mine_refs, got_refs):
        out_ref[offset : offset + part, :] = (mine_ref[...] + got_ref[...].astype(F32)).astype(BF16)


def call(kernel, name, ins, outs, scratch=(), raw=(), passed=(), flops=0, size=0):
    spaces = [pltpu.VMEM] * len(ins) + [pl.ANY] * len(passed)
    ins = list(ins)
    for i in raw:
        spaces[i] = pl.ANY
        ins[i] = pltpu.with_memory_space_constraint(ins[i], pltpu.HBM)
    shapes = [jax.ShapeDtypeStruct(s, d) for s, d in outs]
    shapes += [jax.ShapeDtypeStruct(x.shape, x.dtype) for x in passed]
    return pl.pallas_call(
        kernel,
        name=name,
        out_shape=shapes,
        in_specs=[pl.BlockSpec(memory_space=space) for space in spaces],
        out_specs=[pl.BlockSpec(memory_space=space) for space in [pltpu.VMEM] * len(outs) + [pl.ANY] * len(passed)],
        scratch_shapes=scratch,
        input_output_aliases={len(ins) + i: len(outs) + i for i in range(len(passed))},
        compiler_params=pltpu.CompilerParams(vmem_limit_bytes=VMEM_LIMIT),
        cost_estimate=pl.CostEstimate(flops=flops, bytes_accessed=size, transcendentals=0),
    )(*ins, *passed)


def local(queries, out_grad, latents, log_norm, out_delta, plan):
    n_seq = lax.axis_size("seq")
    n_head = lax.axis_size("head")
    low = n_head // 2
    rows = BLOCK // low
    packet, heads, width = queries.shape
    columns = packet * heads

    lat_t = latents.T
    q_t = jnp.transpose(queries, (1, 2, 0))
    grad = out_grad.reshape(columns, LAT)
    norm_t = log_norm.T
    delta_t = out_delta.T
    visit_flops = 2 * columns * BLOCK * (2 * width + 2 * LAT)

    def route(d, back):
        pairs = []
        for i in range(n_seq):
            for j in range(n_head):
                to = j // low * low + (j + d) % low
                pairs.append((i * n_head + j, (i - back) % n_seq * n_head + to))
        return pairs

    chunks = chunks_of(rows)

    sent = call(
        functools.partial(send_block_kernel, low),
        "send_block",
        (plan, lat_t),
        [((low * part, width), BF16) for _, part in chunks],
        [pltpu.SMEM(plan.shape, plan.dtype), pltpu.VMEM(lat_t.shape, BF16), pltpu.SemaphoreType.DMA((2,))],
        flops=visit_flops,
        raw=(0, 1),
    )

    def forward(x):
        return lax.ppermute(x, "seq", [(i, (i + 1) % n_seq) for i in range(n_seq)])

    def own_outs(part):
        return [((low * part, columns), BF16), ((part, width), F32)] + [((part, width), BF16)] * (low - 1)

    def scratch(part):
        return [pltpu.VMEM((low * part, columns), BF16), pltpu.VMEM((low * part, width), F32)]

    far_keys = [forward(sent[0])]
    (_, part), *_ = chunks
    grad_rows, sel, *first = call(
        functools.partial(own_first_kernel, low, CHUNKS - 1),
        "own_visit_0",
        (plan, lat_t, q_t, grad, norm_t, delta_t),
        [((columns, LAT), BF16), ((8, width), F32)] + [((low * p, width), BF16) for _, p in chunks] + own_outs(part),
        scratch(part),
        passed=sent[1:],
    )
    own_keys, first = first[:CHUNKS], first[CHUNKS:]
    own, later = [first[: 1 + low]], first[1 + low :]
    far_keys += [forward(x) for x in later]
    for c, (offset, part) in list(enumerate(chunks))[1:]:
        own.append(
            call(
                functools.partial(own_next_kernel, low, offset),
                f"own_visit_{c}",
                (plan, own_keys[c], q_t, grad_rows, norm_t, delta_t),
                own_outs(part),
                scratch(part),
            )
        )
    own_parts = []
    for _, keep, *pieces in own:
        sends = enumerate(pieces, 1)
        own_parts.append([keep] + [lax.ppermute(x, ("seq", "head"), route(d, 0)) for d, x in sends])

    far_ds, far_parts = [], []
    for c, (_, part) in enumerate(chunks):
        ds, *far = call(
            functools.partial(far_kernel, low),
            f"far_visit_{c}",
            (far_keys[c], q_t, grad_rows, norm_t, delta_t, *(far_ds[-1:] or [own[-1][0]])),
            [((low * part, columns), BF16)] + [((part, width), BF16)] * low,
            scratch(part),
        )
        far_ds.append(ds)
        far_parts.append([lax.ppermute(far[d], ("seq", "head"), route(d, 1)) for d in reversed(range(low))])

    mine, got = [None] * CHUNKS, [None] * CHUNKS
    for c, (_, part) in reversed(list(enumerate(chunks))):
        send, mine[c] = call(
            functools.partial(combine_kernel, low),
            f"combine_{c}",
            (sel, *own_parts[c], *far_parts[c]),
            [((part, width), BF16), ((part, width), F32)],
        )
        got[c] = lax.ppermute(send, "head", [(j, (j + low) % n_head) for j in range(n_head)])

    (query_t,) = call(
        query_kernel,
        "query_grad",
        (*own_keys, *far_keys, *(x[0] for x in own), *far_ds),
        [((heads, width, packet), BF16)],
        flops=4 * columns * BLOCK * width,
    )
    (latent_out,) = call(last_kernel, "last_sum", (*mine[::-1], *got[::-1]), [((rows, width), BF16)])
    return jnp.transpose(query_t, (2, 0, 1)), latent_out


def solution(mesh):
    return jax.shard_map(
        local,
        mesh=mesh,
        in_specs=(
            P("seq", "head", None),
            P("seq", "head", None),
            P("seq", None),
            P("seq", "head"),
            P("seq", "head"),
            P("seq", None),
        ),
        out_specs=(P("seq", "head", None), P(("seq", "head"), None)),
        check_vma=False,
    )
```

```python
import functools

import jax
import jax.numpy as jnp
from jax import lax
from jax.experimental import pallas as pl
from jax.experimental.pallas import tpu as pltpu
from jax.sharding import PartitionSpec as P

LAT = 512
PACKET = 128
BLOCK = 384
SHARD = 768
WIDE = 256
VMEM_LIMIT = 24 * 2**20
NEVER = 1e30
CHUNKS = 2
FIRST_SHARE = 5 / 12
COST_SUM = 10**9
COST_COMBINE = 10**9
COST_OWN = 3 * 10**9

F32 = jnp.float32
BF16 = jnp.bfloat16


def dot(a, b):
    return lax.dot_general(a, b, (((1,), (0,)), ((), ())), preferred_element_type=F32)


def dot_nt(a, b):
    return lax.dot_general(a, b, (((1,), (1,)), ((), ())), preferred_element_type=F32)


def chunks_of(rows):
    first = -(-int(rows * FIRST_SHARE) // 16) * 16
    return [(0, first), (first, rows - first)]


def chunk_rows(keys, low, out_refs):
    rows = BLOCK // low
    for (offset, part), out_ref in zip(chunks_of(rows), out_refs):
        for j in range(low):
            start = j * rows + offset
            out_ref[j * part : (j + 1) * part, :] = keys[start : start + part, :]


def send_block_kernel(low, plan_hbm, lat_hbm, *rest):
    out_refs = rest[:CHUNKS]
    plan_ref, lat_ref, sems = rest[CHUNKS:]

    def block_copy(block):
        here = pl.ds(pl.multiple_of(block * BLOCK, 128), BLOCK)
        return pltpu.make_async_copy(lat_hbm.at[:, here], lat_ref.at[block], sems.at[block])

    blocks = lat_ref.shape[0]
    plan_copy = pltpu.make_async_copy(plan_hbm, plan_ref, sems.at[blocks])
    plan_copy.start()
    for block in range(blocks):
        block_copy(block).start()
    plan_copy.wait()
    sent = plan_ref[0, 1]
    block_copy(sent).wait()
    chunk_rows(lat_ref[sent].T, low, out_refs)
    for i in range(1, blocks):
        block_copy(lax.rem(sent + i, blocks)).wait()


def heads_side_by_side(q_ref, first, count):
    return jnp.concatenate([q_ref[first + i] for i in range(count)], axis=1)


def visit(keys, q_ref, grad_ref, norm_ref, delta_ref, live, visible, ds_ref, p_ref, grad_out_ref):
    heads = q_ref.shape[0]
    per = WIDE // PACKET
    for first in range(0, heads, per):
        cols = slice(first * PACKET, (first + per) * PACKET)
        scores = dot(keys, heads_side_by_side(q_ref, first, per))
        prob_grad = dot_nt(keys[:, :LAT], grad_ref[cols, :])
        for i in range(per):
            lanes = slice(i * PACKET, (i + 1) * PACKET)
            norm = norm_ref[first + i : first + i + 1, :].astype(F32)
            if live is not None:
                norm = jnp.where(live, norm, NEVER)
            delta = delta_ref[first + i : first + i + 1, :].astype(F32)
            prob = jnp.exp(scores[:, lanes] - norm)
            if visible is not None:
                prob = jnp.where(visible, prob, 0.0)
            here = slice((first + i) * PACKET, (first + i + 1) * PACKET)
            ds_ref[:, here] = (prob * (prob_grad[:, lanes] - delta)).astype(BF16)
            p_ref[:, here] = prob.astype(BF16)
    key_grad = dot_nt(ds_ref[...], heads_side_by_side(q_ref, 0, heads))
    value_grad = dot(p_ref[...], grad_ref[...])
    grad_out_ref[:, :LAT] = key_grad[:, :LAT] + value_grad
    grad_out_ref[:, LAT:] = key_grad[:, LAT:]


def pieces_out(total_ref, low, offset, out_refs):
    rows = total_ref.shape[0] // low
    r = lax.rem(lax.axis_index("head"), low)
    for d, out_ref in out_refs:
        start = pl.multiple_of(lax.rem(r + d, low) * rows, 16) + offset
        out_ref[...] = total_ref[pl.ds(start, out_ref.shape[0]), :].astype(out_ref.dtype)


def own_chunk(plan_ref, keys, offset, part, refs, low, q_ref, rows_ref, norm_ref, delta_ref):
    ds_ref, keep_ref, *out_refs, p_ref, total_ref = refs
    rows = BLOCK // low
    at = lax.broadcasted_iota(jnp.int32, (part, PACKET), 0)
    at = jnp.concatenate([at + (j * rows + offset) for j in range(low)], axis=0)
    k_pos = plan_ref[0:1, 0:1] * BLOCK + at
    q_pos = SHARD - PACKET + lax.broadcasted_iota(jnp.int32, at.shape, 1)
    visit(keys, q_ref, rows_ref, norm_ref, delta_ref, None, k_pos <= q_pos, ds_ref, p_ref, total_ref)
    pieces_out(total_ref, low, 0, list(enumerate([keep_ref, *out_refs])))


def own_first_kernel(low, held, plan_ref, lat_ref, q_ref, grad_ref, norm_ref, delta_ref, *rest):
    rest = rest[held:]
    rows_ref, sel_ref = rest[:2]
    keys_refs = rest[2 : 2 + CHUNKS]
    ds_ref, keep_ref = rest[2 + CHUNKS : 4 + CHUNKS]
    out_refs = rest[4 + CHUNKS : 3 + CHUNKS + low]
    heads = q_ref.shape[0]
    group = WIDE // heads
    at = lax.broadcasted_iota(jnp.int32, (WIDE, WIDE), 0)
    come = lax.broadcasted_iota(jnp.int32, (WIDE, WIDE), 1)
    order = (come == lax.rem(at, group) * heads + lax.div(at, group)).astype(F32).astype(BF16)
    for g in range(PACKET // group):
        moved = dot(order, grad_ref[g * WIDE : (g + 1) * WIDE, :]).astype(BF16)
        for h in range(heads):
            rows_ref[h * PACKET + g * group : h * PACKET + (g + 1) * group, :] = moved[h * group : (h + 1) * group, :]
    b0, b1 = plan_ref[0:1, 0:1], plan_ref[0:1, 1:2]
    t = lax.div(lax.axis_index("head"), low)
    for i, hit in enumerate((b0 == t, b0 != t, b1 == t, b1 != t)):
        sel_ref[i : i + 1, :] = jnp.broadcast_to(jnp.where(hit, 1.0, 0.0), (1, sel_ref.shape[1])).astype(F32)
    last = jnp.where(b0 > 0, 1.0, 0.0).astype(BF16)
    first = jnp.where(b0 > 0, 0.0, 1.0).astype(BF16)
    keys = (lat_ref[:, :BLOCK] * first + lat_ref[:, BLOCK:] * last).T
    chunk_rows(keys, low, keys_refs)
    (offset, part), *_ = chunks_of(BLOCK // low)
    refs = [ds_ref, keep_ref, *out_refs, *rest[-2:]]
    own_chunk(plan_ref, keys_refs[0][...], offset, part, refs, low, q_ref, rows_ref, norm_ref, delta_ref)


def own_next_kernel(low, offset, plan_ref, keys_ref, q_ref, rows_ref, norm_ref, delta_ref, *rest):
    part = keys_ref.shape[0] // low
    own_chunk(plan_ref, keys_ref[...], offset, part, rest, low, q_ref, rows_ref, norm_ref, delta_ref)


def far_kernel(low, keys_ref, q_ref, grad_ref, norm_ref, delta_ref, *rest):
    ds_ref = rest[-3 - low]
    out_refs = rest[-2 - low : -2]
    p_ref, total_ref = rest[-2:]
    live = lax.axis_index("seq") > 0
    visit(keys_ref[...], q_ref, grad_ref, norm_ref, delta_ref, live, None, ds_ref, p_ref, total_ref)
    pieces_out(total_ref, low, 0, list(enumerate(out_refs)))


def query_kernel(*refs):
    count = len(refs) // 2
    keys_refs, ds_refs, out_ref = refs[:count], refs[count:-1], refs[-1]
    heads = out_ref.shape[0]
    per = WIDE // PACKET
    keys = [ref[...].T for ref in keys_refs]
    for first in range(0, heads, per):
        cols = slice(first * PACKET, (first + per) * PACKET)
        total = sum(dot(k, ds_ref[:, cols]) for k, ds_ref in zip(keys, ds_refs))
        for i in range(per):
            out_ref[first + i] = total[:, i * PACKET : (i + 1) * PACKET].astype(BF16)


def combine_kernel(low, sel_ref, *rest):
    own_refs = rest[:low]
    far_refs = rest[low : 2 * low]
    send_ref, mine_ref = rest[-2:]
    own = own_refs[0][...]
    for ref in own_refs[1:]:
        own = own + ref[...].astype(F32)
    far = far_refs[0][...].astype(F32)
    for ref in far_refs[1:]:
        far = far + ref[...].astype(F32)
    send_ref[...] = (own * sel_ref[1:2, :] + far * sel_ref[3:4, :]).astype(BF16)
    mine_ref[...] = own * sel_ref[0:1, :] + far * sel_ref[2:3, :]


def first_sum_kernel(mine_ref, got_ref, out_ref):
    out_ref[...] = (mine_ref[...] + got_ref[...].astype(F32)).astype(BF16)


def last_kernel(*refs):
    *done_refs, mine_ref, got_ref, out_ref = refs
    *firsts, (offset, part) = chunks_of(out_ref.shape[0])
    for (at, size), done_ref in zip(firsts, done_refs):
        out_ref[at : at + size, :] = done_ref[...]
    out_ref[offset : offset + part, :] = (mine_ref[...] + got_ref[...].astype(F32)).astype(BF16)


def call(kernel, name, ins, outs, scratch=(), raw=(), passed=(), flops=0, size=0):
    spaces = [pltpu.VMEM] * len(ins) + [pl.ANY] * len(passed)
    ins = list(ins)
    for i in raw:
        spaces[i] = pl.ANY
        ins[i] = pltpu.with_memory_space_constraint(ins[i], pltpu.HBM)
    shapes = [jax.ShapeDtypeStruct(s, d) for s, d in outs]
    shapes += [jax.ShapeDtypeStruct(x.shape, x.dtype) for x in passed]
    return pl.pallas_call(
        kernel,
        name=name,
        out_shape=shapes,
        in_specs=[pl.BlockSpec(memory_space=space) for space in spaces],
        out_specs=[pl.BlockSpec(memory_space=space) for space in [pltpu.VMEM] * len(outs) + [pl.ANY] * len(passed)],
        scratch_shapes=scratch,
        input_output_aliases={len(ins) + i: len(outs) + i for i in range(len(passed))},
        compiler_params=pltpu.CompilerParams(vmem_limit_bytes=VMEM_LIMIT),
        cost_estimate=pl.CostEstimate(flops=flops, bytes_accessed=size, transcendentals=0),
    )(*ins, *passed)


def local(queries, out_grad, latents, log_norm, out_delta, plan):
    n_seq = lax.axis_size("seq")
    n_head = lax.axis_size("head")
    low = n_head // 2
    rows = BLOCK // low
    packet, heads, width = queries.shape
    columns = packet * heads

    lat_t = latents.T
    q_t = jnp.transpose(queries, (1, 2, 0))
    grad = out_grad.reshape(columns, LAT)
    norm_t = log_norm.T
    delta_t = out_delta.T
    visit_flops = 2 * columns * BLOCK * (2 * width + 2 * LAT)

    def route(d, back):
        pairs = []
        for i in range(n_seq):
            for j in range(n_head):
                to = j // low * low + (j + d) % low
                pairs.append((i * n_head + j, (i - back) % n_seq * n_head + to))
        return pairs

    chunks = chunks_of(rows)
    blocks = SHARD // BLOCK

    sent = call(
        functools.partial(send_block_kernel, low),
        "send_block",
        (plan, lat_t),
        [((low * part, width), BF16) for _, part in chunks],
        [pltpu.SMEM(plan.shape, plan.dtype), pltpu.VMEM((blocks, width, BLOCK), BF16), pltpu.SemaphoreType.DMA((blocks + 1,))],
        flops=visit_flops,
        raw=(0, 1),
    )

    def forward(x):
        return lax.ppermute(x, "seq", [(i, (i + 1) % n_seq) for i in range(n_seq)])

    def own_outs(part):
        return [((low * part, columns), BF16), ((part, width), F32)] + [((part, width), BF16)] * (low - 1)

    def scratch(part):
        return [pltpu.VMEM((low * part, columns), BF16), pltpu.VMEM((low * part, width), F32)]

    far_keys = [forward(sent[0])]
    (_, part), *_ = chunks
    grad_rows, sel, *first = call(
        functools.partial(own_first_kernel, low, CHUNKS - 1),
        "own_visit_0",
        (plan, lat_t, q_t, grad, norm_t, delta_t),
        [((columns, LAT), BF16), ((8, width), F32)] + [((low * p, width), BF16) for _, p in chunks] + own_outs(part),
        scratch(part),
        passed=sent[1:],
    )
    own_keys, first = first[:CHUNKS], first[CHUNKS:]
    own, later = [first[: 1 + low]], first[1 + low :]
    far_keys += [forward(x) for x in later]
    for c, (offset, part) in list(enumerate(chunks))[1:]:
        own.append(
            call(
                functools.partial(own_next_kernel, low, offset),
                f"own_visit_{c}",
                (plan, own_keys[c], q_t, grad_rows, norm_t, delta_t),
                own_outs(part),
                scratch(part),
                flops=COST_OWN,
            )
        )
    own_parts = []
    for _, keep, *pieces in own:
        sends = enumerate(pieces, 1)
        own_parts.append([keep] + [lax.ppermute(x, ("seq", "head"), route(d, 0)) for d, x in sends])

    far_ds, far_parts = [], []
    for c, (_, part) in enumerate(chunks):
        ds, *far = call(
            functools.partial(far_kernel, low),
            f"far_visit_{c}",
            (far_keys[c], q_t, grad_rows, norm_t, delta_t, *(far_ds[-1:] or [own[-1][0]])),
            [((low * part, columns), BF16)] + [((part, width), BF16)] * low,
            scratch(part),
        )
        far_ds.append(ds)
        far_parts.append([lax.ppermute(far[d], ("seq", "head"), route(d, 1)) for d in reversed(range(low))])

    mine, got = [None] * CHUNKS, [None] * CHUNKS
    for c, (_, part) in reversed(list(enumerate(chunks))):
        send, mine[c] = call(
            functools.partial(combine_kernel, low),
            f"combine_{c}",
            (sel, *own_parts[c], *far_parts[c]),
            [((part, width), BF16), ((part, width), F32)],
            flops=COST_COMBINE,
        )
        got[c] = lax.ppermute(send, "head", [(j, (j + low) % n_head) for j in range(n_head)])

    (query_t,) = call(
        query_kernel,
        "query_grad",
        (*own_keys, *far_keys, *(x[0] for x in own), *far_ds),
        [((heads, width, packet), BF16)],
        flops=4 * columns * BLOCK * width,
    )
    done = [
        call(first_sum_kernel, f"sum_{c}", (mine[c], got[c]), [((part, width), BF16)], flops=COST_SUM)[0]
        for c, (_, part) in list(enumerate(chunks))[:-1]
    ]
    (latent_out,) = call(last_kernel, "last_sum", (*done, mine[-1], got[-1]), [((rows, width), BF16)])
    return jnp.transpose(query_t, (2, 0, 1)), latent_out


def solution(mesh):
    return jax.shard_map(
        local,
        mesh=mesh,
        in_specs=(
            P("seq", "head", None),
            P("seq", "head", None),
            P("seq", None),
            P("seq", "head"),
            P("seq", "head"),
            P("seq", None),
        ),
        out_specs=(P("seq", "head", None), P(("seq", "head"), None)),
        check_vma=False,
    )
```

```python
import functools

import jax
import jax.numpy as jnp
from jax import lax
from jax.experimental import pallas as pl
from jax.experimental.pallas import tpu as pltpu
from jax.sharding import PartitionSpec as P

LAT = 512
PACKET = 128
BLOCK = 384
SHARD = 768
WIDE = 256
VMEM_LIMIT = 24 * 2**20
NEVER = 1e30
CHUNKS = 2
FIRST_SHARE = 1 / 2
COST_SUM = 10**9
COST_COMBINE = 10**9
COST_OWN = 0

F32 = jnp.float32
BF16 = jnp.bfloat16


def dot(a, b):
    return lax.dot_general(a, b, (((1,), (0,)), ((), ())), preferred_element_type=F32)


def dot_nt(a, b):
    return lax.dot_general(a, b, (((1,), (1,)), ((), ())), preferred_element_type=F32)


def chunks_of(rows):
    first = -(-int(rows * FIRST_SHARE) // 16) * 16
    return [(0, first), (first, rows - first)]


def piece_at(place, low):
    return lax.rem(lax.axis_index("head") + place, low)


def chunk_rows(keys, low, out_refs):
    rows = BLOCK // low
    for j in range(low):
        place = lax.rem(j + low - piece_at(0, low), low)
        for (offset, part), out_ref in zip(chunks_of(rows), out_refs):
            start = j * rows + offset
            out_ref[pl.ds(pl.multiple_of(place * part, 16), part), :] = keys[start : start + part, :]


def send_block_kernel(low, plan_hbm, lat_hbm, *rest):
    out_refs = rest[:CHUNKS]
    plan_ref, lat_ref, sems = rest[CHUNKS:]

    def block_copy(block):
        here = pl.ds(pl.multiple_of(block * BLOCK, 128), BLOCK)
        return pltpu.make_async_copy(lat_hbm.at[:, here], lat_ref.at[block], sems.at[block])

    blocks = lat_ref.shape[0]
    plan_copy = pltpu.make_async_copy(plan_hbm, plan_ref, sems.at[blocks])
    plan_copy.start()
    for block in range(blocks):
        block_copy(block).start()
    plan_copy.wait()
    sent = plan_ref[0, 1]
    block_copy(sent).wait()
    chunk_rows(lat_ref[sent].T, low, out_refs)
    for i in range(1, blocks):
        block_copy(lax.rem(sent + i, blocks)).wait()


def heads_side_by_side(q_ref, first, count):
    return jnp.concatenate([q_ref[first + i] for i in range(count)], axis=1)


def visit(keys, q_ref, grad_ref, norm_ref, delta_ref, live, visible, ds_ref, p_ref, out_refs):
    heads = q_ref.shape[0]
    per = WIDE // PACKET
    for first in range(0, heads, per):
        cols = slice(first * PACKET, (first + per) * PACKET)
        scores = dot(keys, heads_side_by_side(q_ref, first, per))
        prob_grad = dot_nt(keys[:, :LAT], grad_ref[cols, :])
        for i in range(per):
            lanes = slice(i * PACKET, (i + 1) * PACKET)
            norm = norm_ref[first + i : first + i + 1, :].astype(F32)
            if live is not None:
                norm = jnp.where(live, norm, NEVER)
            delta = delta_ref[first + i : first + i + 1, :].astype(F32)
            prob = jnp.exp(scores[:, lanes] - norm)
            if visible is not None:
                prob = jnp.where(visible, prob, 0.0)
            here = slice((first + i) * PACKET, (first + i + 1) * PACKET)
            ds_ref[:, here] = (prob * (prob_grad[:, lanes] - delta)).astype(BF16)
            p_ref[:, here] = prob.astype(BF16)
    value_grad = dot(p_ref[...], grad_ref[...])
    key_grad = dot_nt(ds_ref[...], heads_side_by_side(q_ref, 0, heads))
    part = keys.shape[0] // len(out_refs)
    for d, out_ref in enumerate(out_refs):
        here = slice(d * part, (d + 1) * part)
        out_ref[:, :LAT] = (key_grad[here, :LAT] + value_grad[here, :]).astype(out_ref.dtype)
        out_ref[:, LAT:] = key_grad[here, LAT:].astype(out_ref.dtype)


def own_chunk(plan_ref, keys, offset, refs, low, q_ref, rows_ref, norm_ref, delta_ref):
    ds_ref, *out_refs, p_ref = refs
    rows, part = BLOCK // low, keys.shape[0] // low
    at = lax.broadcasted_iota(jnp.int32, (part, PACKET), 0)
    at = jnp.concatenate([at + (piece_at(d, low) * rows + offset) for d in range(low)], axis=0)
    k_pos = plan_ref[0:1, 0:1] * BLOCK + at
    q_pos = SHARD - PACKET + lax.broadcasted_iota(jnp.int32, at.shape, 1)
    visit(keys, q_ref, rows_ref, norm_ref, delta_ref, None, k_pos <= q_pos, ds_ref, p_ref, out_refs)


def own_first_kernel(low, held, plan_ref, lat_ref, q_ref, grad_ref, norm_ref, delta_ref, *rest):
    rest = rest[held:]
    rows_ref, sel_ref = rest[:2]
    keys_refs = rest[2 : 2 + CHUNKS]
    refs = [*rest[2 + CHUNKS : 3 + CHUNKS + low], rest[-1]]
    heads = q_ref.shape[0]
    group = WIDE // heads
    at = lax.broadcasted_iota(jnp.int32, (WIDE, WIDE), 0)
    come = lax.broadcasted_iota(jnp.int32, (WIDE, WIDE), 1)
    order = (come == lax.rem(at, group) * heads + lax.div(at, group)).astype(F32).astype(BF16)
    for g in range(PACKET // group):
        moved = dot(order, grad_ref[g * WIDE : (g + 1) * WIDE, :]).astype(BF16)
        for h in range(heads):
            rows_ref[h * PACKET + g * group : h * PACKET + (g + 1) * group, :] = moved[h * group : (h + 1) * group, :]
    b0, b1 = plan_ref[0:1, 0:1], plan_ref[0:1, 1:2]
    t = lax.div(lax.axis_index("head"), low)
    for i, hit in enumerate((b0 == t, b0 != t, b1 == t, b1 != t)):
        sel_ref[i : i + 1, :] = jnp.broadcast_to(jnp.where(hit, 1.0, 0.0), (1, sel_ref.shape[1])).astype(F32)
    last = jnp.where(b0 > 0, 1.0, 0.0).astype(BF16)
    first = jnp.where(b0 > 0, 0.0, 1.0).astype(BF16)
    keys = (lat_ref[:, :BLOCK] * first + lat_ref[:, BLOCK:] * last).T
    chunk_rows(keys, low, keys_refs)
    (offset, _), *_ = chunks_of(BLOCK // low)
    own_chunk(plan_ref, keys_refs[0][...], offset, refs, low, q_ref, rows_ref, norm_ref, delta_ref)


def own_next_kernel(low, offset, plan_ref, keys_ref, q_ref, rows_ref, norm_ref, delta_ref, *rest):
    own_chunk(plan_ref, keys_ref[...], offset, rest, low, q_ref, rows_ref, norm_ref, delta_ref)


def far_kernel(low, keys_ref, q_ref, grad_ref, norm_ref, delta_ref, *rest):
    ds_ref, *out_refs, p_ref = rest[-2 - low :]
    live = lax.axis_index("seq") > 0
    visit(keys_ref[...], q_ref, grad_ref, norm_ref, delta_ref, live, None, ds_ref, p_ref, out_refs)


def query_kernel(*refs):
    count = len(refs) // 2
    keys_refs, ds_refs, out_ref = refs[:count], refs[count:-1], refs[-1]
    heads = out_ref.shape[0]
    per = WIDE // PACKET
    keys = [ref[...].T for ref in keys_refs]
    for first in range(0, heads, per):
        cols = slice(first * PACKET, (first + per) * PACKET)
        total = sum(dot(k, ds_ref[:, cols]) for k, ds_ref in zip(keys, ds_refs))
        for i in range(per):
            out_ref[first + i] = total[:, i * PACKET : (i + 1) * PACKET].astype(BF16)


def combine_kernel(low, sel_ref, *rest):
    own_refs = rest[:low]
    far_refs = rest[low : 2 * low]
    send_ref, mine_ref = rest[-2:]
    own = own_refs[0][...]
    for ref in own_refs[1:]:
        own = own + ref[...].astype(F32)
    far = far_refs[0][...].astype(F32)
    for ref in far_refs[1:]:
        far = far + ref[...].astype(F32)
    send_ref[...] = (own * sel_ref[1:2, :] + far * sel_ref[3:4, :]).astype(BF16)
    mine_ref[...] = own * sel_ref[0:1, :] + far * sel_ref[2:3, :]


def first_sum_kernel(mine_ref, got_ref, out_ref):
    out_ref[...] = (mine_ref[...] + got_ref[...].astype(F32)).astype(BF16)


def last_kernel(*refs):
    *done_refs, mine_ref, got_ref, out_ref = refs
    *firsts, (offset, part) = chunks_of(out_ref.shape[0])
    for (at, size), done_ref in zip(firsts, done_refs):
        out_ref[at : at + size, :] = done_ref[...]
    out_ref[offset : offset + part, :] = (mine_ref[...] + got_ref[...].astype(F32)).astype(BF16)


def call(kernel, name, ins, outs, scratch=(), raw=(), passed=(), flops=0, size=0):
    spaces = [pltpu.VMEM] * len(ins) + [pl.ANY] * len(passed)
    ins = list(ins)
    for i in raw:
        spaces[i] = pl.ANY
        ins[i] = pltpu.with_memory_space_constraint(ins[i], pltpu.HBM)
    shapes = [jax.ShapeDtypeStruct(s, d) for s, d in outs]
    shapes += [jax.ShapeDtypeStruct(x.shape, x.dtype) for x in passed]
    return pl.pallas_call(
        kernel,
        name=name,
        out_shape=shapes,
        in_specs=[pl.BlockSpec(memory_space=space) for space in spaces],
        out_specs=[pl.BlockSpec(memory_space=space) for space in [pltpu.VMEM] * len(outs) + [pl.ANY] * len(passed)],
        scratch_shapes=scratch,
        input_output_aliases={len(ins) + i: len(outs) + i for i in range(len(passed))},
        compiler_params=pltpu.CompilerParams(vmem_limit_bytes=VMEM_LIMIT),
        cost_estimate=pl.CostEstimate(flops=flops, bytes_accessed=size, transcendentals=0),
    )(*ins, *passed)


def local(queries, out_grad, latents, log_norm, out_delta, plan):
    n_seq = lax.axis_size("seq")
    n_head = lax.axis_size("head")
    low = n_head // 2
    rows = BLOCK // low
    packet, heads, width = queries.shape
    columns = packet * heads

    lat_t = latents.T
    q_t = jnp.transpose(queries, (1, 2, 0))
    grad = out_grad.reshape(columns, LAT)
    norm_t = log_norm.T
    delta_t = out_delta.T
    visit_flops = 2 * columns * BLOCK * (2 * width + 2 * LAT)

    def route(d, back):
        pairs = []
        for i in range(n_seq):
            for j in range(n_head):
                to = j // low * low + (j + d) % low
                pairs.append((i * n_head + j, (i - back) % n_seq * n_head + to))
        return pairs

    chunks = chunks_of(rows)
    blocks = SHARD // BLOCK

    sent = call(
        functools.partial(send_block_kernel, low),
        "send_block",
        (plan, lat_t),
        [((low * part, width), BF16) for _, part in chunks],
        [pltpu.SMEM(plan.shape, plan.dtype), pltpu.VMEM((blocks, width, BLOCK), BF16), pltpu.SemaphoreType.DMA((blocks + 1,))],
        flops=visit_flops,
        raw=(0, 1),
    )

    def forward(x):
        return lax.ppermute(x, "seq", [(i, (i + 1) % n_seq) for i in range(n_seq)])

    def own_outs(part):
        return [((low * part, columns), BF16), ((part, width), F32)] + [((part, width), BF16)] * (low - 1)

    def scratch(part):
        return [pltpu.VMEM((low * part, columns), BF16)]

    far_keys = [forward(sent[0])]
    (_, part), *_ = chunks
    grad_rows, sel, *first = call(
        functools.partial(own_first_kernel, low, CHUNKS - 1),
        "own_visit_0",
        (plan, lat_t, q_t, grad, norm_t, delta_t),
        [((columns, LAT), BF16), ((8, width), F32)] + [((low * p, width), BF16) for _, p in chunks] + own_outs(part),
        scratch(part),
        passed=sent[1:],
    )
    own_keys, first = first[:CHUNKS], first[CHUNKS:]
    own, later = [first[: 1 + low]], first[1 + low :]
    far_keys += [forward(x) for x in later]
    for c, (offset, part) in list(enumerate(chunks))[1:]:
        own.append(
            call(
                functools.partial(own_next_kernel, low, offset),
                f"own_visit_{c}",
                (plan, own_keys[c], q_t, grad_rows, norm_t, delta_t),
                own_outs(part),
                scratch(part),
                flops=COST_OWN,
            )
        )
    own_parts = []
    for _, keep, *pieces in own:
        sends = enumerate(pieces, 1)
        own_parts.append([keep] + [lax.ppermute(x, ("seq", "head"), route(d, 0)) for d, x in sends])

    far_ds, far_parts = [], []
    for c, (_, part) in enumerate(chunks):
        ds, *far = call(
            functools.partial(far_kernel, low),
            f"far_visit_{c}",
            (far_keys[c], q_t, grad_rows, norm_t, delta_t, *(far_ds[-1:] or [own[-1][0]])),
            [((low * part, columns), BF16)] + [((part, width), BF16)] * low,
            scratch(part),
        )
        far_ds.append(ds)
        far_parts.append([lax.ppermute(far[d], ("seq", "head"), route(d, 1)) for d in reversed(range(low))])

    mine, got = [None] * CHUNKS, [None] * CHUNKS
    for c, (_, part) in reversed(list(enumerate(chunks))):
        send, mine[c] = call(
            functools.partial(combine_kernel, low),
            f"combine_{c}",
            (sel, *own_parts[c], *far_parts[c]),
            [((part, width), BF16), ((part, width), F32)],
            flops=COST_COMBINE,
        )
        got[c] = lax.ppermute(send, "head", [(j, (j + low) % n_head) for j in range(n_head)])

    (query_t,) = call(
        query_kernel,
        "query_grad",
        (*own_keys, *far_keys, *(x[0] for x in own), *far_ds),
        [((heads, width, packet), BF16)],
        flops=4 * columns * BLOCK * width,
    )
    done = [
        call(first_sum_kernel, f"sum_{c}", (mine[c], got[c]), [((part, width), BF16)], flops=COST_SUM)[0]
        for c, (_, part) in list(enumerate(chunks))[:-1]
    ]
    (latent_out,) = call(last_kernel, "last_sum", (*done, mine[-1], got[-1]), [((rows, width), BF16)])
    return jnp.transpose(query_t, (2, 0, 1)), latent_out


def solution(mesh):
    return jax.shard_map(
        local,
        mesh=mesh,
        in_specs=(
            P("seq", "head", None),
            P("seq", "head", None),
            P("seq", None),
            P("seq", "head"),
            P("seq", "head"),
            P("seq", None),
        ),
        out_specs=(P("seq", "head", None), P(("seq", "head"), None)),
        check_vma=False,
    )
```

```python
import functools

import jax
import jax.numpy as jnp
from jax import lax
from jax.experimental import pallas as pl
from jax.experimental.pallas import tpu as pltpu
from jax.sharding import PartitionSpec as P

LAT = 512
PACKET = 128
BLOCK = 384
SHARD = 768
WIDE = 256
VMEM_LIMIT = 24 * 2**20
NEVER = 1e30
CHUNKS = 2
FIRST_SHARE = 1 / 2
COST_SUM = 10**9
COST_COMBINE = 10**9
COST_OWN = 0

F32 = jnp.float32
BF16 = jnp.bfloat16


def dot(a, b):
    return lax.dot_general(a, b, (((1,), (0,)), ((), ())), preferred_element_type=F32)


def dot_nt(a, b):
    return lax.dot_general(a, b, (((1,), (1,)), ((), ())), preferred_element_type=F32)


def chunks_of(rows):
    first = -(-int(rows * FIRST_SHARE) // 16) * 16
    return [(0, first), (first, rows - first)]


def chunk_rows(keys, low, out_refs):
    rows = BLOCK // low
    for (offset, part), out_ref in zip(chunks_of(rows), out_refs):
        for j in range(low):
            start = j * rows + offset
            out_ref[j * part : (j + 1) * part, :] = keys[start : start + part, :]


def send_block_kernel(low, plan_hbm, lat_hbm, *rest):
    out_refs = rest[:CHUNKS]
    lat_ref, plan_ref, sems = rest[CHUNKS:]

    def block_copy(block):
        here = pl.ds(pl.multiple_of(block * BLOCK, 128), BLOCK)
        return pltpu.make_async_copy(lat_hbm.at[:, here], lat_ref.at[block], sems.at[block])

    blocks = lat_ref.shape[0]
    plan_copy = pltpu.make_async_copy(plan_hbm, plan_ref, sems.at[blocks])
    plan_copy.start()
    for block in range(blocks):
        block_copy(block).start()
    plan_copy.wait()
    sent = plan_ref[0, 1]
    block_copy(sent).wait()
    chunk_rows(lat_ref[sent].T, low, out_refs)
    for i in range(1, blocks):
        block_copy(lax.rem(sent + i, blocks)).wait()


def heads_side_by_side(q_ref, first, count):
    return jnp.concatenate([q_ref[first + i] for i in range(count)], axis=1)


def visit(keys, q_ref, grad_ref, norm_ref, delta_ref, live, visible, ds_ref, p_ref, grad_out_ref):
    heads = q_ref.shape[0]
    per = WIDE // PACKET
    for first in range(0, heads, per):
        cols = slice(first * PACKET, (first + per) * PACKET)
        scores = dot(keys, heads_side_by_side(q_ref, first, per))
        prob_grad = dot_nt(keys[:, :LAT], grad_ref[cols, :])
        for i in range(per):
            lanes = slice(i * PACKET, (i + 1) * PACKET)
            norm = norm_ref[first + i : first + i + 1, :].astype(F32)
            if live is not None:
                norm = jnp.where(live, norm, NEVER)
            delta = delta_ref[first + i : first + i + 1, :].astype(F32)
            prob = jnp.exp(scores[:, lanes] - norm)
            if visible is not None:
                prob = jnp.where(visible, prob, 0.0)
            here = slice((first + i) * PACKET, (first + i + 1) * PACKET)
            ds_ref[:, here] = (prob * (prob_grad[:, lanes] - delta)).astype(BF16)
            p_ref[:, here] = prob.astype(BF16)
    key_grad = dot_nt(ds_ref[...], heads_side_by_side(q_ref, 0, heads))
    value_grad = dot(p_ref[...], grad_ref[...])
    grad_out_ref[:, :LAT] = key_grad[:, :LAT] + value_grad
    grad_out_ref[:, LAT:] = key_grad[:, LAT:]


def pieces_out(total_ref, low, offset, out_refs):
    rows = total_ref.shape[0] // low
    r = lax.rem(lax.axis_index("head"), low)
    for d, out_ref in out_refs:
        start = pl.multiple_of(lax.rem(r + d, low) * rows, 16) + offset
        out_ref[...] = total_ref[pl.ds(start, out_ref.shape[0]), :].astype(out_ref.dtype)


def own_chunk(plan_ref, keys, offset, part, refs, low, q_ref, rows_ref, norm_ref, delta_ref):
    ds_ref, keep_ref, *out_refs, p_ref, total_ref = refs
    rows = BLOCK // low
    at = lax.broadcasted_iota(jnp.int32, (part, PACKET), 0)
    at = jnp.concatenate([at + (j * rows + offset) for j in range(low)], axis=0)
    k_pos = plan_ref[0:1, 0:1] * BLOCK + at
    q_pos = SHARD - PACKET + lax.broadcasted_iota(jnp.int32, at.shape, 1)
    visit(keys, q_ref, rows_ref, norm_ref, delta_ref, None, k_pos <= q_pos, ds_ref, p_ref, total_ref)
    pieces_out(total_ref, low, 0, list(enumerate([keep_ref, *out_refs])))


def own_first_kernel(low, held, plan_ref, lat_ref, q_ref, grad_ref, norm_ref, delta_ref, *rest):
    rest = rest[held:]
    rows_ref, sel_ref = rest[:2]
    keys_refs = rest[2 : 2 + CHUNKS]
    ds_ref, keep_ref = rest[2 + CHUNKS : 4 + CHUNKS]
    out_refs = rest[4 + CHUNKS : 3 + CHUNKS + low]
    heads = q_ref.shape[0]
    group = WIDE // heads
    at = lax.broadcasted_iota(jnp.int32, (WIDE, WIDE), 0)
    come = lax.broadcasted_iota(jnp.int32, (WIDE, WIDE), 1)
    order = (come == lax.rem(at, group) * heads + lax.div(at, group)).astype(F32).astype(BF16)
    for g in range(PACKET // group):
        moved = dot(order, grad_ref[g * WIDE : (g + 1) * WIDE, :]).astype(BF16)
        for h in range(heads):
            rows_ref[h * PACKET + g * group : h * PACKET + (g + 1) * group, :] = moved[h * group : (h + 1) * group, :]
    b0, b1 = plan_ref[0:1, 0:1], plan_ref[0:1, 1:2]
    t = lax.div(lax.axis_index("head"), low)
    for i, hit in enumerate((b0 == t, b0 != t, b1 == t, b1 != t)):
        sel_ref[i : i + 1, :] = jnp.broadcast_to(jnp.where(hit, 1.0, 0.0), (1, sel_ref.shape[1])).astype(F32)
    last = jnp.where(b0 > 0, 1.0, 0.0).astype(BF16)
    first = jnp.where(b0 > 0, 0.0, 1.0).astype(BF16)
    keys = (lat_ref[0] * first + lat_ref[1] * last).T
    chunk_rows(keys, low, keys_refs)
    (offset, part), *_ = chunks_of(BLOCK // low)
    refs = [ds_ref, keep_ref, *out_refs, *rest[-2:]]
    own_chunk(plan_ref, keys_refs[0][...], offset, part, refs, low, q_ref, rows_ref, norm_ref, delta_ref)


def own_next_kernel(low, offset, plan_ref, keys_ref, q_ref, rows_ref, norm_ref, delta_ref, *rest):
    part = keys_ref.shape[0] // low
    own_chunk(plan_ref, keys_ref[...], offset, part, rest, low, q_ref, rows_ref, norm_ref, delta_ref)


def far_kernel(low, keys_ref, q_ref, grad_ref, norm_ref, delta_ref, *rest):
    ds_ref = rest[-3 - low]
    out_refs = rest[-2 - low : -2]
    p_ref, total_ref = rest[-2:]
    live = lax.axis_index("seq") > 0
    visit(keys_ref[...], q_ref, grad_ref, norm_ref, delta_ref, live, None, ds_ref, p_ref, total_ref)
    pieces_out(total_ref, low, 0, list(enumerate(out_refs)))


def query_kernel(*refs):
    count = len(refs) // 2
    keys_refs, ds_refs, out_ref = refs[:count], refs[count:-1], refs[-1]
    heads = out_ref.shape[0]
    per = WIDE // PACKET
    keys = [ref[...].T for ref in keys_refs]
    for first in range(0, heads, per):
        cols = slice(first * PACKET, (first + per) * PACKET)
        total = sum(dot(k, ds_ref[:, cols]) for k, ds_ref in zip(keys, ds_refs))
        for i in range(per):
            out_ref[first + i] = total[:, i * PACKET : (i + 1) * PACKET].astype(BF16)


def combine_kernel(low, sel_ref, *rest):
    own_refs = rest[:low]
    far_refs = rest[low : 2 * low]
    send_ref, mine_ref = rest[-2:]
    own = own_refs[0][...]
    for ref in own_refs[1:]:
        own = own + ref[...].astype(F32)
    far = far_refs[0][...].astype(F32)
    for ref in far_refs[1:]:
        far = far + ref[...].astype(F32)
    send_ref[...] = (own * sel_ref[1:2, :] + far * sel_ref[3:4, :]).astype(BF16)
    mine_ref[...] = own * sel_ref[0:1, :] + far * sel_ref[2:3, :]


def first_sum_kernel(mine_ref, got_ref, out_ref):
    out_ref[...] = (mine_ref[...] + got_ref[...].astype(F32)).astype(BF16)


def last_kernel(*refs):
    *done_refs, mine_ref, got_ref, out_ref = refs
    *firsts, (offset, part) = chunks_of(out_ref.shape[0])
    for (at, size), done_ref in zip(firsts, done_refs):
        out_ref[at : at + size, :] = done_ref[...]
    out_ref[offset : offset + part, :] = (mine_ref[...] + got_ref[...].astype(F32)).astype(BF16)


def call(kernel, name, ins, outs, scratch=(), raw=(), passed=(), flops=0, size=0):
    spaces = [pltpu.VMEM] * len(ins) + [pl.ANY] * len(passed)
    ins = list(ins)
    for i in raw:
        spaces[i] = pl.ANY
        ins[i] = pltpu.with_memory_space_constraint(ins[i], pltpu.HBM)
    shapes = [jax.ShapeDtypeStruct(s, d) for s, d in outs]
    shapes += [jax.ShapeDtypeStruct(x.shape, x.dtype) for x in passed]
    return pl.pallas_call(
        kernel,
        name=name,
        out_shape=shapes,
        in_specs=[pl.BlockSpec(memory_space=space) for space in spaces],
        out_specs=[pl.BlockSpec(memory_space=space) for space in [pltpu.VMEM] * len(outs) + [pl.ANY] * len(passed)],
        scratch_shapes=scratch,
        input_output_aliases={len(ins) + i: len(outs) + i for i in range(len(passed))},
        compiler_params=pltpu.CompilerParams(vmem_limit_bytes=VMEM_LIMIT),
        cost_estimate=pl.CostEstimate(flops=flops, bytes_accessed=size, transcendentals=0),
    )(*ins, *passed)


def local(queries, out_grad, latents, log_norm, out_delta, plan):
    n_seq = lax.axis_size("seq")
    n_head = lax.axis_size("head")
    low = n_head // 2
    rows = BLOCK // low
    packet, heads, width = queries.shape
    columns = packet * heads

    lat_t = latents.T
    q_t = jnp.transpose(queries, (1, 2, 0))
    grad = out_grad.reshape(columns, LAT)
    norm_t = log_norm.T
    delta_t = out_delta.T
    visit_flops = 2 * columns * BLOCK * (2 * width + 2 * LAT)

    def route(d, back):
        pairs = []
        for i in range(n_seq):
            for j in range(n_head):
                to = j // low * low + (j + d) % low
                pairs.append((i * n_head + j, (i - back) % n_seq * n_head + to))
        return pairs

    chunks = chunks_of(rows)
    blocks = SHARD // BLOCK

    *sent, lat_blocks = call(
        functools.partial(send_block_kernel, low),
        "send_block",
        (plan, lat_t),
        [((low * part, width), BF16) for _, part in chunks] + [((blocks, width, BLOCK), BF16)],
        [pltpu.SMEM(plan.shape, plan.dtype), pltpu.SemaphoreType.DMA((blocks + 1,))],
        flops=visit_flops,
        raw=(0, 1),
    )

    def forward(x):
        return lax.ppermute(x, "seq", [(i, (i + 1) % n_seq) for i in range(n_seq)])

    def own_outs(part):
        return [((low * part, columns), BF16), ((part, width), F32)] + [((part, width), BF16)] * (low - 1)

    def scratch(part):
        return [pltpu.VMEM((low * part, columns), BF16), pltpu.VMEM((low * part, width), F32)]

    far_keys = [forward(sent[0])]
    (_, part), *_ = chunks
    grad_rows, sel, *first = call(
        functools.partial(own_first_kernel, low, CHUNKS - 1),
        "own_visit_0",
        (plan, lat_blocks, q_t, grad, norm_t, delta_t),
        [((columns, LAT), BF16), ((8, width), F32)] + [((low * p, width), BF16) for _, p in chunks] + own_outs(part),
        scratch(part),
        passed=sent[1:],
    )
    own_keys, first = first[:CHUNKS], first[CHUNKS:]
    own, later = [first[: 1 + low]], first[1 + low :]
    far_keys += [forward(x) for x in later]
    for c, (offset, part) in list(enumerate(chunks))[1:]:
        own.append(
            call(
                functools.partial(own_next_kernel, low, offset),
                f"own_visit_{c}",
                (plan, own_keys[c], q_t, grad_rows, norm_t, delta_t),
                own_outs(part),
                scratch(part),
                flops=COST_OWN,
            )
        )
    own_parts = []
    for _, keep, *pieces in own:
        sends = enumerate(pieces, 1)
        own_parts.append([keep] + [lax.ppermute(x, ("seq", "head"), route(d, 0)) for d, x in sends])

    far_ds, far_parts = [], []
    for c, (_, part) in enumerate(chunks):
        ds, *far = call(
            functools.partial(far_kernel, low),
            f"far_visit_{c}",
            (far_keys[c], q_t, grad_rows, norm_t, delta_t, *(far_ds[-1:] or [own[-1][0]])),
            [((low * part, columns), BF16)] + [((part, width), BF16)] * low,
            scratch(part),
        )
        far_ds.append(ds)
        far_parts.append([lax.ppermute(far[d], ("seq", "head"), route(d, 1)) for d in reversed(range(low))])

    mine, got = [None] * CHUNKS, [None] * CHUNKS
    for c, (_, part) in reversed(list(enumerate(chunks))):
        send, mine[c] = call(
            functools.partial(combine_kernel, low),
            f"combine_{c}",
            (sel, *own_parts[c], *far_parts[c]),
            [((part, width), BF16), ((part, width), F32)],
            flops=COST_COMBINE,
        )
        got[c] = lax.ppermute(send, "head", [(j, (j + low) % n_head) for j in range(n_head)])

    (query_t,) = call(
        query_kernel,
        "query_grad",
        (*own_keys, *far_keys, *(x[0] for x in own), *far_ds),
        [((heads, width, packet), BF16)],
        flops=4 * columns * BLOCK * width,
    )
    done = [
        call(first_sum_kernel, f"sum_{c}", (mine[c], got[c]), [((part, width), BF16)], flops=COST_SUM)[0]
        for c, (_, part) in list(enumerate(chunks))[:-1]
    ]
    (latent_out,) = call(last_kernel, "last_sum", (*done, mine[-1], got[-1]), [((rows, width), BF16)])
    return jnp.transpose(query_t, (2, 0, 1)), latent_out


def solution(mesh):
    return jax.shard_map(
        local,
        mesh=mesh,
        in_specs=(
            P("seq", "head", None),
            P("seq", "head", None),
            P("seq", None),
            P("seq", "head"),
            P("seq", "head"),
            P("seq", None),
        ),
        out_specs=(P("seq", "head", None), P(("seq", "head"), None)),
        check_vma=False,
    )
```

```python
import functools

import jax
import jax.numpy as jnp
from jax import lax
from jax.experimental import pallas as pl
from jax.experimental.pallas import tpu as pltpu
from jax.sharding import PartitionSpec as P

LAT = 512
PACKET = 128
BLOCK = 384
SHARD = 768
WIDE = 256
VMEM_LIMIT = 24 * 2**20
NEVER = 1e30
CHUNKS = 2

F32 = jnp.float32
BF16 = jnp.bfloat16


def dot(a, b):
    return lax.dot_general(a, b, (((1,), (0,)), ((), ())), preferred_element_type=F32)


def dot_nt(a, b):
    return lax.dot_general(a, b, (((1,), (1,)), ((), ())), preferred_element_type=F32)


def send_block_kernel(low, plan_hbm, lat_hbm, *rest):
    out_refs = rest[:CHUNKS]
    lat_ref, plan_ref, sems = rest[CHUNKS:]

    def block_copy(block):
        here = pl.ds(pl.multiple_of(block * BLOCK, 128), BLOCK)
        return pltpu.make_async_copy(lat_hbm.at[:, here], lat_ref.at[block], sems.at[block])

    blocks = lat_ref.shape[0]
    plan_copy = pltpu.make_async_copy(plan_hbm, plan_ref, sems.at[blocks])
    plan_copy.start()
    for block in range(blocks):
        block_copy(block).start()
    plan_copy.wait()
    sent = plan_ref[0, 1]
    block_copy(sent).wait()
    keys = lat_ref[sent].T
    rows = BLOCK // low
    part = rows // CHUNKS
    for c, out_ref in enumerate(out_refs):
        for j in range(low):
            start = j * rows + c * part
            out_ref[j * part : (j + 1) * part, :] = keys[start : start + part, :]
    for i in range(1, blocks):
        block_copy(lax.rem(sent + i, blocks)).wait()


def heads_side_by_side(q_ref, first, count):
    return jnp.concatenate([q_ref[first + i] for i in range(count)], axis=1)


def visit(keys, q_ref, grad_ref, norm_ref, delta_ref, live, visible, ds_ref, p_ref, grad_out_ref):
    heads = q_ref.shape[0]
    per = WIDE // PACKET
    for first in range(0, heads, per):
        cols = slice(first * PACKET, (first + per) * PACKET)
        scores = dot(keys, heads_side_by_side(q_ref, first, per))
        prob_grad = dot_nt(keys[:, :LAT], grad_ref[cols, :])
        for i in range(per):
            lanes = slice(i * PACKET, (i + 1) * PACKET)
            norm = norm_ref[first + i : first + i + 1, :].astype(F32)
            if live is not None:
                norm = jnp.where(live, norm, NEVER)
            delta = delta_ref[first + i : first + i + 1, :].astype(F32)
            prob = jnp.exp(scores[:, lanes] - norm)
            if visible is not None:
                tail = jnp.where(visible[-PACKET:], prob[-PACKET:], 0.0)
                prob = jnp.concatenate([prob[:-PACKET], tail], axis=0)
            here = slice((first + i) * PACKET, (first + i + 1) * PACKET)
            ds_ref[:, here] = (prob * (prob_grad[:, lanes] - delta)).astype(BF16)
            p_ref[:, here] = prob.astype(BF16)
    key_grad = dot_nt(ds_ref[...], heads_side_by_side(q_ref, 0, heads))
    value_grad = dot(p_ref[...], grad_ref[...])
    grad_out_ref[:, :LAT] = key_grad[:, :LAT] + value_grad
    grad_out_ref[:, LAT:] = key_grad[:, LAT:]


def pieces_out(total_ref, low, offset, out_refs):
    rows = total_ref.shape[0] // low
    r = lax.rem(lax.axis_index("head"), low)
    for d, out_ref in out_refs:
        start = pl.multiple_of(lax.rem(r + d, low) * rows, 16) + offset
        out_ref[...] = total_ref[pl.ds(start, out_ref.shape[0]), :].astype(out_ref.dtype)


def own_kernel(low, plan_ref, lat_ref, q_ref, grad_ref, norm_ref, delta_ref, *rest):
    rows_ref, ds_ref, sel_ref, keep_ref = rest[:4]
    out_refs = rest[4:-2]
    p_ref, total_ref = rest[-2:]
    heads = q_ref.shape[0]
    group = WIDE // heads
    at = lax.broadcasted_iota(jnp.int32, (WIDE, WIDE), 0)
    come = lax.broadcasted_iota(jnp.int32, (WIDE, WIDE), 1)
    order = (come == lax.rem(at, group) * heads + lax.div(at, group)).astype(F32).astype(BF16)
    for g in range(PACKET // group):
        moved = dot(order, grad_ref[g * WIDE : (g + 1) * WIDE, :]).astype(BF16)
        for h in range(heads):
            rows_ref[h * PACKET + g * group : h * PACKET + (g + 1) * group, :] = moved[h * group : (h + 1) * group, :]
    b0, b1 = plan_ref[0:1, 0:1], plan_ref[0:1, 1:2]
    t = lax.div(lax.axis_index("head"), low)
    for i, hit in enumerate((b0 == t, b0 != t, b1 == t, b1 != t)):
        sel_ref[i : i + 1, :] = jnp.broadcast_to(jnp.where(hit, 1.0, 0.0), (1, sel_ref.shape[1])).astype(F32)
    last = jnp.where(b0 > 0, 1.0, 0.0).astype(BF16)
    first = jnp.where(b0 > 0, 0.0, 1.0).astype(BF16)
    keys = (lat_ref[0] * first + lat_ref[1] * last).T
    k_pos = b0 * BLOCK + lax.broadcasted_iota(jnp.int32, (BLOCK, PACKET), 0)
    q_pos = SHARD - PACKET + lax.broadcasted_iota(jnp.int32, (BLOCK, PACKET), 1)
    visit(keys, q_ref, rows_ref, norm_ref, delta_ref, None, k_pos <= q_pos, ds_ref, p_ref, total_ref)
    pieces_out(total_ref, low, 0, [(0, keep_ref)])
    for i, out_ref in enumerate(out_refs):
        part = out_ref.shape[0]
        pieces_out(total_ref, low, i % CHUNKS * part, [(1 + i // CHUNKS, out_ref)])


def far_kernel(low, held, keys_ref, q_ref, grad_ref, norm_ref, delta_ref, *rest):
    ds_ref = rest[held]
    out_refs = rest[held + 1 : held + 1 + low]
    p_ref, total_ref = rest[-2:]
    live = lax.axis_index("seq") > 0
    visit(keys_ref[...], q_ref, grad_ref, norm_ref, delta_ref, live, None, ds_ref, p_ref, total_ref)
    pieces_out(total_ref, low, 0, list(enumerate(out_refs)))


def query_kernel(plan_ref, lat_ref, own_ds_ref, *rest):
    far_refs = rest[:CHUNKS]
    far_ds_refs = rest[CHUNKS : 2 * CHUNKS]
    out_ref = rest[-1]
    heads = out_ref.shape[0]
    per = WIDE // PACKET
    b0 = plan_ref[0:1, 0:1]
    last = jnp.where(b0 > 0, 1.0, 0.0).astype(BF16)
    first_block = jnp.where(b0 > 0, 0.0, 1.0).astype(BF16)
    own = lat_ref[0] * first_block + lat_ref[1] * last
    fars = [ref[...].T for ref in far_refs]
    for first in range(0, heads, per):
        cols = slice(first * PACKET, (first + per) * PACKET)
        total = dot(own, own_ds_ref[:, cols])
        for far, ds_ref in zip(fars, far_ds_refs):
            total = total + dot(far, ds_ref[:, cols])
        for i in range(per):
            out_ref[first + i] = total[:, i * PACKET : (i + 1) * PACKET].astype(BF16)


def combine_kernel(low, chunk, sel_ref, *rest):
    own_refs = rest[:low]
    far_refs = rest[low : 2 * low]
    send_ref, mine_ref = rest[-2:]
    part = send_ref.shape[0]
    here = slice(chunk * part, (chunk + 1) * part)
    own = own_refs[0][here, :]
    for ref in own_refs[1:]:
        own = own + ref[...].astype(F32)
    far = far_refs[0][...].astype(F32)
    for ref in far_refs[1:]:
        far = far + ref[...].astype(F32)
    send_ref[...] = (own * sel_ref[1:2, :] + far * sel_ref[3:4, :]).astype(BF16)
    mine_ref[...] = own * sel_ref[0:1, :] + far * sel_ref[2:3, :]


def last_kernel(*refs):
    mine_refs, got_refs, out_ref = refs[:CHUNKS][::-1], refs[CHUNKS : 2 * CHUNKS][::-1], refs[-1]
    part = out_ref.shape[0] // CHUNKS
    for c in range(CHUNKS):
        out_ref[c * part : (c + 1) * part, :] = (mine_refs[c][...] + got_refs[c][...].astype(F32)).astype(BF16)


def call(kernel, name, ins, outs, scratch=(), smem=(), raw=(), passed=(), flops=0, transcendentals=0):
    spaces = [pltpu.SMEM if i in smem else pltpu.VMEM for i in range(len(ins))]
    ins = list(ins)
    for i in raw:
        spaces[i] = pl.ANY
        ins[i] = pltpu.with_memory_space_constraint(ins[i], pltpu.HBM)
    size = sum(x.size * x.dtype.itemsize for x in ins)
    size += sum(functools.reduce(lambda a, b: a * b, s, jnp.dtype(d).itemsize) for s, d in outs)
    out_spaces = [pltpu.VMEM] * len(outs) + [pl.ANY] * len(passed)
    shapes = [jax.ShapeDtypeStruct(s, d) for s, d in outs]
    shapes += [jax.ShapeDtypeStruct(x.shape, x.dtype) for x in passed]
    aliases = {len(ins) + i: len(outs) + i for i in range(len(passed))}
    return pl.pallas_call(
        kernel,
        name=name,
        out_shape=shapes,
        in_specs=[pl.BlockSpec(memory_space=space) for space in spaces + [pl.ANY] * len(passed)],
        out_specs=[pl.BlockSpec(memory_space=space) for space in out_spaces],
        scratch_shapes=scratch,
        input_output_aliases=aliases,
        compiler_params=pltpu.CompilerParams(vmem_limit_bytes=VMEM_LIMIT),
        cost_estimate=pl.CostEstimate(flops=flops, bytes_accessed=size, transcendentals=transcendentals),
    )(*ins, *passed)


def local(queries, out_grad, latents, log_norm, out_delta, plan):
    n_seq = lax.axis_size("seq")
    n_head = lax.axis_size("head")
    low = n_head // 2
    rows = BLOCK // low
    packet, heads, width = queries.shape
    columns = packet * heads

    lat_t = latents.T
    q_t = jnp.transpose(queries, (1, 2, 0))
    grad = out_grad.reshape(columns, LAT)
    norm_t = log_norm.T
    delta_t = out_delta.T
    visit_flops = 2 * columns * BLOCK * (2 * width + 2 * LAT)

    def route(d, back):
        pairs = []
        for i in range(n_seq):
            for j in range(n_head):
                to = j // low * low + (j + d) % low
                pairs.append((i * n_head + j, (i - back) % n_seq * n_head + to))
        return pairs

    part = rows // CHUNKS
    keys = BLOCK // CHUNKS

    blocks = SHARD // BLOCK
    *sent, lat_blocks = call(
        functools.partial(send_block_kernel, low),
        "send_block",
        (plan, lat_t),
        [((keys, width), BF16)] * CHUNKS + [((blocks, width, BLOCK), BF16)],
        [pltpu.SMEM(plan.shape, plan.dtype), pltpu.SemaphoreType.DMA((blocks + 1,))],
        flops=visit_flops,
        raw=(0, 1),
    )
    far_keys = [lax.ppermute(x, "seq", [(i, (i + 1) % n_seq) for i in range(n_seq)]) for x in sent]

    grad_rows, own_ds, sel, keep, *own = call(
        functools.partial(own_kernel, low),
        "own_visit",
        (plan, lat_blocks, q_t, grad, norm_t, delta_t),
        [((columns, LAT), BF16), ((BLOCK, columns), BF16), ((8, width), F32), ((rows, width), F32)]
        + [((part, width), BF16)] * (CHUNKS * (low - 1)),
        [pltpu.VMEM((BLOCK, columns), BF16), pltpu.VMEM((BLOCK, width), F32)],
    )

    far_ds, own_parts, far_parts = [], [], []
    for c in range(CHUNKS):
        parts = own[c::CHUNKS]
        own_parts.append([keep] + [lax.ppermute(parts[d - 1], ("seq", "head"), route(d, 0)) for d in range(1, low)])
        later = [i for i in range(len(own)) if i % CHUNKS > c]
        ds, *far = call(
            functools.partial(far_kernel, low, len(later)),
            f"far_visit_{c}",
            (far_keys[c], q_t, grad_rows, norm_t, delta_t),
            [((keys, columns), BF16)] + [((part, width), BF16)] * low,
            [pltpu.VMEM((keys, columns), BF16), pltpu.VMEM((keys, width), F32)],
            passed=[own[i] for i in later],
        )
        for i, x in zip(later, far[low:]):
            own[i] = x
        far_ds.append(ds)
        far_parts.append([lax.ppermute(far[d], ("seq", "head"), route(d, 1)) for d in reversed(range(low))])

    mine, got = [None] * CHUNKS, [None] * CHUNKS
    for c in reversed(range(CHUNKS)):
        send, mine[c] = call(
            functools.partial(combine_kernel, low, c),
            f"combine_{c}",
            (sel, *own_parts[c], *far_parts[c]),
            [((part, width), BF16), ((part, width), F32)],
        )
        got[c] = lax.ppermute(send, "head", [(j, (j + low) % n_head) for j in range(n_head)])

    (query_t,) = call(
        query_kernel,
        "query_grad",
        (plan, lat_blocks, own_ds, *far_keys, *far_ds),
        [((heads, width, packet), BF16)],
        flops=4 * columns * BLOCK * width,
    )
    (latent_out,) = call(last_kernel, "last_sum", (*mine[::-1], *got[::-1]), [((rows, width), BF16)])
    return jnp.transpose(query_t, (2, 0, 1)), latent_out


def solution(mesh):
    return jax.shard_map(
        local,
        mesh=mesh,
        in_specs=(
            P("seq", "head", None),
            P("seq", "head", None),
            P("seq", None),
            P("seq", "head"),
            P("seq", "head"),
            P("seq", None),
        ),
        out_specs=(P("seq", "head", None), P(("seq", "head"), None)),
        check_vma=False,
    )
```

```python
import functools

import jax
import jax.numpy as jnp
from jax import lax
from jax.experimental import pallas as pl
from jax.experimental.pallas import tpu as pltpu
from jax.sharding import PartitionSpec as P

LAT = 512
PACKET = 128
BLOCK = 384
SHARD = 768
WIDE = 256
VISIT_WIDE = 512
VMEM_LIMIT = 24 * 2**20
NEVER = 1e30
CHUNKS = 2

F32 = jnp.float32
BF16 = jnp.bfloat16


def dot(a, b):
    return lax.dot_general(a, b, (((1,), (0,)), ((), ())), preferred_element_type=F32)


def dot_nt(a, b):
    return lax.dot_general(a, b, (((1,), (1,)), ((), ())), preferred_element_type=F32)


def send_block_kernel(low, plan_hbm, lat_hbm, *rest):
    out_refs = rest[:CHUNKS]
    lat_ref, plan_ref, sems = rest[CHUNKS:]

    def block_copy(block):
        here = pl.ds(pl.multiple_of(block * BLOCK, 128), BLOCK)
        return pltpu.make_async_copy(lat_hbm.at[:, here], lat_ref.at[block], sems.at[block])

    blocks = lat_ref.shape[0]
    plan_copy = pltpu.make_async_copy(plan_hbm, plan_ref, sems.at[blocks])
    plan_copy.start()
    for block in range(blocks):
        block_copy(block).start()
    plan_copy.wait()
    sent = plan_ref[0, 1]
    block_copy(sent).wait()
    keys = lat_ref[sent].T
    rows = BLOCK // low
    part = rows // CHUNKS
    for c, out_ref in enumerate(out_refs):
        for j in range(low):
            start = j * rows + c * part
            out_ref[j * part : (j + 1) * part, :] = keys[start : start + part, :]
    for i in range(1, blocks):
        block_copy(lax.rem(sent + i, blocks)).wait()


def heads_side_by_side(q_ref, first, count):
    return jnp.concatenate([q_ref[first + i] for i in range(count)], axis=1)


def visit(keys, q_ref, grad_ref, norm_ref, delta_ref, live, visible, ds_ref, p_ref, grad_out_ref):
    heads = q_ref.shape[0]
    per = VISIT_WIDE // PACKET
    for first in range(0, heads, per):
        cols = slice(first * PACKET, (first + per) * PACKET)
        scores = dot(keys, heads_side_by_side(q_ref, first, per))
        prob_grad = dot_nt(keys[:, :LAT], grad_ref[cols, :])
        for i in range(per):
            lanes = slice(i * PACKET, (i + 1) * PACKET)
            norm = norm_ref[first + i : first + i + 1, :].astype(F32)
            if live is not None:
                norm = jnp.where(live, norm, NEVER)
            delta = delta_ref[first + i : first + i + 1, :].astype(F32)
            prob = jnp.exp(scores[:, lanes] - norm)
            if visible is not None:
                tail = jnp.where(visible[-PACKET:], prob[-PACKET:], 0.0)
                prob = jnp.concatenate([prob[:-PACKET], tail], axis=0)
            here = slice((first + i) * PACKET, (first + i + 1) * PACKET)
            ds_ref[:, here] = (prob * (prob_grad[:, lanes] - delta)).astype(BF16)
            p_ref[:, here] = prob.astype(BF16)
    key_grad = dot_nt(ds_ref[...], heads_side_by_side(q_ref, 0, heads))
    value_grad = dot(p_ref[...], grad_ref[...])
    grad_out_ref[:, :LAT] = key_grad[:, :LAT] + value_grad
    grad_out_ref[:, LAT:] = key_grad[:, LAT:]


def pieces_out(total_ref, low, offset, out_refs):
    rows = total_ref.shape[0] // low
    r = lax.rem(lax.axis_index("head"), low)
    for d, out_ref in out_refs:
        start = pl.multiple_of(lax.rem(r + d, low) * rows, 16) + offset
        out_ref[...] = total_ref[pl.ds(start, out_ref.shape[0]), :].astype(out_ref.dtype)


def own_kernel(low, plan_ref, lat_ref, q_ref, grad_ref, norm_ref, delta_ref, *rest):
    rows_ref, ds_ref, sel_ref, keep_ref = rest[:4]
    out_refs = rest[4:-2]
    p_ref, total_ref = rest[-2:]
    heads = q_ref.shape[0]
    group = WIDE // heads
    at = lax.broadcasted_iota(jnp.int32, (WIDE, WIDE), 0)
    come = lax.broadcasted_iota(jnp.int32, (WIDE, WIDE), 1)
    order = (come == lax.rem(at, group) * heads + lax.div(at, group)).astype(F32).astype(BF16)
    for g in range(PACKET // group):
        moved = dot(order, grad_ref[g * WIDE : (g + 1) * WIDE, :]).astype(BF16)
        for h in range(heads):
            rows_ref[h * PACKET + g * group : h * PACKET + (g + 1) * group, :] = moved[h * group : (h + 1) * group, :]
    b0, b1 = plan_ref[0:1, 0:1], plan_ref[0:1, 1:2]
    t = lax.div(lax.axis_index("head"), low)
    for i, hit in enumerate((b0 == t, b0 != t, b1 == t, b1 != t)):
        sel_ref[i : i + 1, :] = jnp.broadcast_to(jnp.where(hit, 1.0, 0.0), (1, sel_ref.shape[1])).astype(F32)
    last = jnp.where(b0 > 0, 1.0, 0.0).astype(BF16)
    first = jnp.where(b0 > 0, 0.0, 1.0).astype(BF16)
    keys = (lat_ref[0] * first + lat_ref[1] * last).T
    k_pos = b0 * BLOCK + lax.broadcasted_iota(jnp.int32, (BLOCK, PACKET), 0)
    q_pos = SHARD - PACKET + lax.broadcasted_iota(jnp.int32, (BLOCK, PACKET), 1)
    visit(keys, q_ref, rows_ref, norm_ref, delta_ref, None, k_pos <= q_pos, ds_ref, p_ref, total_ref)
    pieces_out(total_ref, low, 0, [(0, keep_ref)])
    for i, out_ref in enumerate(out_refs):
        part = out_ref.shape[0]
        pieces_out(total_ref, low, i % CHUNKS * part, [(1 + i // CHUNKS, out_ref)])


def far_kernel(low, held, keys_ref, q_ref, grad_ref, norm_ref, delta_ref, *rest):
    ds_ref = rest[held]
    out_refs = rest[held + 1 : held + 1 + low]
    p_ref, total_ref = rest[-2:]
    live = lax.axis_index("seq") > 0
    visit(keys_ref[...], q_ref, grad_ref, norm_ref, delta_ref, live, None, ds_ref, p_ref, total_ref)
    pieces_out(total_ref, low, 0, list(enumerate(out_refs)))


def query_kernel(plan_ref, lat_ref, own_ds_ref, *rest):
    far_refs = rest[:CHUNKS]
    far_ds_refs = rest[CHUNKS : 2 * CHUNKS]
    out_ref = rest[-1]
    heads = out_ref.shape[0]
    per = WIDE // PACKET
    b0 = plan_ref[0:1, 0:1]
    last = jnp.where(b0 > 0, 1.0, 0.0).astype(BF16)
    first_block = jnp.where(b0 > 0, 0.0, 1.0).astype(BF16)
    own = lat_ref[0] * first_block + lat_ref[1] * last
    fars = [ref[...].T for ref in far_refs]
    for first in range(0, heads, per):
        cols = slice(first * PACKET, (first + per) * PACKET)
        total = dot(own, own_ds_ref[:, cols])
        for far, ds_ref in zip(fars, far_ds_refs):
            total = total + dot(far, ds_ref[:, cols])
        for i in range(per):
            out_ref[first + i] = total[:, i * PACKET : (i + 1) * PACKET].astype(BF16)


def combine_kernel(low, chunk, sel_ref, *rest):
    own_refs = rest[:low]
    far_refs = rest[low : 2 * low]
    send_ref, mine_ref = rest[-2:]
    part = send_ref.shape[0]
    here = slice(chunk * part, (chunk + 1) * part)
    own = own_refs[0][here, :]
    for ref in own_refs[1:]:
        own = own + ref[...].astype(F32)
    far = far_refs[0][...].astype(F32)
    for ref in far_refs[1:]:
        far = far + ref[...].astype(F32)
    send_ref[...] = (own * sel_ref[1:2, :] + far * sel_ref[3:4, :]).astype(BF16)
    mine_ref[...] = own * sel_ref[0:1, :] + far * sel_ref[2:3, :]


def last_kernel(*refs):
    mine_refs, got_refs, out_ref = refs[:CHUNKS][::-1], refs[CHUNKS : 2 * CHUNKS][::-1], refs[-1]
    part = out_ref.shape[0] // CHUNKS
    for c in range(CHUNKS):
        out_ref[c * part : (c + 1) * part, :] = (mine_refs[c][...] + got_refs[c][...].astype(F32)).astype(BF16)


def call(kernel, name, ins, outs, scratch=(), smem=(), raw=(), passed=(), flops=0, transcendentals=0):
    spaces = [pltpu.SMEM if i in smem else pltpu.VMEM for i in range(len(ins))]
    ins = list(ins)
    for i in raw:
        spaces[i] = pl.ANY
        ins[i] = pltpu.with_memory_space_constraint(ins[i], pltpu.HBM)
    size = sum(x.size * x.dtype.itemsize for x in ins)
    size += sum(functools.reduce(lambda a, b: a * b, s, jnp.dtype(d).itemsize) for s, d in outs)
    out_spaces = [pltpu.VMEM] * len(outs) + [pl.ANY] * len(passed)
    shapes = [jax.ShapeDtypeStruct(s, d) for s, d in outs]
    shapes += [jax.ShapeDtypeStruct(x.shape, x.dtype) for x in passed]
    aliases = {len(ins) + i: len(outs) + i for i in range(len(passed))}
    return pl.pallas_call(
        kernel,
        name=name,
        out_shape=shapes,
        in_specs=[pl.BlockSpec(memory_space=space) for space in spaces + [pl.ANY] * len(passed)],
        out_specs=[pl.BlockSpec(memory_space=space) for space in out_spaces],
        scratch_shapes=scratch,
        input_output_aliases=aliases,
        compiler_params=pltpu.CompilerParams(vmem_limit_bytes=VMEM_LIMIT),
        cost_estimate=pl.CostEstimate(flops=flops, bytes_accessed=size, transcendentals=transcendentals),
    )(*ins, *passed)


def local(queries, out_grad, latents, log_norm, out_delta, plan):
    n_seq = lax.axis_size("seq")
    n_head = lax.axis_size("head")
    low = n_head // 2
    rows = BLOCK // low
    packet, heads, width = queries.shape
    columns = packet * heads

    lat_t = latents.T
    q_t = jnp.transpose(queries, (1, 2, 0))
    grad = out_grad.reshape(columns, LAT)
    norm_t = log_norm.T
    delta_t = out_delta.T
    visit_flops = 2 * columns * BLOCK * (2 * width + 2 * LAT)

    def route(d, back):
        pairs = []
        for i in range(n_seq):
            for j in range(n_head):
                to = j // low * low + (j + d) % low
                pairs.append((i * n_head + j, (i - back) % n_seq * n_head + to))
        return pairs

    part = rows // CHUNKS
    keys = BLOCK // CHUNKS

    blocks = SHARD // BLOCK
    *sent, lat_blocks = call(
        functools.partial(send_block_kernel, low),
        "send_block",
        (plan, lat_t),
        [((keys, width), BF16)] * CHUNKS + [((blocks, width, BLOCK), BF16)],
        [pltpu.SMEM(plan.shape, plan.dtype), pltpu.SemaphoreType.DMA((blocks + 1,))],
        flops=visit_flops,
        raw=(0, 1),
    )
    far_keys = [lax.ppermute(x, "seq", [(i, (i + 1) % n_seq) for i in range(n_seq)]) for x in sent]

    grad_rows, own_ds, sel, keep, *own = call(
        functools.partial(own_kernel, low),
        "own_visit",
        (plan, lat_blocks, q_t, grad, norm_t, delta_t),
        [((columns, LAT), BF16), ((BLOCK, columns), BF16), ((8, width), F32), ((rows, width), F32)]
        + [((part, width), BF16)] * (CHUNKS * (low - 1)),
        [pltpu.VMEM((BLOCK, columns), BF16), pltpu.VMEM((BLOCK, width), F32)],
    )

    far_ds, own_parts, far_parts = [], [], []
    for c in range(CHUNKS):
        parts = own[c::CHUNKS]
        own_parts.append([keep] + [lax.ppermute(parts[d - 1], ("seq", "head"), route(d, 0)) for d in range(1, low)])
        later = [i for i in range(len(own)) if i % CHUNKS > c]
        ds, *far = call(
            functools.partial(far_kernel, low, len(later)),
            f"far_visit_{c}",
            (far_keys[c], q_t, grad_rows, norm_t, delta_t),
            [((keys, columns), BF16)] + [((part, width), BF16)] * low,
            [pltpu.VMEM((keys, columns), BF16), pltpu.VMEM((keys, width), F32)],
            passed=[own[i] for i in later],
        )
        for i, x in zip(later, far[low:]):
            own[i] = x
        far_ds.append(ds)
        far_parts.append([lax.ppermute(far[d], ("seq", "head"), route(d, 1)) for d in reversed(range(low))])

    mine, got = [None] * CHUNKS, [None] * CHUNKS
    for c in reversed(range(CHUNKS)):
        send, mine[c] = call(
            functools.partial(combine_kernel, low, c),
            f"combine_{c}",
            (sel, *own_parts[c], *far_parts[c]),
            [((part, width), BF16), ((part, width), F32)],
        )
        got[c] = lax.ppermute(send, "head", [(j, (j + low) % n_head) for j in range(n_head)])

    (query_t,) = call(
        query_kernel,
        "query_grad",
        (plan, lat_blocks, own_ds, *far_keys, *far_ds),
        [((heads, width, packet), BF16)],
        flops=4 * columns * BLOCK * width,
    )
    (latent_out,) = call(last_kernel, "last_sum", (*mine[::-1], *got[::-1]), [((rows, width), BF16)])
    return jnp.transpose(query_t, (2, 0, 1)), latent_out


def solution(mesh):
    return jax.shard_map(
        local,
        mesh=mesh,
        in_specs=(
            P("seq", "head", None),
            P("seq", "head", None),
            P("seq", None),
            P("seq", "head"),
            P("seq", "head"),
            P("seq", None),
        ),
        out_specs=(P("seq", "head", None), P(("seq", "head"), None)),
        check_vma=False,
    )
```

```python
import functools

import jax
import jax.numpy as jnp
from jax import lax
from jax.experimental import pallas as pl
from jax.experimental.pallas import tpu as pltpu
from jax.sharding import PartitionSpec as P

LAT = 512
PACKET = 128
BLOCK = 384
SHARD = 768
WIDE = 256
VMEM_LIMIT = 24 * 2**20
NEVER = 1e30
CHUNKS = 2

F32 = jnp.float32
BF16 = jnp.bfloat16


def dot(a, b):
    return lax.dot_general(a, b, (((1,), (0,)), ((), ())), preferred_element_type=F32)


def dot_nt(a, b):
    return lax.dot_general(a, b, (((1,), (1,)), ((), ())), preferred_element_type=F32)


def send_block_kernel(low, plan_hbm, lat_hbm, *rest):
    out_refs = rest[:CHUNKS]
    lat_ref, plan_ref, sems = rest[CHUNKS:]

    def block_copy(block):
        here = pl.ds(pl.multiple_of(block * BLOCK, 128), BLOCK)
        return pltpu.make_async_copy(lat_hbm.at[:, here], lat_ref.at[block], sems.at[block])

    blocks = lat_ref.shape[0]
    plan_copy = pltpu.make_async_copy(plan_hbm, plan_ref, sems.at[blocks])
    plan_copy.start()
    for block in range(blocks):
        block_copy(block).start()
    plan_copy.wait()
    sent = plan_ref[0, 1]
    block_copy(sent).wait()
    keys = lat_ref[sent].T
    rows = BLOCK // low
    part = rows // CHUNKS
    for c, out_ref in enumerate(out_refs):
        for j in range(low):
            start = j * rows + c * part
            out_ref[j * part : (j + 1) * part, :] = keys[start : start + part, :]
    for i in range(1, blocks):
        block_copy(lax.rem(sent + i, blocks)).wait()


def heads_side_by_side(q_ref, first, count):
    return jnp.concatenate([q_ref[first + i] for i in range(count)], axis=1)


def visit(keys, q_ref, grad_ref, norm_ref, delta_ref, live, visible, ds_ref, p_ref, grad_out_ref):
    heads = q_ref.shape[0]
    per = WIDE // PACKET
    for first in range(0, heads, per):
        cols = slice(first * PACKET, (first + per) * PACKET)
        scores = dot(keys, heads_side_by_side(q_ref, first, per))
        prob_grad = dot_nt(keys[:, :LAT], grad_ref[cols, :])
        for i in range(per):
            lanes = slice(i * PACKET, (i + 1) * PACKET)
            norm = norm_ref[first + i : first + i + 1, :].astype(F32)
            if live is not None:
                norm = jnp.where(live, norm, NEVER)
            delta = delta_ref[first + i : first + i + 1, :].astype(F32)
            prob = jnp.exp(scores[:, lanes] - norm)
            if visible is not None:
                tail = jnp.where(visible[-PACKET:], prob[-PACKET:], 0.0)
                prob = jnp.concatenate([prob[:-PACKET], tail], axis=0)
            here = slice((first + i) * PACKET, (first + i + 1) * PACKET)
            ds_ref[:, here] = (prob * (prob_grad[:, lanes] - delta)).astype(BF16)
            p_ref[:, here] = prob.astype(BF16)
        if (first + per) % (heads // 2) == 0:
            half = slice((first + per) * PACKET - heads // 2 * PACKET, (first + per) * PACKET)
            key_grad = dot_nt(ds_ref[:, half], heads_side_by_side(q_ref, first + per - heads // 2, heads // 2))
            value_grad = dot(p_ref[:, half], grad_ref[half, :])
            if first + per > heads // 2:
                grad_out_ref[:, :LAT] += key_grad[:, :LAT] + value_grad
                grad_out_ref[:, LAT:] += key_grad[:, LAT:]
            else:
                grad_out_ref[:, :LAT] = key_grad[:, :LAT] + value_grad
                grad_out_ref[:, LAT:] = key_grad[:, LAT:]


def pieces_out(total_ref, low, offset, out_refs):
    rows = total_ref.shape[0] // low
    r = lax.rem(lax.axis_index("head"), low)
    for d, out_ref in out_refs:
        start = pl.multiple_of(lax.rem(r + d, low) * rows, 16) + offset
        out_ref[...] = total_ref[pl.ds(start, out_ref.shape[0]), :].astype(out_ref.dtype)


def own_kernel(low, plan_ref, lat_ref, q_ref, grad_ref, norm_ref, delta_ref, *rest):
    rows_ref, ds_ref, sel_ref, keep_ref = rest[:4]
    out_refs = rest[4:-2]
    p_ref, total_ref = rest[-2:]
    heads = q_ref.shape[0]
    group = WIDE // heads
    at = lax.broadcasted_iota(jnp.int32, (WIDE, WIDE), 0)
    come = lax.broadcasted_iota(jnp.int32, (WIDE, WIDE), 1)
    order = (come == lax.rem(at, group) * heads + lax.div(at, group)).astype(F32).astype(BF16)
    for g in range(PACKET // group):
        moved = dot(order, grad_ref[g * WIDE : (g + 1) * WIDE, :]).astype(BF16)
        for h in range(heads):
            rows_ref[h * PACKET + g * group : h * PACKET + (g + 1) * group, :] = moved[h * group : (h + 1) * group, :]
    b0, b1 = plan_ref[0:1, 0:1], plan_ref[0:1, 1:2]
    t = lax.div(lax.axis_index("head"), low)
    for i, hit in enumerate((b0 == t, b0 != t, b1 == t, b1 != t)):
        sel_ref[i : i + 1, :] = jnp.broadcast_to(jnp.where(hit, 1.0, 0.0), (1, sel_ref.shape[1])).astype(F32)
    last = jnp.where(b0 > 0, 1.0, 0.0).astype(BF16)
    first = jnp.where(b0 > 0, 0.0, 1.0).astype(BF16)
    keys = (lat_ref[0] * first + lat_ref[1] * last).T
    k_pos = b0 * BLOCK + lax.broadcasted_iota(jnp.int32, (BLOCK, PACKET), 0)
    q_pos = SHARD - PACKET + lax.broadcasted_iota(jnp.int32, (BLOCK, PACKET), 1)
    visit(keys, q_ref, rows_ref, norm_ref, delta_ref, None, k_pos <= q_pos, ds_ref, p_ref, total_ref)
    pieces_out(total_ref, low, 0, [(0, keep_ref)])
    for i, out_ref in enumerate(out_refs):
        part = out_ref.shape[0]
        pieces_out(total_ref, low, i % CHUNKS * part, [(1 + i // CHUNKS, out_ref)])


def far_kernel(low, held, keys_ref, q_ref, grad_ref, norm_ref, delta_ref, *rest):
    ds_ref = rest[held]
    out_refs = rest[held + 1 : held + 1 + low]
    p_ref, total_ref = rest[-2:]
    live = lax.axis_index("seq") > 0
    visit(keys_ref[...], q_ref, grad_ref, norm_ref, delta_ref, live, None, ds_ref, p_ref, total_ref)
    pieces_out(total_ref, low, 0, list(enumerate(out_refs)))


def query_kernel(plan_ref, lat_ref, own_ds_ref, *rest):
    far_refs = rest[:CHUNKS]
    far_ds_refs = rest[CHUNKS : 2 * CHUNKS]
    out_ref = rest[-1]
    heads = out_ref.shape[0]
    per = WIDE // PACKET
    b0 = plan_ref[0:1, 0:1]
    last = jnp.where(b0 > 0, 1.0, 0.0).astype(BF16)
    first_block = jnp.where(b0 > 0, 0.0, 1.0).astype(BF16)
    own = lat_ref[0] * first_block + lat_ref[1] * last
    fars = [ref[...].T for ref in far_refs]
    for first in range(0, heads, per):
        cols = slice(first * PACKET, (first + per) * PACKET)
        total = dot(own, own_ds_ref[:, cols])
        for far, ds_ref in zip(fars, far_ds_refs):
            total = total + dot(far, ds_ref[:, cols])
        for i in range(per):
            out_ref[first + i] = total[:, i * PACKET : (i + 1) * PACKET].astype(BF16)


def combine_kernel(low, chunk, sel_ref, *rest):
    own_refs = rest[:low]
    far_refs = rest[low : 2 * low]
    send_ref, mine_ref = rest[-2:]
    part = send_ref.shape[0]
    here = slice(chunk * part, (chunk + 1) * part)
    own = own_refs[0][here, :]
    for ref in own_refs[1:]:
        own = own + ref[...].astype(F32)
    far = far_refs[0][...].astype(F32)
    for ref in far_refs[1:]:
        far = far + ref[...].astype(F32)
    send_ref[...] = (own * sel_ref[1:2, :] + far * sel_ref[3:4, :]).astype(BF16)
    mine_ref[...] = own * sel_ref[0:1, :] + far * sel_ref[2:3, :]


def last_kernel(*refs):
    mine_refs, got_refs, out_ref = refs[:CHUNKS][::-1], refs[CHUNKS : 2 * CHUNKS][::-1], refs[-1]
    part = out_ref.shape[0] // CHUNKS
    for c in range(CHUNKS):
        out_ref[c * part : (c + 1) * part, :] = (mine_refs[c][...] + got_refs[c][...].astype(F32)).astype(BF16)


def call(kernel, name, ins, outs, scratch=(), smem=(), raw=(), passed=(), flops=0, transcendentals=0):
    spaces = [pltpu.SMEM if i in smem else pltpu.VMEM for i in range(len(ins))]
    ins = list(ins)
    for i in raw:
        spaces[i] = pl.ANY
        ins[i] = pltpu.with_memory_space_constraint(ins[i], pltpu.HBM)
    size = sum(x.size * x.dtype.itemsize for x in ins)
    size += sum(functools.reduce(lambda a, b: a * b, s, jnp.dtype(d).itemsize) for s, d in outs)
    out_spaces = [pltpu.VMEM] * len(outs) + [pl.ANY] * len(passed)
    shapes = [jax.ShapeDtypeStruct(s, d) for s, d in outs]
    shapes += [jax.ShapeDtypeStruct(x.shape, x.dtype) for x in passed]
    aliases = {len(ins) + i: len(outs) + i for i in range(len(passed))}
    return pl.pallas_call(
        kernel,
        name=name,
        out_shape=shapes,
        in_specs=[pl.BlockSpec(memory_space=space) for space in spaces + [pl.ANY] * len(passed)],
        out_specs=[pl.BlockSpec(memory_space=space) for space in out_spaces],
        scratch_shapes=scratch,
        input_output_aliases=aliases,
        compiler_params=pltpu.CompilerParams(vmem_limit_bytes=VMEM_LIMIT),
        cost_estimate=pl.CostEstimate(flops=flops, bytes_accessed=size, transcendentals=transcendentals),
    )(*ins, *passed)


def local(queries, out_grad, latents, log_norm, out_delta, plan):
    n_seq = lax.axis_size("seq")
    n_head = lax.axis_size("head")
    low = n_head // 2
    rows = BLOCK // low
    packet, heads, width = queries.shape
    columns = packet * heads

    lat_t = latents.T
    q_t = jnp.transpose(queries, (1, 2, 0))
    grad = out_grad.reshape(columns, LAT)
    norm_t = log_norm.T
    delta_t = out_delta.T
    visit_flops = 2 * columns * BLOCK * (2 * width + 2 * LAT)

    def route(d, back):
        pairs = []
        for i in range(n_seq):
            for j in range(n_head):
                to = j // low * low + (j + d) % low
                pairs.append((i * n_head + j, (i - back) % n_seq * n_head + to))
        return pairs

    part = rows // CHUNKS
    keys = BLOCK // CHUNKS

    blocks = SHARD // BLOCK
    *sent, lat_blocks = call(
        functools.partial(send_block_kernel, low),
        "send_block",
        (plan, lat_t),
        [((keys, width), BF16)] * CHUNKS + [((blocks, width, BLOCK), BF16)],
        [pltpu.SMEM(plan.shape, plan.dtype), pltpu.SemaphoreType.DMA((blocks + 1,))],
        flops=visit_flops,
        raw=(0, 1),
    )
    far_keys = [lax.ppermute(x, "seq", [(i, (i + 1) % n_seq) for i in range(n_seq)]) for x in sent]

    grad_rows, own_ds, sel, keep, *own = call(
        functools.partial(own_kernel, low),
        "own_visit",
        (plan, lat_blocks, q_t, grad, norm_t, delta_t),
        [((columns, LAT), BF16), ((BLOCK, columns), BF16), ((8, width), F32), ((rows, width), F32)]
        + [((part, width), BF16)] * (CHUNKS * (low - 1)),
        [pltpu.VMEM((BLOCK, columns), BF16), pltpu.VMEM((BLOCK, width), F32)],
    )

    far_ds, own_parts, far_parts = [], [], []
    for c in range(CHUNKS):
        parts = own[c::CHUNKS]
        own_parts.append([keep] + [lax.ppermute(parts[d - 1], ("seq", "head"), route(d, 0)) for d in range(1, low)])
        later = [i for i in range(len(own)) if i % CHUNKS > c]
        ds, *far = call(
            functools.partial(far_kernel, low, len(later)),
            f"far_visit_{c}",
            (far_keys[c], q_t, grad_rows, norm_t, delta_t),
            [((keys, columns), BF16)] + [((part, width), BF16)] * low,
            [pltpu.VMEM((keys, columns), BF16), pltpu.VMEM((keys, width), F32)],
            passed=[own[i] for i in later],
        )
        for i, x in zip(later, far[low:]):
            own[i] = x
        far_ds.append(ds)
        far_parts.append([lax.ppermute(far[d], ("seq", "head"), route(d, 1)) for d in reversed(range(low))])

    mine, got = [None] * CHUNKS, [None] * CHUNKS
    for c in reversed(range(CHUNKS)):
        send, mine[c] = call(
            functools.partial(combine_kernel, low, c),
            f"combine_{c}",
            (sel, *own_parts[c], *far_parts[c]),
            [((part, width), BF16), ((part, width), F32)],
        )
        got[c] = lax.ppermute(send, "head", [(j, (j + low) % n_head) for j in range(n_head)])

    (query_t,) = call(
        query_kernel,
        "query_grad",
        (plan, lat_blocks, own_ds, *far_keys, *far_ds),
        [((heads, width, packet), BF16)],
        flops=4 * columns * BLOCK * width,
    )
    (latent_out,) = call(last_kernel, "last_sum", (*mine[::-1], *got[::-1]), [((rows, width), BF16)])
    return jnp.transpose(query_t, (2, 0, 1)), latent_out


def solution(mesh):
    return jax.shard_map(
        local,
        mesh=mesh,
        in_specs=(
            P("seq", "head", None),
            P("seq", "head", None),
            P("seq", None),
            P("seq", "head"),
            P("seq", "head"),
            P("seq", None),
        ),
        out_specs=(P("seq", "head", None), P(("seq", "head"), None)),
        check_vma=False,
    )
```

```python
import functools

import jax
import jax.numpy as jnp
from jax import lax
from jax.experimental import pallas as pl
from jax.experimental.pallas import tpu as pltpu
from jax.sharding import PartitionSpec as P

LAT = 512
PACKET = 128
BLOCK = 384
SHARD = 768
WIDE = 256
VMEM_LIMIT = 24 * 2**20
NEVER = 1e30
CHUNKS = 2
FIRST_SHARE = 7 / 12

F32 = jnp.float32
BF16 = jnp.bfloat16


def dot(a, b):
    return lax.dot_general(a, b, (((1,), (0,)), ((), ())), preferred_element_type=F32)


def dot_nt(a, b):
    return lax.dot_general(a, b, (((1,), (1,)), ((), ())), preferred_element_type=F32)


def chunks_of(rows):
    first = -(-int(rows * FIRST_SHARE) // 16) * 16
    return [(0, first), (first, rows - first)]


def send_block_kernel(low, plan_hbm, lat_hbm, *rest):
    out_refs = rest[:CHUNKS]
    lat_ref, plan_ref, sems = rest[CHUNKS:]

    def block_copy(block):
        here = pl.ds(pl.multiple_of(block * BLOCK, 128), BLOCK)
        return pltpu.make_async_copy(lat_hbm.at[:, here], lat_ref.at[block], sems.at[block])

    blocks = lat_ref.shape[0]
    plan_copy = pltpu.make_async_copy(plan_hbm, plan_ref, sems.at[blocks])
    plan_copy.start()
    for block in range(blocks):
        block_copy(block).start()
    plan_copy.wait()
    sent = plan_ref[0, 1]
    block_copy(sent).wait()
    keys = lat_ref[sent].T
    rows = BLOCK // low
    for (offset, part), out_ref in zip(chunks_of(rows), out_refs):
        for j in range(low):
            start = j * rows + offset
            out_ref[j * part : (j + 1) * part, :] = keys[start : start + part, :]
    for i in range(1, blocks):
        block_copy(lax.rem(sent + i, blocks)).wait()


def heads_side_by_side(q_ref, first, count):
    return jnp.concatenate([q_ref[first + i] for i in range(count)], axis=1)


def visit(keys, q_ref, grad_ref, norm_ref, delta_ref, live, visible, ds_ref, p_ref, grad_out_ref):
    heads = q_ref.shape[0]
    per = WIDE // PACKET
    for first in range(0, heads, per):
        cols = slice(first * PACKET, (first + per) * PACKET)
        scores = dot(keys, heads_side_by_side(q_ref, first, per))
        prob_grad = dot_nt(keys[:, :LAT], grad_ref[cols, :])
        for i in range(per):
            lanes = slice(i * PACKET, (i + 1) * PACKET)
            norm = norm_ref[first + i : first + i + 1, :].astype(F32)
            if live is not None:
                norm = jnp.where(live, norm, NEVER)
            delta = delta_ref[first + i : first + i + 1, :].astype(F32)
            prob = jnp.exp(scores[:, lanes] - norm)
            if visible is not None:
                tail = jnp.where(visible[-PACKET:], prob[-PACKET:], 0.0)
                prob = jnp.concatenate([prob[:-PACKET], tail], axis=0)
            here = slice((first + i) * PACKET, (first + i + 1) * PACKET)
            ds_ref[:, here] = (prob * (prob_grad[:, lanes] - delta)).astype(BF16)
            p_ref[:, here] = prob.astype(BF16)
    key_grad = dot_nt(ds_ref[...], heads_side_by_side(q_ref, 0, heads))
    value_grad = dot(p_ref[...], grad_ref[...])
    grad_out_ref[:, :LAT] = key_grad[:, :LAT] + value_grad
    grad_out_ref[:, LAT:] = key_grad[:, LAT:]


def pieces_out(total_ref, low, offset, out_refs):
    rows = total_ref.shape[0] // low
    r = lax.rem(lax.axis_index("head"), low)
    for d, out_ref in out_refs:
        start = pl.multiple_of(lax.rem(r + d, low) * rows, 16) + offset
        out_ref[...] = total_ref[pl.ds(start, out_ref.shape[0]), :].astype(out_ref.dtype)


def own_kernel(low, plan_ref, lat_ref, q_ref, grad_ref, norm_ref, delta_ref, *rest):
    rows_ref, ds_ref, sel_ref, keep_ref = rest[:4]
    out_refs = rest[4:-2]
    p_ref, total_ref = rest[-2:]
    heads = q_ref.shape[0]
    group = WIDE // heads
    at = lax.broadcasted_iota(jnp.int32, (WIDE, WIDE), 0)
    come = lax.broadcasted_iota(jnp.int32, (WIDE, WIDE), 1)
    order = (come == lax.rem(at, group) * heads + lax.div(at, group)).astype(F32).astype(BF16)
    for g in range(PACKET // group):
        moved = dot(order, grad_ref[g * WIDE : (g + 1) * WIDE, :]).astype(BF16)
        for h in range(heads):
            rows_ref[h * PACKET + g * group : h * PACKET + (g + 1) * group, :] = moved[h * group : (h + 1) * group, :]
    b0, b1 = plan_ref[0:1, 0:1], plan_ref[0:1, 1:2]
    t = lax.div(lax.axis_index("head"), low)
    for i, hit in enumerate((b0 == t, b0 != t, b1 == t, b1 != t)):
        sel_ref[i : i + 1, :] = jnp.broadcast_to(jnp.where(hit, 1.0, 0.0), (1, sel_ref.shape[1])).astype(F32)
    last = jnp.where(b0 > 0, 1.0, 0.0).astype(BF16)
    first = jnp.where(b0 > 0, 0.0, 1.0).astype(BF16)
    keys = (lat_ref[0] * first + lat_ref[1] * last).T
    k_pos = b0 * BLOCK + lax.broadcasted_iota(jnp.int32, (BLOCK, PACKET), 0)
    q_pos = SHARD - PACKET + lax.broadcasted_iota(jnp.int32, (BLOCK, PACKET), 1)
    visit(keys, q_ref, rows_ref, norm_ref, delta_ref, None, k_pos <= q_pos, ds_ref, p_ref, total_ref)
    pieces_out(total_ref, low, 0, [(0, keep_ref)])
    for i, out_ref in enumerate(out_refs):
        offset, _ = chunks_of(BLOCK // low)[i % CHUNKS]
        pieces_out(total_ref, low, offset, [(1 + i // CHUNKS, out_ref)])


def far_kernel(low, held, keys_ref, q_ref, grad_ref, norm_ref, delta_ref, *rest):
    ds_ref = rest[held]
    out_refs = rest[held + 1 : held + 1 + low]
    p_ref, total_ref = rest[-2:]
    live = lax.axis_index("seq") > 0
    visit(keys_ref[...], q_ref, grad_ref, norm_ref, delta_ref, live, None, ds_ref, p_ref, total_ref)
    pieces_out(total_ref, low, 0, list(enumerate(out_refs)))


def query_kernel(plan_ref, lat_ref, own_ds_ref, *rest):
    far_refs = rest[:CHUNKS]
    far_ds_refs = rest[CHUNKS : 2 * CHUNKS]
    out_ref = rest[-1]
    heads = out_ref.shape[0]
    per = WIDE // PACKET
    b0 = plan_ref[0:1, 0:1]
    last = jnp.where(b0 > 0, 1.0, 0.0).astype(BF16)
    first_block = jnp.where(b0 > 0, 0.0, 1.0).astype(BF16)
    own = lat_ref[0] * first_block + lat_ref[1] * last
    fars = [ref[...].T for ref in far_refs]
    for first in range(0, heads, per):
        cols = slice(first * PACKET, (first + per) * PACKET)
        total = dot(own, own_ds_ref[:, cols])
        for far, ds_ref in zip(fars, far_ds_refs):
            total = total + dot(far, ds_ref[:, cols])
        for i in range(per):
            out_ref[first + i] = total[:, i * PACKET : (i + 1) * PACKET].astype(BF16)


def combine_kernel(low, offset, sel_ref, *rest):
    own_refs = rest[:low]
    far_refs = rest[low : 2 * low]
    send_ref, mine_ref = rest[-2:]
    part = send_ref.shape[0]
    here = slice(offset, offset + part)
    own = own_refs[0][here, :]
    for ref in own_refs[1:]:
        own = own + ref[...].astype(F32)
    far = far_refs[0][...].astype(F32)
    for ref in far_refs[1:]:
        far = far + ref[...].astype(F32)
    send_ref[...] = (own * sel_ref[1:2, :] + far * sel_ref[3:4, :]).astype(BF16)
    mine_ref[...] = own * sel_ref[0:1, :] + far * sel_ref[2:3, :]


def last_kernel(*refs):
    mine_refs, got_refs, out_ref = refs[:CHUNKS][::-1], refs[CHUNKS : 2 * CHUNKS][::-1], refs[-1]
    for (offset, part), mine_ref, got_ref in zip(chunks_of(out_ref.shape[0]), mine_refs, got_refs):
        out_ref[offset : offset + part, :] = (mine_ref[...] + got_ref[...].astype(F32)).astype(BF16)


def call(kernel, name, ins, outs, scratch=(), smem=(), raw=(), passed=(), flops=0, transcendentals=0):
    spaces = [pltpu.SMEM if i in smem else pltpu.VMEM for i in range(len(ins))]
    ins = list(ins)
    for i in raw:
        spaces[i] = pl.ANY
        ins[i] = pltpu.with_memory_space_constraint(ins[i], pltpu.HBM)
    size = sum(x.size * x.dtype.itemsize for x in ins)
    size += sum(functools.reduce(lambda a, b: a * b, s, jnp.dtype(d).itemsize) for s, d in outs)
    out_spaces = [pltpu.VMEM] * len(outs) + [pl.ANY] * len(passed)
    shapes = [jax.ShapeDtypeStruct(s, d) for s, d in outs]
    shapes += [jax.ShapeDtypeStruct(x.shape, x.dtype) for x in passed]
    aliases = {len(ins) + i: len(outs) + i for i in range(len(passed))}
    return pl.pallas_call(
        kernel,
        name=name,
        out_shape=shapes,
        in_specs=[pl.BlockSpec(memory_space=space) for space in spaces + [pl.ANY] * len(passed)],
        out_specs=[pl.BlockSpec(memory_space=space) for space in out_spaces],
        scratch_shapes=scratch,
        input_output_aliases=aliases,
        compiler_params=pltpu.CompilerParams(vmem_limit_bytes=VMEM_LIMIT),
        cost_estimate=pl.CostEstimate(flops=flops, bytes_accessed=size, transcendentals=transcendentals),
    )(*ins, *passed)


def local(queries, out_grad, latents, log_norm, out_delta, plan):
    n_seq = lax.axis_size("seq")
    n_head = lax.axis_size("head")
    low = n_head // 2
    rows = BLOCK // low
    packet, heads, width = queries.shape
    columns = packet * heads

    lat_t = latents.T
    q_t = jnp.transpose(queries, (1, 2, 0))
    grad = out_grad.reshape(columns, LAT)
    norm_t = log_norm.T
    delta_t = out_delta.T
    visit_flops = 2 * columns * BLOCK * (2 * width + 2 * LAT)

    def route(d, back):
        pairs = []
        for i in range(n_seq):
            for j in range(n_head):
                to = j // low * low + (j + d) % low
                pairs.append((i * n_head + j, (i - back) % n_seq * n_head + to))
        return pairs

    chunks = chunks_of(rows)

    blocks = SHARD // BLOCK
    *sent, lat_blocks = call(
        functools.partial(send_block_kernel, low),
        "send_block",
        (plan, lat_t),
        [((low * part, width), BF16) for _, part in chunks] + [((blocks, width, BLOCK), BF16)],
        [pltpu.SMEM(plan.shape, plan.dtype), pltpu.SemaphoreType.DMA((blocks + 1,))],
        flops=visit_flops,
        raw=(0, 1),
    )
    far_keys = [lax.ppermute(x, "seq", [(i, (i + 1) % n_seq) for i in range(n_seq)]) for x in sent]

    grad_rows, own_ds, sel, keep, *own = call(
        functools.partial(own_kernel, low),
        "own_visit",
        (plan, lat_blocks, q_t, grad, norm_t, delta_t),
        [((columns, LAT), BF16), ((BLOCK, columns), BF16), ((8, width), F32), ((rows, width), F32)]
        + [((part, width), BF16) for _, part in chunks] * (low - 1),
        [pltpu.VMEM((BLOCK, columns), BF16), pltpu.VMEM((BLOCK, width), F32)],
    )

    far_ds, own_parts, far_parts = [], [], []
    for c, (_, part) in enumerate(chunks):
        keys = low * part
        parts = own[c::CHUNKS]
        own_parts.append([keep] + [lax.ppermute(parts[d - 1], ("seq", "head"), route(d, 0)) for d in range(1, low)])
        later = [i for i in range(len(own)) if i % CHUNKS > c]
        ds, *far = call(
            functools.partial(far_kernel, low, len(later)),
            f"far_visit_{c}",
            (far_keys[c], q_t, grad_rows, norm_t, delta_t),
            [((keys, columns), BF16)] + [((part, width), BF16)] * low,
            [pltpu.VMEM((keys, columns), BF16), pltpu.VMEM((keys, width), F32)],
            passed=[own[i] for i in later],
        )
        for i, x in zip(later, far[low:]):
            own[i] = x
        far_ds.append(ds)
        far_parts.append([lax.ppermute(far[d], ("seq", "head"), route(d, 1)) for d in reversed(range(low))])

    mine, got = [None] * CHUNKS, [None] * CHUNKS
    for c, (offset, part) in reversed(list(enumerate(chunks))):
        send, mine[c] = call(
            functools.partial(combine_kernel, low, offset),
            f"combine_{c}",
            (sel, *own_parts[c], *far_parts[c]),
            [((part, width), BF16), ((part, width), F32)],
        )
        got[c] = lax.ppermute(send, "head", [(j, (j + low) % n_head) for j in range(n_head)])

    (query_t,) = call(
        query_kernel,
        "query_grad",
        (plan, lat_blocks, own_ds, *far_keys, *far_ds),
        [((heads, width, packet), BF16)],
        flops=4 * columns * BLOCK * width,
    )
    (latent_out,) = call(last_kernel, "last_sum", (*mine[::-1], *got[::-1]), [((rows, width), BF16)])
    return jnp.transpose(query_t, (2, 0, 1)), latent_out


def solution(mesh):
    return jax.shard_map(
        local,
        mesh=mesh,
        in_specs=(
            P("seq", "head", None),
            P("seq", "head", None),
            P("seq", None),
            P("seq", "head"),
            P("seq", "head"),
            P("seq", None),
        ),
        out_specs=(P("seq", "head", None), P(("seq", "head"), None)),
        check_vma=False,
    )
```

```python
import functools

import jax
import jax.numpy as jnp
from jax import lax
from jax.experimental import pallas as pl
from jax.experimental.pallas import tpu as pltpu
from jax.sharding import PartitionSpec as P

LAT = 512
PACKET = 128
BLOCK = 384
SHARD = 768
WIDE = 256
VMEM_LIMIT = 24 * 2**20
NEVER = 1e30
CHUNKS = 2

F32 = jnp.float32
BF16 = jnp.bfloat16


def dot(a, b):
    return lax.dot_general(a, b, (((1,), (0,)), ((), ())), preferred_element_type=F32)


def dot_nt(a, b):
    return lax.dot_general(a, b, (((1,), (1,)), ((), ())), preferred_element_type=F32)


def send_block_kernel(low, plan_hbm, lat_hbm, *rest):
    out_refs = rest[:CHUNKS]
    lat_ref, plan_ref, sems = rest[CHUNKS:]

    def block_copy(block):
        here = pl.ds(pl.multiple_of(block * BLOCK, 128), BLOCK)
        return pltpu.make_async_copy(lat_hbm.at[:, here], lat_ref.at[block], sems.at[block])

    blocks = lat_ref.shape[0]
    plan_copy = pltpu.make_async_copy(plan_hbm, plan_ref, sems.at[blocks])
    plan_copy.start()
    for block in range(blocks):
        block_copy(block).start()
    plan_copy.wait()
    sent = plan_ref[0, 1]
    block_copy(sent).wait()
    keys = lat_ref[sent].T
    rows = BLOCK // low
    part = rows // CHUNKS
    for c, out_ref in enumerate(out_refs):
        for j in range(low):
            start = j * rows + c * part
            out_ref[j * part : (j + 1) * part, :] = keys[start : start + part, :]
    for i in range(1, blocks):
        block_copy(lax.rem(sent + i, blocks)).wait()


def heads_side_by_side(q_ref, first, count):
    return jnp.concatenate([q_ref[first + i] for i in range(count)], axis=1)


def visit(keys, q_ref, grad_ref, norm_ref, delta_ref, live, visible, ds_ref, p_ref, grad_out_ref):
    heads = q_ref.shape[0]
    per = WIDE // PACKET
    for first in range(0, heads, per):
        cols = slice(first * PACKET, (first + per) * PACKET)
        scores = dot(keys, heads_side_by_side(q_ref, first, per))
        prob_grad = dot_nt(keys[:, :LAT], grad_ref[cols, :])
        for i in range(per):
            lanes = slice(i * PACKET, (i + 1) * PACKET)
            norm = norm_ref[first + i : first + i + 1, :].astype(F32)
            if live is not None:
                norm = jnp.where(live, norm, NEVER)
            delta = delta_ref[first + i : first + i + 1, :].astype(F32)
            prob = jnp.exp(scores[:, lanes] - norm)
            if visible is not None:
                tail = jnp.where(visible[-PACKET:], prob[-PACKET:], 0.0)
                prob = jnp.concatenate([prob[:-PACKET], tail], axis=0)
            here = slice((first + i) * PACKET, (first + i + 1) * PACKET)
            ds_ref[:, here] = (prob * (prob_grad[:, lanes] - delta)).astype(BF16)
            p_ref[:, here] = prob.astype(BF16)
    key_grad = dot_nt(ds_ref[...], heads_side_by_side(q_ref, 0, heads))
    value_grad = dot(p_ref[...], grad_ref[...])
    grad_out_ref[:, :LAT] = key_grad[:, :LAT] + value_grad
    grad_out_ref[:, LAT:] = key_grad[:, LAT:]


def pieces_out(total_ref, low, offset, out_refs):
    rows = total_ref.shape[0] // low
    r = lax.rem(lax.axis_index("head"), low)
    for d, out_ref in out_refs:
        start = pl.multiple_of(lax.rem(r + d, low) * rows, 16) + offset
        out_ref[...] = total_ref[pl.ds(start, out_ref.shape[0]), :].astype(out_ref.dtype)


def own_kernel(low, plan_ref, lat_ref, q_ref, grad_ref, norm_ref, delta_ref, *rest):
    rows_ref, ds_ref, sel_ref, keep_ref = rest[:4]
    out_refs = rest[4:-2]
    p_ref, total_ref = rest[-2:]
    heads = q_ref.shape[0]
    group = WIDE // heads
    at = lax.broadcasted_iota(jnp.int32, (WIDE, WIDE), 0)
    come = lax.broadcasted_iota(jnp.int32, (WIDE, WIDE), 1)
    order = (come == lax.rem(at, group) * heads + lax.div(at, group)).astype(F32).astype(BF16)
    for g in range(PACKET // group):
        moved = dot(order, grad_ref[g * WIDE : (g + 1) * WIDE, :]).astype(BF16)
        for h in range(heads):
            rows_ref[h * PACKET + g * group : h * PACKET + (g + 1) * group, :] = moved[h * group : (h + 1) * group, :]
    b0, b1 = plan_ref[0:1, 0:1], plan_ref[0:1, 1:2]
    t = lax.div(lax.axis_index("head"), low)
    for i, hit in enumerate((b0 == t, b0 != t, b1 == t, b1 != t)):
        sel_ref[i : i + 1, :] = jnp.broadcast_to(jnp.where(hit, 1.0, 0.0), (1, sel_ref.shape[1])).astype(F32)
    last = jnp.where(b0 > 0, 1.0, 0.0).astype(BF16)
    first = jnp.where(b0 > 0, 0.0, 1.0).astype(BF16)
    keys = (lat_ref[0] * first + lat_ref[1] * last).T
    k_pos = b0 * BLOCK + lax.broadcasted_iota(jnp.int32, (BLOCK, PACKET), 0)
    q_pos = SHARD - PACKET + lax.broadcasted_iota(jnp.int32, (BLOCK, PACKET), 1)
    visit(keys, q_ref, rows_ref, norm_ref, delta_ref, None, k_pos <= q_pos, ds_ref, p_ref, total_ref)
    pieces_out(total_ref, low, 0, [(0, keep_ref)])
    for i, out_ref in enumerate(out_refs):
        part = out_ref.shape[0]
        pieces_out(total_ref, low, i % CHUNKS * part, [(1 + i // CHUNKS, out_ref)])


def far_kernel(low, held, keys_ref, q_ref, grad_ref, norm_ref, delta_ref, *rest):
    ds_ref = rest[held]
    out_refs = rest[held + 1 : held + 1 + low]
    p_ref, total_ref = rest[-2:]
    live = lax.axis_index("seq") > 0
    visit(keys_ref[...], q_ref, grad_ref, norm_ref, delta_ref, live, None, ds_ref, p_ref, total_ref)
    pieces_out(total_ref, low, 0, list(enumerate(out_refs)))


def query_kernel(plan_ref, lat_ref, own_ds_ref, *rest):
    far_refs = rest[:CHUNKS]
    far_ds_refs = rest[CHUNKS : 2 * CHUNKS]
    out_ref = rest[-1]
    heads = out_ref.shape[0]
    per = WIDE // PACKET
    b0 = plan_ref[0:1, 0:1]
    last = jnp.where(b0 > 0, 1.0, 0.0).astype(BF16)
    first_block = jnp.where(b0 > 0, 0.0, 1.0).astype(BF16)
    own = lat_ref[0] * first_block + lat_ref[1] * last
    fars = [ref[...].T for ref in far_refs]
    for first in range(0, heads, per):
        cols = slice(first * PACKET, (first + per) * PACKET)
        total = dot(own, own_ds_ref[:, cols])
        for far, ds_ref in zip(fars, far_ds_refs):
            total = total + dot(far, ds_ref[:, cols])
        for i in range(per):
            out_ref[first + i] = total[:, i * PACKET : (i + 1) * PACKET].astype(BF16)


def combine_kernel(low, chunk, sel_ref, *rest):
    far_refs = rest[:low]
    own_refs = rest[low : 2 * low]
    send_ref, mine_ref = rest[-2:]
    part = send_ref.shape[0]
    here = slice(chunk * part, (chunk + 1) * part)
    own = own_refs[0][here, :]
    for ref in own_refs[1:]:
        own = own + ref[...].astype(F32)
    far = far_refs[0][...].astype(F32)
    for ref in far_refs[1:]:
        far = far + ref[...].astype(F32)
    send_ref[...] = (own * sel_ref[1:2, :] + far * sel_ref[3:4, :]).astype(BF16)
    mine_ref[...] = own * sel_ref[0:1, :] + far * sel_ref[2:3, :]


def last_kernel(*refs):
    mine_refs, got_refs, out_ref = refs[:CHUNKS][::-1], refs[CHUNKS : 2 * CHUNKS][::-1], refs[-1]
    part = out_ref.shape[0] // CHUNKS
    for c in range(CHUNKS):
        out_ref[c * part : (c + 1) * part, :] = (mine_refs[c][...] + got_refs[c][...].astype(F32)).astype(BF16)


def call(kernel, name, ins, outs, scratch=(), smem=(), raw=(), passed=(), flops=0, transcendentals=0):
    spaces = [pltpu.SMEM if i in smem else pltpu.VMEM for i in range(len(ins))]
    ins = list(ins)
    for i in raw:
        spaces[i] = pl.ANY
        ins[i] = pltpu.with_memory_space_constraint(ins[i], pltpu.HBM)
    size = sum(x.size * x.dtype.itemsize for x in ins)
    size += sum(functools.reduce(lambda a, b: a * b, s, jnp.dtype(d).itemsize) for s, d in outs)
    out_spaces = [pltpu.VMEM] * len(outs) + [pl.ANY] * len(passed)
    shapes = [jax.ShapeDtypeStruct(s, d) for s, d in outs]
    shapes += [jax.ShapeDtypeStruct(x.shape, x.dtype) for x in passed]
    aliases = {len(ins) + i: len(outs) + i for i in range(len(passed))}
    return pl.pallas_call(
        kernel,
        name=name,
        out_shape=shapes,
        in_specs=[pl.BlockSpec(memory_space=space) for space in spaces + [pl.ANY] * len(passed)],
        out_specs=[pl.BlockSpec(memory_space=space) for space in out_spaces],
        scratch_shapes=scratch,
        input_output_aliases=aliases,
        compiler_params=pltpu.CompilerParams(vmem_limit_bytes=VMEM_LIMIT),
        cost_estimate=pl.CostEstimate(flops=flops, bytes_accessed=size, transcendentals=transcendentals),
    )(*ins, *passed)


def local(queries, out_grad, latents, log_norm, out_delta, plan):
    n_seq = lax.axis_size("seq")
    n_head = lax.axis_size("head")
    low = n_head // 2
    rows = BLOCK // low
    packet, heads, width = queries.shape
    columns = packet * heads

    lat_t = latents.T
    q_t = jnp.transpose(queries, (1, 2, 0))
    grad = out_grad.reshape(columns, LAT)
    norm_t = log_norm.T
    delta_t = out_delta.T
    visit_flops = 2 * columns * BLOCK * (2 * width + 2 * LAT)

    def route(d, back):
        pairs = []
        for i in range(n_seq):
            for j in range(n_head):
                to = j // low * low + (j + d) % low
                pairs.append((i * n_head + j, (i - back) % n_seq * n_head + to))
        return pairs

    part = rows // CHUNKS
    keys = BLOCK // CHUNKS

    blocks = SHARD // BLOCK
    *sent, lat_blocks = call(
        functools.partial(send_block_kernel, low),
        "send_block",
        (plan, lat_t),
        [((keys, width), BF16)] * CHUNKS + [((blocks, width, BLOCK), BF16)],
        [pltpu.SMEM(plan.shape, plan.dtype), pltpu.SemaphoreType.DMA((blocks + 1,))],
        flops=visit_flops,
        raw=(0, 1),
    )
    far_keys = [lax.ppermute(x, "seq", [(i, (i + 1) % n_seq) for i in range(n_seq)]) for x in sent]

    grad_rows, own_ds, sel, keep, *own = call(
        functools.partial(own_kernel, low),
        "own_visit",
        (plan, lat_blocks, q_t, grad, norm_t, delta_t),
        [((columns, LAT), BF16), ((BLOCK, columns), BF16), ((8, width), F32), ((rows, width), F32)]
        + [((part, width), BF16)] * (CHUNKS * (low - 1)),
        [pltpu.VMEM((BLOCK, columns), BF16), pltpu.VMEM((BLOCK, width), F32)],
    )

    far_ds, own_parts, far_parts = [], [], []
    for c in range(CHUNKS):
        later = [i for i in range(len(own)) if i % CHUNKS and i % CHUNKS >= c]
        ds, *far = call(
            functools.partial(far_kernel, low, len(later)),
            f"far_visit_{c}",
            (far_keys[c], q_t, grad_rows, norm_t, delta_t),
            [((keys, columns), BF16)] + [((part, width), BF16)] * low,
            [pltpu.VMEM((keys, columns), BF16), pltpu.VMEM((keys, width), F32)],
            passed=[own[i] for i in later],
        )
        for i, x in zip(later, far[low:]):
            own[i] = x
        parts = own[c::CHUNKS]
        own_parts.append([keep] + [lax.ppermute(parts[d - 1], ("seq", "head"), route(d, 0)) for d in range(1, low)])
        far_ds.append(ds)
        far_parts.append([lax.ppermute(far[d], ("seq", "head"), route(d, 1)) for d in reversed(range(low))])

    mine, got = [None] * CHUNKS, [None] * CHUNKS
    for c in reversed(range(CHUNKS)):
        send, mine[c] = call(
            functools.partial(combine_kernel, low, c),
            f"combine_{c}",
            (sel, *far_parts[c], *own_parts[c]),
            [((part, width), BF16), ((part, width), F32)],
        )
        got[c] = lax.ppermute(send, "head", [(j, (j + low) % n_head) for j in range(n_head)])

    (query_t,) = call(
        query_kernel,
        "query_grad",
        (plan, lat_blocks, own_ds, *far_keys, *far_ds),
        [((heads, width, packet), BF16)],
        flops=4 * columns * BLOCK * width,
    )
    (latent_out,) = call(last_kernel, "last_sum", (*mine[::-1], *got[::-1]), [((rows, width), BF16)])
    return jnp.transpose(query_t, (2, 0, 1)), latent_out


def solution(mesh):
    return jax.shard_map(
        local,
        mesh=mesh,
        in_specs=(
            P("seq", "head", None),
            P("seq", "head", None),
            P("seq", None),
            P("seq", "head"),
            P("seq", "head"),
            P("seq", None),
        ),
        out_specs=(P("seq", "head", None), P(("seq", "head"), None)),
        check_vma=False,
    )
```
